32 devices in a mesh: scen: 8 (over z, core), col: 4 (over y, x).
Axes of the slice: x: 2, y: 2, z: 4, core: 2. Of those that a mesh axis runs over, the one named last changes fastest.
Arguments:
- inverse_factor: bfloat16 [32, 512, 512], P(('scen', 'col')), as said below
- true_orders: int32 [32], P(('scen', 'col')), may hold values from 64 to 512, as said below
- slab_border: bfloat16 [32, 256, 512], P(('scen', 'col')), may hold values from -0.25 to 0.25
- slab_columns: int32 [32, 256], P('scen'), may hold values from 0 to 511
- panel_border: bfloat16 [4, 32, 48, 512], P('col', 'scen'), may hold values from -6 to 6
- panel_rows: int32 [4, 32, 48], P('col', 'scen'), may hold values from 0 to 1919
- barrier_diag: float32 [512], replicated, may hold values from 20 to 400
Outputs:
- diag_factor: float32 [512, 512], P('col')
- panel_factor: float32 [7680, 512], P(('scen', 'col'))
The draws below stay inside these ranges and needn't reach their ends.
Inputs may be any that keep to these rules, and one draw needn't show every extreme that they name: `inverse_factor`: symmetric; its leading block of each scenario's true order is positive definite. `true_orders`: scenario 0 has the full padded order.
All inputs are finite; a program needn't handle non-finite values.
Results may differ from the reference program's by a relative error of at most 0.0003.
The reference program's roundings to bfloat16 on the way (of `masked` and `transformed`) count: a program that leaves them out, or rounds other values in their place, can miss the bound.
Values may be sent and summed in bfloat16 or wider, within the bound.
No kernel may reach another device: no remote copies, remote signals or barrier semaphores. Data moves between devices by JAX's collectives and lax.ppermute only.
A program may use at most 64 MiB of HBM per device.

```python
import math
import jax
import jax.numpy as jnp
from jax import lax

P_SIZE = 512
DIAG = 512
CBJ = 256
CBP = 48
SCEN = 32
ROWS_PANEL = 1920
ROWS_DEV = 240
N_SCEN = 8
N_COL = 4


def draw_inverse_factor(key, part):

    def draw_single(position):
        folded = jax.random.fold_in(key, position)
        first_key, second_key = jax.random.split(folded)
        noise = jax.random.normal(first_key, (P_SIZE, P_SIZE), jnp.float32)
        symmetric = (noise + noise.T) * (0.4 / math.sqrt(2.0 * P_SIZE))
        leading = jax.random.uniform(second_key, (P_SIZE,), jnp.float32, 1.5, 2.5)
        return (symmetric + jnp.diag(leading)).astype(jnp.bfloat16)
    return lax.map(draw_single, jnp.arange(SCEN, dtype=jnp.int32))


def draw_true_orders(key, part):
    values = jax.random.randint(key, (SCEN,), P_SIZE // 8, P_SIZE + 1, dtype=jnp.int32)
    values = values.at[0].set(P_SIZE)
    return values.at[1].set(P_SIZE // 8)


def place_ends(entries, rng, low, high):
    dims = entries.shape
    place = [jax.random.randint(jax.random.fold_in(rng, axis), (), 0, dims[axis]) for axis in range(len(dims))]
    entries = entries.at[tuple(place)].set(low)
    longest = dims.index(max(dims))
    place[longest] = (place[longest] + 1) % dims[longest]
    return entries.at[tuple(place)].set(high)


def steps_of(own_key, extent, cuts, low, high):
    def one(dim, shards_of):
        draws = jax.random.uniform(jax.random.fold_in(jax.random.fold_in(own_key, 6), dim), (shards_of,), jnp.float32, low / len(cuts), high / len(cuts))
        return jnp.repeat(jnp.exp(draws), extent[dim] // shards_of).reshape((-1,) + (1,) * (len(extent) - dim - 1))

    factor_of = one(*cuts[0])
    for cut in cuts[1:]:
        factor_of = factor_of * one(*cut)
    return factor_of


def normal_values(stream_key, shape, width, limit, cuts=(), kind=jnp.bfloat16):
    array = jax.random.normal(stream_key, shape, jnp.float32) * width
    if len(cuts) > 0:
        array = steps_of(stream_key, shape, cuts, -0.22, 0.18) * array
    return jnp.clip(array, min=-limit, max=limit).astype(kind)


def setup_inputs(seed: int = 0) -> dict:
    streams_of = jax.random.split(jax.random.key(seed), 8)
    return {
        "inverse_factor": draw_inverse_factor(jax.random.fold_in(streams_of[7], 71), 0),
        "true_orders": draw_true_orders(jax.random.fold_in(streams_of[7], 71), 0),
        "slab_border": normal_values(streams_of[2], (SCEN, CBJ, P_SIZE), P_SIZE ** -0.5, 0.25, ((0, 32),)),
        "slab_columns": place_ends(jax.random.randint(streams_of[3], (SCEN, CBJ), 0, DIAG), jax.random.fold_in(streams_of[3], 1), 0, DIAG - 1).astype(jnp.int32),
        "panel_border": normal_values(streams_of[4], (N_COL, SCEN, CBP, P_SIZE), 1.0, 6.0, ((0, 4), (1, 8))),
        "panel_rows": place_ends(jax.random.randint(streams_of[5], (N_COL, SCEN, CBP), 0, ROWS_PANEL), jax.random.fold_in(streams_of[5], 1), 0, ROWS_PANEL - 1).astype(jnp.int32),
        "barrier_diag": jnp.clip(jnp.exp(jax.random.uniform(streams_of[6], (DIAG,), jnp.float32, math.log(20.0), math.log(400.0))), 20.0, 400.0),
    }


def reference(inverse_factor, true_orders, slab_border, slab_columns, panel_border, panel_rows, barrier_diag):
    positions = jnp.arange(P_SIZE, dtype=jnp.int32)

    def transform(operands):
        factor, order_value, border = operands
        inside = positions < order_value
        masked = jnp.where(inside[:, None] & inside[None, :], factor, jnp.zeros((), jnp.bfloat16))
        return jnp.dot(border.astype(jnp.float32), masked.astype(jnp.float32), preferred_element_type=jnp.float32).astype(jnp.bfloat16)
    transformed = lax.map(transform, (inverse_factor, true_orders, slab_border))

    def diag_step(running, operands):
        border, moved_rows, columns = operands
        coupling = jnp.dot(border.astype(jnp.float32), moved_rows.T.astype(jnp.float32), preferred_element_type=jnp.float32)
        return (running.at[columns[:, None], columns[None, :]].add(coupling), None)
    schur_diag, _ = lax.scan(diag_step, jnp.diag(barrier_diag), (slab_border, transformed, slab_columns))

    def panel_total(operands):
        border_part, rows_part = operands

        def panel_step(running, inner):
            border_values, moved_rows, row_index, columns = inner
            coupling = jnp.dot(border_values.astype(jnp.float32), moved_rows.T.astype(jnp.float32), preferred_element_type=jnp.float32)
            return (running.at[row_index[:, None], columns[None, :]].add(coupling), None)
        zero_panel = jnp.zeros((ROWS_PANEL, DIAG), jnp.float32)
        result, _ = lax.scan(panel_step, zero_panel, (border_part, transformed, rows_part, slab_columns))
        return result
    panels = lax.map(panel_total, (panel_border, panel_rows))
    slab_rows = panels.reshape(N_COL, N_SCEN, ROWS_DEV, DIAG).transpose(1, 0, 2, 3).reshape(N_COL * ROWS_PANEL, DIAG)
    symmetric = 0.5 * (schur_diag + schur_diag.T)
    diag_factor = jnp.linalg.cholesky(symmetric)
    panel_factor = lax.linalg.triangular_solve(diag_factor, slab_rows, left_side=False, lower=True, transpose_a=True)
    return (diag_factor, panel_factor)
```

```python
import functools

import jax
import jax.numpy as jnp
from jax import lax
from jax.experimental import pallas as pl
from jax.experimental.pallas import tpu as pltpu
from jax.sharding import PartitionSpec as P

NF = 8192
BLOCK = 128
HIGHEST = lax.Precision.HIGHEST
VMEM = pl.BlockSpec(memory_space=pltpu.VMEM)
SMEM = pl.BlockSpec(memory_space=pltpu.SMEM)
PARAMS = pltpu.CompilerParams(vmem_limit_bytes=40 * 2**20)


def split_two(value):
    high = value.astype(jnp.bfloat16)
    low = (value - high.astype(jnp.float32)).astype(jnp.bfloat16)
    return high, low


def matmul(left, right):
    return jnp.dot(left, right, preferred_element_type=jnp.float32)


def matmul_nt(left, right):
    return lax.dot_general(
        left, right, (((1,), (1,)), ((), ())), preferred_element_type=jnp.float32
    )


def exact_tn(left, right):
    return lax.dot_general(
        left,
        right,
        (((0,), (0,)), ((), ())),
        precision=HIGHEST,
        preferred_element_type=jnp.float32,
    )


def exact(left, right):
    return jnp.dot(left, right, precision=HIGHEST, preferred_element_type=jnp.float32)


def exact_nt(left, right):
    return lax.dot_general(
        left,
        right,
        (((1,), (1,)), ((), ())),
        precision=HIGHEST,
        preferred_element_type=jnp.float32,
    )


def upper_blocks(width):
    count = width // BLOCK
    return [(i, j) for i in range(count) for j in range(i, count)]


def front_kernel(
    order_ref, factor_ref, border_ref, columns_ref, moved_ref, keep_ref, send_ref, packed_ref, *, width
):
    count = factor_ref.shape[0]
    core = lax.rem(lax.axis_index("scen"), 2)
    place = lax.axis_index("col")
    order = order_ref[0]
    border = border_ref[0]
    within = lax.broadcasted_iota(jnp.int32, border.shape, 1) < order
    inside = jnp.where(within, border.astype(jnp.float32), 0.0).astype(jnp.bfloat16)
    product = matmul(inside, factor_ref[0])
    moved = jnp.where(within, product, 0.0).astype(jnp.bfloat16)
    moved_ref[...] = moved
    terms = 0.5 * (matmul_nt(border, moved) + matmul_nt(moved, border))
    columns = columns_ref[pl.ds(place * count, 1), :]
    spread = (
        lax.broadcasted_iota(jnp.int32, (width, columns.shape[1]), 0) == columns
    ).astype(jnp.bfloat16)
    high, low = split_two(terms)
    half_spread = matmul_nt(high, spread) + matmul_nt(low, spread)
    high, low = split_two(half_spread)
    row = 0
    for i in range(width // BLOCK):
        rows = spread[i * BLOCK : (i + 1) * BLOCK]
        part = matmul(rows, high[:, i * BLOCK :]) + matmul(rows, low[:, i * BLOCK :])
        for j in range(i, width // BLOCK):
            packed_ref[row : row + BLOCK, :] = part[:, (j - i) * BLOCK : (j - i + 1) * BLOCK]
            row += BLOCK
    half = keep_ref.shape[0]
    keep_ref[...] = packed_ref[pl.ds(pl.multiple_of(core * half, 8), half), :]
    send_ref[...] = packed_ref[pl.ds(pl.multiple_of((1 - core) * half, 8), half), :]


def front(order, factor, border, columns, width):
    total = len(upper_blocks(width)) * BLOCK
    half = jax.ShapeDtypeStruct((total // 2, BLOCK), jnp.float32)
    return pl.pallas_call(
        functools.partial(front_kernel, width=width),
        out_shape=[jax.ShapeDtypeStruct(border.shape[1:], jnp.bfloat16), half, half],
        in_specs=[SMEM, VMEM, VMEM, VMEM],
        out_specs=[VMEM, VMEM, VMEM],
        scratch_shapes=[pltpu.VMEM((total, BLOCK), jnp.float32)],
        compiler_params=PARAMS,
        name="front",
    )(order, factor, border, columns)


def quarter_kernel(keep_ref, got_ref, *out_refs):
    place = lax.axis_index("col")
    rows = out_refs[0].shape[0]
    for m, out_ref in enumerate(out_refs):
        at = pl.ds(pl.multiple_of((place ^ m) * rows, 8), rows)
        out_ref[...] = keep_ref[at, :] + got_ref[at, :]


def quarters(keep, got, col_count):
    piece = jax.ShapeDtypeStruct((keep.shape[0] // col_count, BLOCK), jnp.float32)
    return pl.pallas_call(
        quarter_kernel,
        out_shape=[piece] * col_count,
        in_specs=[VMEM, VMEM],
        out_specs=[VMEM] * col_count,
        compiler_params=PARAMS,
        name="quarters",
    )(keep, got)


def swap(value, axis, step):
    count = lax.axis_size(axis)
    return lax.ppermute(value, axis, [(i, i ^ step) for i in range(count)])


def tree_sum(values):
    while len(values) > 1:
        values = [values[i] + values[i + 1] for i in range(0, len(values), 2)]
    return values[0]


def row_of(tile, i):
    return jnp.broadcast_to(tile[i : i + 1, :], tile.shape)


def column_of(tile, j):
    return jnp.broadcast_to(tile[:, j : j + 1], (tile.shape[0], BLOCK))


def factor_block(block):
    groups = BLOCK // 8
    sub = lax.broadcasted_iota(jnp.int32, (8, BLOCK), 0)
    lane = lax.broadcasted_iota(jnp.int32, (8, BLOCK), 1)
    left = [block[8 * t : 8 * t + 8, :] for t in range(groups)]
    right = [(lane == sub + 8 * t).astype(jnp.float32) for t in range(groups)]
    upper = []
    inverse = []
    for g in range(groups):
        a, b = left[g], right[g]
        near = [column_of(a, 8 * g + m) for m in range(8)]
        out_a, out_b = a, b
        for i in range(8):
            pivot = row_of(near[i], i)
            recip = 1.0 / pivot
            root = lax.rsqrt(pivot)
            factor = jnp.where(sub == i, 1.0 - recip, near[i] * recip)
            row_a, row_b = row_of(a, i), row_of(b, i)
            out_a = jnp.where(sub == i, row_a * root, out_a)
            out_b = jnp.where(sub == i, row_b * root, out_b)
            for m in range(i + 1, 8):
                near[m] = near[m] - factor * row_of(near[m], i)
            a = a - factor * row_a
            b = b - factor * row_b
        upper.append(jnp.where(lane >= sub + 8 * g, out_a, 0.0))
        inverse.append(out_b)
        if g + 1 < groups:
            rows_a = [row_of(a, i) for i in range(8)]
            rows_b = [row_of(b, i) for i in range(8)]
            for t in range(g + 1, groups):
                weights = [column_of(left[t], 8 * g + i) for i in range(8)]
                sum_a = weights[0] * rows_a[0]
                sum_b = weights[0] * rows_b[0]
                for i in range(1, 8):
                    sum_a = sum_a + weights[i] * rows_a[i]
                    sum_b = sum_b + weights[i] * rows_b[i]
                left[t] = left[t] - sum_a
                right[t] = right[t] - sum_b
    return jnp.concatenate(upper, 0), jnp.concatenate(inverse, 0)


def cholesky_kernel(*refs, col_count):
    pieces = refs[: 2 * col_count]
    barrier_ref, upper_ref, inverse_ref, slice_ref, packed_ref, lower_ref = refs[2 * col_count :]
    width = barrier_ref.shape[1]
    count = width // BLOCK
    rows = pieces[0].shape[0]
    core = lax.rem(lax.axis_index("scen"), 2)
    place = lax.axis_index("col")
    for side in range(2):
        owner = core if side == 0 else 1 - core
        for m in range(col_count):
            at = (owner * col_count + (place ^ m)) * rows
            packed_ref[pl.ds(pl.multiple_of(at, 8), rows), :] = pieces[side * col_count + m][...]
    diagonal = lax.broadcasted_iota(jnp.int32, (BLOCK, BLOCK), 0) == lax.broadcasted_iota(
        jnp.int32, (BLOCK, BLOCK), 1
    )
    blocks = {}
    for n, (i, j) in enumerate(upper_blocks(width)):
        blocks[i, j] = packed_ref[n * BLOCK : (n + 1) * BLOCK, :]
        if i == j:
            extra = barrier_ref[:, i * BLOCK : (i + 1) * BLOCK]
            blocks[i, j] = blocks[i, j] + jnp.where(diagonal, extra, 0.0)
    panels = [jnp.concatenate([blocks[i, j] for j in range(i, count)], 1) for i in range(count)]
    lower_ref[...] = jnp.zeros(lower_ref.shape, jnp.float32)
    for i in range(count):
        here = slice(i * BLOCK, (i + 1) * BLOCK)
        own, inverse = factor_block(panels[i][:, :BLOCK])
        upper_ref[here, here] = own
        inverse_ref[i] = inverse
        lower_ref[here, here] = own.T
        if i + 1 < count:
            rest = exact(inverse, panels[i][:, BLOCK:])
            upper_ref[here, (i + 1) * BLOCK :] = rest
            for j in range(i + 1, count):
                first = (j - i - 1) * BLOCK
                block = rest[:, first : first + BLOCK]
                lower_ref[j * BLOCK : (j + 1) * BLOCK, here] = block.T
                panels[j] = panels[j] - exact_tn(block, rest[:, first:])
    slice_rows = slice_ref.shape[0]
    slice_ref[...] = lower_ref[pl.ds(pl.multiple_of(place * slice_rows, 8), slice_rows), :]


def cholesky(pieces, barrier):
    width = barrier.shape[0]
    col_count = len(pieces) // 2
    return pl.pallas_call(
        functools.partial(cholesky_kernel, col_count=col_count),
        out_shape=[
            jax.ShapeDtypeStruct((width, width), jnp.float32),
            jax.ShapeDtypeStruct((width // BLOCK, BLOCK, BLOCK), jnp.float32),
            jax.ShapeDtypeStruct((width // col_count, width), jnp.float32),
        ],
        in_specs=[VMEM] * (len(pieces) + 1),
        out_specs=[VMEM] * 3,
        scratch_shapes=[
            pltpu.VMEM((len(upper_blocks(width)) * BLOCK, BLOCK), jnp.float32),
            pltpu.VMEM((width, width), jnp.float32),
        ],
        compiler_params=PARAMS,
        cost_estimate=pl.CostEstimate(
            flops=2 * width**3, bytes_accessed=12 * width**2, transcendentals=width
        ),
        name="cholesky",
    )(*pieces, barrier[None])


def coupling_kernel(moved_ref, *refs):
    count = len(refs) // 2
    moved = moved_ref[...]
    for border_ref, out_ref in zip(refs[:count], refs[count:]):
        out_ref[...] = matmul_nt(border_ref[...], moved)


def couplings(moved, borders):
    shape = jax.ShapeDtypeStruct((borders[0].shape[0], moved.shape[0]), jnp.float32)
    return pl.pallas_call(
        coupling_kernel,
        out_shape=[shape] * len(borders),
        in_specs=[VMEM] * (len(borders) + 1),
        out_specs=[VMEM] * len(borders),
        compiler_params=PARAMS,
        name="couplings",
    )(moved, *borders)


def solve_rows(rows, upper, inverse, out_ref):
    width = rows.shape[1]
    solved = []
    for k in range(width // BLOCK):
        here = slice(k * BLOCK, (k + 1) * BLOCK)
        left = rows[:, here]
        if k > 0:
            left = left - exact(jnp.concatenate(solved, 1), upper[: k * BLOCK, here])
        solved.append(exact_nt(left, inverse[k]))
        out_ref[:, here] = solved[-1]


def panel_kernel(*refs, group):
    groups = refs[:-3]
    upper_ref, inverse_ref, out_ref = refs[-3:]
    rows_here, width = out_ref.shape
    first = lax.axis_index("scen") * rows_here
    total = jnp.zeros((rows_here, width), jnp.float32)
    for group_ref in groups:
        wide = group_ref.shape[1]
        size = (group_ref.shape[0] - 8) // group
        index = group_ref[group * size :, :]
        spreads = []
        for i in range(group):
            columns = index[i : i + 1, :].astype(jnp.int32)
            spread = lax.broadcasted_iota(jnp.int32, (width, wide), 0) == columns
            high, low = split_two(group_ref[i * size : (i + 1) * size, :])
            both = matmul_nt(
                jnp.concatenate([high, low], 0), spread.astype(jnp.bfloat16)
            )
            spreads.append(both[:size] + both[size:])
        widened = jnp.concatenate(spreads, 0)
        row_index = index[group : group + 1, : group * size].astype(jnp.int32) - first
        row_map = (
            lax.broadcasted_iota(jnp.int32, (rows_here, group * size), 0) == row_index
        ).astype(jnp.bfloat16)
        high, low = split_two(widened)
        total = total + (matmul(row_map, high) + matmul(row_map, low))
    solve_rows(total, upper_ref[...], inverse_ref[...], out_ref)


def panel_rows_of(groups, group, upper, inverse, rows_here):
    return pl.pallas_call(
        functools.partial(panel_kernel, group=group),
        out_shape=jax.ShapeDtypeStruct((rows_here, upper.shape[1]), jnp.float32),
        in_specs=[VMEM] * (len(groups) + 2),
        out_specs=VMEM,
        compiler_params=PARAMS,
        name="panel",
    )(*groups, upper, inverse)


def dense_panel(couplings_here, rows, columns, rows_panel, width):
    def step(running, operands):
        coupling, row_index, column_index = operands
        column_map = (column_index[:, None] == jnp.arange(width)[None, :]).astype(jnp.float32)
        row_map = (row_index[:, None] == jnp.arange(rows_panel)[None, :]).astype(jnp.float32)
        widened = jnp.dot(coupling, column_map, precision=HIGHEST)
        return running + jnp.einsum("br,bd->rd", row_map, widened, precision=HIGHEST), None

    zero = jnp.zeros((rows_panel, width), jnp.float32)
    total, _ = lax.scan(step, zero, (couplings_here, rows, columns))
    return lax.psum_scatter(total, "scen", scatter_dimension=0, tiled=True)


def dense_solve(rows, upper, inverse):
    width = rows.shape[1]
    solved = []
    for k in range(width // BLOCK):
        here = slice(k * BLOCK, (k + 1) * BLOCK)
        left = rows[:, here]
        if k > 0:
            left = left - jnp.dot(
                jnp.concatenate(solved, 1), upper[: k * BLOCK, here], precision=HIGHEST
            )
        solved.append(jnp.dot(left, inverse[k].T, precision=HIGHEST))
    return jnp.concatenate(solved, 1)


def shards(
    rows_here,
    inverse_factor,
    true_orders,
    slab_border,
    slab_columns,
    panel_border,
    panel_rows,
    barrier_diag,
):
    scen_count = lax.axis_size("scen")
    col_count = lax.axis_size("col")
    place = lax.axis_index("col")
    width = barrier_diag.shape[0]
    group, size, depth = panel_border.shape[1:]
    wide = slab_columns.shape[1]

    order = [place ^ m for m in range(col_count)]
    own_borders = [
        lax.dynamic_index_in_dim(panel_border[0], order[m], 0, keepdims=False)
        for m in range(col_count)
    ]
    borders = [own_borders[0]] + [swap(own_borders[m], "col", m) for m in range(1, col_count)]

    moved, keep, send = front(true_orders, inverse_factor, slab_border, slab_columns, width)
    got = swap(send, "scen", 1)
    parts = quarters(keep, got, col_count)
    part = tree_sum([parts[0]] + [swap(parts[m], "col", m) for m in range(1, col_count)])
    part = tree_sum([part] + [swap(part, "scen", 2 * m) for m in range(1, scen_count // 2)])
    pieces = [part] + [swap(part, "col", m) for m in range(1, col_count)]
    pieces = pieces + [swap(piece, "scen", 1) for piece in pieces]
    upper, inverse, factor_rows = cholesky(pieces, barrier_diag)

    partial = couplings(moved, borders)
    mine = [partial[0]] + [swap(partial[m], "col", m) for m in range(1, col_count)]
    rows_panel = rows_here * scen_count
    fits = group < 8 and group * size <= wide
    if fits and scen_count * group * size * wide < rows_panel * width:
        order = jnp.stack(order)
        rows_index = panel_rows[0][order].reshape(1, group * size)
        rows_index = jnp.pad(rows_index, ((0, 0), (0, wide - group * size)))
        index = jnp.concatenate([slab_columns[order], rows_index], 0).astype(jnp.float32)
        index = jnp.pad(index, ((0, 7 - group), (0, 0)))
        own = jnp.concatenate(mine + [index], 0)
        near = [own] + [swap(own, "scen", 2 * m) for m in range(1, scen_count // 2)]
        groups = near + [swap(value, "scen", 1) for value in near]
        solved = panel_rows_of(groups, group, upper, inverse, rows_here)
    else:
        rows = dense_panel(
            jnp.stack(mine), panel_rows[0][jnp.stack(order)], slab_columns[jnp.stack(order)], rows_panel, width
        )
        solved = dense_solve(rows, upper, inverse)
    return factor_rows, solved


def solution(mesh):
    in_specs = (
        P(("scen", "col"), None, None),
        P(("scen", "col")),
        P(("scen", "col"), None, None),
        P("scen", None),
        P("col", "scen", None, None),
        P("col", "scen", None),
        P(),
    )
    out_specs = (P("col", None), P(("scen", "col"), None))

    def whole(*args):
        devices = mesh.shape["scen"] * mesh.shape["col"]
        first_section = NF - args[-1].shape[0]
        body = functools.partial(shards, first_section // devices)
        return jax.shard_map(
            body, mesh=mesh, in_specs=in_specs, out_specs=out_specs, check_vma=False
        )(*args)

    return whole
```

```python
import functools

import jax
import jax.numpy as jnp
from jax import lax
from jax.experimental import pallas as pl
from jax.experimental.pallas import tpu as pltpu
from jax.sharding import PartitionSpec as P

NF = 8192
BLOCK = 128
HIGHEST = lax.Precision.HIGHEST
VMEM = pl.BlockSpec(memory_space=pltpu.VMEM)
SMEM = pl.BlockSpec(memory_space=pltpu.SMEM)
ANY = pl.BlockSpec(memory_space=pl.ANY)
PARAMS = pltpu.CompilerParams(vmem_limit_bytes=40 * 2**20)


def long_cost(micros):
    return pl.CostEstimate(flops=micros * 10**9, bytes_accessed=2**20, transcendentals=0)


def split_two(value):
    high = value.astype(jnp.bfloat16)
    low = (value - high.astype(jnp.float32)).astype(jnp.bfloat16)
    return high, low


def matmul(left, right):
    return jnp.dot(left, right, preferred_element_type=jnp.float32)


def matmul_nt(left, right):
    return lax.dot_general(
        left, right, (((1,), (1,)), ((), ())), preferred_element_type=jnp.float32
    )


def exact_tn(left, right):
    return lax.dot_general(
        left,
        right,
        (((0,), (0,)), ((), ())),
        precision=HIGHEST,
        preferred_element_type=jnp.float32,
    )


def exact(left, right):
    return jnp.dot(left, right, precision=HIGHEST, preferred_element_type=jnp.float32)


def exact_nt(left, right):
    return lax.dot_general(
        left,
        right,
        (((1,), (1,)), ((), ())),
        precision=HIGHEST,
        preferred_element_type=jnp.float32,
    )


def upper_blocks(width):
    count = width // BLOCK
    return [(i, j) for i in range(count) for j in range(i, count)]


def front_kernel(
    order_ref, factor_ref, border_ref, columns_ref, moved_ref, keep_ref, send_ref, packed_ref, *, width
):
    count = factor_ref.shape[0]
    core = lax.rem(lax.axis_index("scen"), 2)
    place = lax.axis_index("col")
    order = order_ref[0]
    border = border_ref[0]
    within = lax.broadcasted_iota(jnp.int32, border.shape, 1) < order
    inside = jnp.where(within, border.astype(jnp.float32), 0.0).astype(jnp.bfloat16)
    product = matmul(inside, factor_ref[0])
    moved = jnp.where(within, product, 0.0).astype(jnp.bfloat16)
    moved_ref[...] = moved
    terms = 0.5 * (matmul_nt(border, moved) + matmul_nt(moved, border))
    columns = columns_ref[pl.ds(place * count, 1), :]
    spread = (
        lax.broadcasted_iota(jnp.int32, (width, columns.shape[1]), 0) == columns
    ).astype(jnp.bfloat16)
    high, low = split_two(terms)
    half_spread = matmul_nt(high, spread) + matmul_nt(low, spread)
    high, low = split_two(half_spread)
    row = 0
    for i in range(width // BLOCK):
        rows = spread[i * BLOCK : (i + 1) * BLOCK]
        part = matmul(rows, high[:, i * BLOCK :]) + matmul(rows, low[:, i * BLOCK :])
        for j in range(i, width // BLOCK):
            packed_ref[row : row + BLOCK, :] = part[:, (j - i) * BLOCK : (j - i + 1) * BLOCK]
            row += BLOCK
    half = keep_ref.shape[0]
    keep_ref[...] = packed_ref[pl.ds(pl.multiple_of(core * half, 8), half), :]
    send_ref[...] = packed_ref[pl.ds(pl.multiple_of((1 - core) * half, 8), half), :]


def front(order, factor, border, columns, width):
    total = len(upper_blocks(width)) * BLOCK
    half = jax.ShapeDtypeStruct((total // 2, BLOCK), jnp.float32)
    return pl.pallas_call(
        functools.partial(front_kernel, width=width),
        out_shape=[jax.ShapeDtypeStruct(border.shape[1:], jnp.bfloat16), half, half],
        in_specs=[SMEM, VMEM, VMEM, VMEM],
        out_specs=[VMEM, VMEM, VMEM],
        scratch_shapes=[pltpu.VMEM((total, BLOCK), jnp.float32)],
        compiler_params=PARAMS,
        cost_estimate=long_cost(20),
        name="front",
    )(order, factor, border, columns)


def quarter_kernel(keep_ref, got_ref, *out_refs):
    place = lax.axis_index("col")
    rows = out_refs[0].shape[0]
    for m, out_ref in enumerate(out_refs):
        at = pl.ds(pl.multiple_of((place ^ m) * rows, 8), rows)
        out_ref[...] = keep_ref[at, :] + got_ref[at, :]


def quarters(keep, got, col_count):
    piece = jax.ShapeDtypeStruct((keep.shape[0] // col_count, BLOCK), jnp.float32)
    return pl.pallas_call(
        quarter_kernel,
        out_shape=[piece] * col_count,
        in_specs=[VMEM, VMEM],
        out_specs=[VMEM] * col_count,
        compiler_params=PARAMS,
        name="quarters",
    )(keep, got)


def swap(value, axis, step):
    count = lax.axis_size(axis)
    return lax.ppermute(value, axis, [(i, i ^ step) for i in range(count)])


def tree_sum(values):
    while len(values) > 1:
        values = [values[i] + values[i + 1] for i in range(0, len(values), 2)]
    return values[0]


def row_of(tile, i):
    return jnp.broadcast_to(tile[i : i + 1, :], tile.shape)


def column_of(tile, j):
    return jnp.broadcast_to(tile[:, j : j + 1], (tile.shape[0], BLOCK))


def factor_block(block):
    groups = BLOCK // 8
    sub = lax.broadcasted_iota(jnp.int32, (8, BLOCK), 0)
    lane = lax.broadcasted_iota(jnp.int32, (8, BLOCK), 1)
    left = [block[8 * t : 8 * t + 8, :] for t in range(groups)]
    right = [(lane == sub + 8 * t).astype(jnp.float32) for t in range(groups)]
    upper = []
    inverse = []
    for g in range(groups):
        a, b = left[g], right[g]
        near = [column_of(a, 8 * g + m) for m in range(8)]
        out_a, out_b = a, b
        for i in range(8):
            pivot = row_of(near[i], i)
            recip = 1.0 / pivot
            root = lax.rsqrt(pivot)
            factor = jnp.where(sub == i, 1.0 - recip, near[i] * recip)
            row_a, row_b = row_of(a, i), row_of(b, i)
            out_a = jnp.where(sub == i, row_a * root, out_a)
            out_b = jnp.where(sub == i, row_b * root, out_b)
            for m in range(i + 1, 8):
                near[m] = near[m] - factor * row_of(near[m], i)
            a = a - factor * row_a
            b = b - factor * row_b
        upper.append(jnp.where(lane >= sub + 8 * g, out_a, 0.0))
        inverse.append(out_b)
        if g + 1 < groups:
            rows_a = [row_of(a, i) for i in range(8)]
            rows_b = [row_of(b, i) for i in range(8)]
            for t in range(g + 1, groups):
                weights = [column_of(left[t], 8 * g + i) for i in range(8)]
                sum_a = weights[0] * rows_a[0]
                sum_b = weights[0] * rows_b[0]
                for i in range(1, 8):
                    sum_a = sum_a + weights[i] * rows_a[i]
                    sum_b = sum_b + weights[i] * rows_b[i]
                left[t] = left[t] - sum_a
                right[t] = right[t] - sum_b
    return jnp.concatenate(upper, 0), jnp.concatenate(inverse, 0)


def eliminate(panels, first, last, upper_ref, inverse_ref):
    count = len(panels)
    for i in range(first, last):
        here = slice((i - first) * BLOCK, (i - first + 1) * BLOCK)
        own, inverse = factor_block(panels[i][:, :BLOCK])
        if i > 0:
            upper_ref[here, : i * BLOCK] = jnp.zeros((BLOCK, i * BLOCK), jnp.float32)
        upper_ref[here, i * BLOCK : (i + 1) * BLOCK] = own
        inverse_ref[i - first] = inverse
        if i + 1 < count:
            rest = exact(inverse, panels[i][:, BLOCK:])
            upper_ref[here, (i + 1) * BLOCK :] = rest
            for j in range(i + 1, count):
                at = (j - i - 1) * BLOCK
                panels[j] = panels[j] - exact_tn(rest[:, at : at + BLOCK], rest[:, at:])


def early_kernel(*refs, col_count):
    pieces = refs[: 2 * col_count]
    barrier_ref, upper_ref, inverse_ref, rest_ref, packed_ref = refs[2 * col_count :]
    width = barrier_ref.shape[1]
    count = width // BLOCK
    rows = pieces[0].shape[0]
    core = lax.rem(lax.axis_index("scen"), 2)
    place = lax.axis_index("col")
    for side in range(2):
        owner = core if side == 0 else 1 - core
        for m in range(col_count):
            at = (owner * col_count + (place ^ m)) * rows
            packed_ref[pl.ds(pl.multiple_of(at, 8), rows), :] = pieces[side * col_count + m][...]
    diagonal = lax.broadcasted_iota(jnp.int32, (BLOCK, BLOCK), 0) == lax.broadcasted_iota(
        jnp.int32, (BLOCK, BLOCK), 1
    )
    blocks = {}
    for n, (i, j) in enumerate(upper_blocks(width)):
        blocks[i, j] = packed_ref[n * BLOCK : (n + 1) * BLOCK, :]
        if i == j:
            extra = barrier_ref[:, i * BLOCK : (i + 1) * BLOCK]
            blocks[i, j] = blocks[i, j] + jnp.where(diagonal, extra, 0.0)
    panels = [jnp.concatenate([blocks[i, j] for j in range(i, count)], 1) for i in range(count)]
    done = inverse_ref.shape[0]
    eliminate(panels, 0, done, upper_ref, inverse_ref)
    for i in range(done, count):
        rest_ref[(i - done) * BLOCK : (i - done + 1) * BLOCK, (i - done) * BLOCK :] = panels[i]


def early_cholesky(pieces, barrier):
    width = barrier.shape[0]
    half = width // 2
    col_count = len(pieces) // 2
    return pl.pallas_call(
        functools.partial(early_kernel, col_count=col_count),
        out_shape=[
            jax.ShapeDtypeStruct((half, width), jnp.float32),
            jax.ShapeDtypeStruct((half // BLOCK, BLOCK, BLOCK), jnp.float32),
            jax.ShapeDtypeStruct((half, half), jnp.float32),
        ],
        in_specs=[VMEM] * (len(pieces) + 1),
        out_specs=[VMEM] * 3,
        scratch_shapes=[pltpu.VMEM((len(upper_blocks(width)) * BLOCK, BLOCK), jnp.float32)],
        compiler_params=PARAMS,
        cost_estimate=long_cost(20),
        name="early",
    )(*pieces, barrier[None])


def late_kernel(*refs):
    early_ref, rest_ref = refs[:2]
    upper_ref, inverse_ref, slice_ref, turned_ref = refs[-4:]
    width = early_ref.shape[1]
    count = width // BLOCK
    done = count // 2
    half = done * BLOCK
    place = lax.axis_index("col")
    panels = [None] * done + [
        rest_ref[i * BLOCK : (i + 1) * BLOCK, i * BLOCK :] for i in range(count - done)
    ]
    eliminate(panels, done, count, upper_ref, inverse_ref)
    slice_rows = slice_ref.shape[0]
    start = place * slice_rows
    block = pl.ds(pl.multiple_of(start // BLOCK * BLOCK, BLOCK), BLOCK)
    turned_ref[:, :half] = early_ref[:, block].T
    turned_ref[:, half:] = upper_ref[:, block].T
    slice_ref[...] = turned_ref[pl.ds(pl.multiple_of(lax.rem(start, BLOCK), 8), slice_rows), :]


def late_cholesky(early, rest, col_count, waits):
    half, width = early.shape
    return pl.pallas_call(
        late_kernel,
        out_shape=[
            jax.ShapeDtypeStruct((half, width), jnp.float32),
            jax.ShapeDtypeStruct((half // BLOCK, BLOCK, BLOCK), jnp.float32),
            jax.ShapeDtypeStruct((width // col_count, width), jnp.float32),
        ],
        in_specs=[VMEM, VMEM] + [ANY] * len(waits),
        out_specs=[VMEM] * 3,
        scratch_shapes=[pltpu.VMEM((BLOCK, width), jnp.float32)],
        compiler_params=PARAMS,
        cost_estimate=long_cost(20),
        name="late",
    )(early, rest, *waits)


def coupling_kernel(moved_ref, *refs, parts):
    count = (len(refs) - parts - 1) // 2
    refs[parts + count][...] = tree_sum([ref[...] for ref in refs[:parts]])
    moved = moved_ref[...]
    for border_ref, out_ref in zip(refs[parts:], refs[parts + count + 1 :]):
        out_ref[...] = matmul_nt(border_ref[...], moved)


def sum_and_couplings(parts, moved, borders):
    shape = jax.ShapeDtypeStruct((borders[0].shape[0], moved.shape[0]), jnp.float32)
    total, *partial = pl.pallas_call(
        functools.partial(coupling_kernel, parts=len(parts)),
        out_shape=[jax.ShapeDtypeStruct(parts[0].shape, jnp.float32)] + [shape] * len(borders),
        in_specs=[VMEM] * (len(parts) + len(borders) + 1),
        out_specs=[VMEM] * (len(borders) + 1),
        compiler_params=PARAMS,
        name="couplings",
    )(moved, *parts, *borders)
    return total, partial


def assemble_kernel(columns_ref, rows_ref, *refs, parts):
    refs[-2][...] = tree_sum([ref[...] for ref in refs[:parts]])
    pieces, out_ref = refs[parts:-2], refs[-1]
    place = lax.axis_index("col")
    size, wide = pieces[0].shape
    count = len(pieces)
    for m, piece in enumerate(pieces):
        out_ref[pl.ds(pl.multiple_of((place ^ m) * size, 8), size), :] = piece[...]
    out_ref[count * size :, :] = jnp.zeros((out_ref.shape[0] - count * size, wide), jnp.float32)
    out_ref[count * size : count * size + count, :] = columns_ref[...].astype(jnp.float32)
    for i in range(count):
        at = count * size + count
        out_ref[at : at + 1, i * size : (i + 1) * size] = rows_ref[0, i : i + 1, :].astype(
            jnp.float32
        )


def sum_and_assemble(parts, pieces, columns, rows):
    size, wide = pieces[0].shape
    return pl.pallas_call(
        functools.partial(assemble_kernel, parts=len(parts)),
        out_shape=[
            jax.ShapeDtypeStruct(parts[0].shape, jnp.float32),
            jax.ShapeDtypeStruct((len(pieces) * size + 8, wide), jnp.float32),
        ],
        in_specs=[VMEM] * (len(parts) + len(pieces) + 2),
        out_specs=[VMEM] * 2,
        compiler_params=PARAMS,
        name="assemble",
    )(columns, rows, *parts, *pieces)


def solve_rows(rows, uppers, inverses, out_ref):
    count = rows.shape[1] // BLOCK
    done = count // 2
    here = [slice(k * BLOCK, (k + 1) * BLOCK) for k in range(count)]
    left = [rows[:, h] for h in here]
    for k in range(count):
        solved = exact_nt(left[k], inverses[k // done][k % done])
        out_ref[:, here[k]] = solved
        for j in range(k + 1, count):
            left[j] = left[j] - exact(solved, uppers[k // done][here[k % done], here[j]])


def panel_kernel(*refs, group):
    groups = refs[:-5]
    out_ref = refs[-1]
    uppers, inverses = refs[-5:-3], refs[-3:-1]
    rows_here, width = out_ref.shape
    first = lax.axis_index("scen") * rows_here
    total = jnp.zeros((rows_here, width), jnp.float32)
    for group_ref in groups:
        wide = group_ref.shape[1]
        size = (group_ref.shape[0] - 8) // group
        index = group_ref[group * size :, :]
        spreads = []
        for i in range(group):
            columns = index[i : i + 1, :].astype(jnp.int32)
            spread = lax.broadcasted_iota(jnp.int32, (width, wide), 0) == columns
            high, low = split_two(group_ref[i * size : (i + 1) * size, :])
            both = matmul_nt(
                jnp.concatenate([high, low], 0), spread.astype(jnp.bfloat16)
            )
            spreads.append(both[:size] + both[size:])
        widened = jnp.concatenate(spreads, 0)
        row_index = index[group : group + 1, : group * size].astype(jnp.int32) - first
        row_map = (
            lax.broadcasted_iota(jnp.int32, (rows_here, group * size), 0) == row_index
        ).astype(jnp.bfloat16)
        high, low = split_two(widened)
        total = total + (matmul(row_map, high) + matmul(row_map, low))
    solve_rows(total, uppers, inverses, out_ref)


def panel_rows_of(groups, group, uppers, inverses, rows_here):
    return pl.pallas_call(
        functools.partial(panel_kernel, group=group),
        out_shape=jax.ShapeDtypeStruct((rows_here, uppers[0].shape[1]), jnp.float32),
        in_specs=[VMEM] * (len(groups) + 4),
        out_specs=VMEM,
        compiler_params=PARAMS,
        name="panel",
    )(*groups, *uppers, *inverses)


def dense_panel(couplings_here, rows, columns, rows_panel, width):
    def step(running, operands):
        coupling, row_index, column_index = operands
        column_map = (column_index[:, None] == jnp.arange(width)[None, :]).astype(jnp.float32)
        row_map = (row_index[:, None] == jnp.arange(rows_panel)[None, :]).astype(jnp.float32)
        widened = jnp.dot(coupling, column_map, precision=HIGHEST)
        return running + jnp.einsum("br,bd->rd", row_map, widened, precision=HIGHEST), None

    zero = jnp.zeros((rows_panel, width), jnp.float32)
    total, _ = lax.scan(step, zero, (couplings_here, rows, columns))
    return lax.psum_scatter(total, "scen", scatter_dimension=0, tiled=True)


def dense_solve(rows, upper, inverse):
    width = rows.shape[1]
    solved = []
    for k in range(width // BLOCK):
        here = slice(k * BLOCK, (k + 1) * BLOCK)
        left = rows[:, here]
        if k > 0:
            left = left - jnp.dot(
                jnp.concatenate(solved, 1), upper[: k * BLOCK, here], precision=HIGHEST
            )
        solved.append(jnp.dot(left, inverse[k].T, precision=HIGHEST))
    return jnp.concatenate(solved, 1)


def shards(
    rows_here,
    inverse_factor,
    true_orders,
    slab_border,
    slab_columns,
    panel_border,
    panel_rows,
    barrier_diag,
):
    scen_count = lax.axis_size("scen")
    col_count = lax.axis_size("col")
    place = lax.axis_index("col")
    width = barrier_diag.shape[0]
    group, size, depth = panel_border.shape[1:]
    wide = slab_columns.shape[1]

    order = [place ^ m for m in range(col_count)]
    own_borders = [
        lax.dynamic_index_in_dim(panel_border[0], order[m], 0, keepdims=False)
        for m in range(col_count)
    ]
    borders = [own_borders[0]] + [swap(own_borders[m], "col", m) for m in range(1, col_count)]

    moved, keep, send = front(true_orders, inverse_factor, slab_border, slab_columns, width)
    got = swap(send, "scen", 1)
    parts = quarters(keep, got, col_count)
    parts = [parts[0]] + [swap(parts[m], "col", m) for m in range(1, col_count)]
    part, partial = sum_and_couplings(parts, moved, borders)
    mine = [partial[0]] + [swap(partial[m], "col", m) for m in range(1, col_count)]
    parts = [part] + [swap(part, "scen", 2 * m) for m in range(1, scen_count // 2)]
    rows_panel = rows_here * scen_count
    fits = group < 8 and group == col_count and group * size <= wide
    sparse = fits and scen_count * group * size * wide < rows_panel * width
    if sparse:
        part, own = sum_and_assemble(parts, mine, slab_columns, panel_rows)
    else:
        part = tree_sum(parts)
    pieces = [part] + [swap(part, "col", m) for m in range(1, col_count)]
    pieces = pieces + [swap(piece, "scen", 1) for piece in pieces]
    early, early_inverse, rest = early_cholesky(pieces, barrier_diag)

    if sparse:
        near = [own] + [swap(own, "scen", 2 * m) for m in range(1, scen_count // 2)]
        late, late_inverse, factor_rows = late_cholesky(early, rest, col_count, near[1:])
        groups = near + [swap(value, "scen", 1) for value in near]
        solved = panel_rows_of(
            groups, group, (early, late), (early_inverse, late_inverse), rows_here
        )
    else:
        order = jnp.stack(order)
        rows = dense_panel(
            jnp.stack(mine), panel_rows[0][order], slab_columns[order], rows_panel, width
        )
        late, late_inverse, factor_rows = late_cholesky(early, rest, col_count, [])
        solved = dense_solve(
            rows,
            jnp.concatenate([early, late], 0),
            jnp.concatenate([early_inverse, late_inverse], 0),
        )
    return factor_rows, solved


def solution(mesh):
    in_specs = (
        P(("scen", "col"), None, None),
        P(("scen", "col")),
        P(("scen", "col"), None, None),
        P("scen", None),
        P("col", "scen", None, None),
        P("col", "scen", None),
        P(),
    )
    out_specs = (P("col", None), P(("scen", "col"), None))

    def whole(*args):
        devices = mesh.shape["scen"] * mesh.shape["col"]
        first_section = NF - args[-1].shape[0]
        body = functools.partial(shards, first_section // devices)
        return jax.shard_map(
            body, mesh=mesh, in_specs=in_specs, out_specs=out_specs, check_vma=False
        )(*args)

    return whole
```

```python
import functools

import jax
import jax.numpy as jnp
from jax import lax
from jax.experimental import pallas as pl
from jax.experimental.pallas import tpu as pltpu
from jax.sharding import PartitionSpec as P

NF = 8192
BLOCK = 128
HIGHEST = lax.Precision.HIGHEST
VMEM = pl.BlockSpec(memory_space=pltpu.VMEM)
SMEM = pl.BlockSpec(memory_space=pltpu.SMEM)
HBM = pl.BlockSpec(memory_space=pltpu.HBM)
PARAMS = pltpu.CompilerParams(vmem_limit_bytes=40 * 2**20)


def long_cost(micros):
    return pl.CostEstimate(flops=micros * 10**9, bytes_accessed=2**20, transcendentals=0)


def in_hbm(value):
    return pltpu.with_memory_space_constraint(value, pltpu.HBM)


def split_two(value):
    high = value.astype(jnp.bfloat16)
    low = (value - high.astype(jnp.float32)).astype(jnp.bfloat16)
    return high, low


def matmul(left, right):
    return jnp.dot(left, right, preferred_element_type=jnp.float32)


def matmul_nt(left, right):
    return lax.dot_general(
        left, right, (((1,), (1,)), ((), ())), preferred_element_type=jnp.float32
    )


def exact_tn(left, right):
    return lax.dot_general(
        left,
        right,
        (((0,), (0,)), ((), ())),
        precision=HIGHEST,
        preferred_element_type=jnp.float32,
    )


def exact(left, right):
    return jnp.dot(left, right, precision=HIGHEST, preferred_element_type=jnp.float32)


def exact_nt(left, right):
    return lax.dot_general(
        left,
        right,
        (((1,), (1,)), ((), ())),
        precision=HIGHEST,
        preferred_element_type=jnp.float32,
    )


def upper_blocks(width):
    count = width // BLOCK
    return [(i, j) for i in range(count) for j in range(i, count)]


def front_kernel(
    order_ref,
    columns_ref,
    factor_ref,
    border_ref,
    wait_ref,
    moved_ref,
    keep_ref,
    send_ref,
    packed_ref,
    factor_here,
    border_here,
    columns_here,
    sems,
    *,
    width,
):
    depth = factor_here.shape[0]
    chunk = depth // 4
    chunks = [slice(k * chunk, (k + 1) * chunk) for k in range(4)]
    loads = [pltpu.make_async_copy(border_ref.at[0], border_here, sems.at[0])]
    columns_load = pltpu.make_async_copy(columns_ref, columns_here, sems.at[5])
    columns_load.start()
    for k, at in enumerate(chunks):
        loads.append(
            pltpu.make_async_copy(factor_ref.at[0, at], factor_here.at[at], sems.at[k + 1])
        )
    for load in loads:
        load.start()
    core = lax.rem(lax.axis_index("scen"), 2)
    place = lax.axis_index("col")
    order = order_ref[0]
    columns_load.wait()
    columns = columns_here[pl.ds(place, 1), :]
    spread = (
        lax.broadcasted_iota(jnp.int32, (width, columns.shape[1]), 0) == columns
    ).astype(jnp.bfloat16)
    loads[0].wait()
    border = border_here[...]
    within = lax.broadcasted_iota(jnp.int32, border.shape, 1) < order
    inside = jnp.where(within, border.astype(jnp.float32), 0.0).astype(jnp.bfloat16)
    product = jnp.zeros(border.shape, jnp.float32)
    for k, at in enumerate(chunks):
        loads[k + 1].wait()
        product = product + matmul(inside[:, at], factor_here[at])
    moved = jnp.where(within, product, 0.0).astype(jnp.bfloat16)
    moved_ref[...] = moved
    terms = 0.5 * (matmul_nt(border, moved) + matmul_nt(moved, border))
    high, low = split_two(terms)
    half_spread = matmul_nt(high, spread) + matmul_nt(low, spread)
    high, low = split_two(half_spread)
    row = 0
    for i in range(width // BLOCK):
        rows = spread[i * BLOCK : (i + 1) * BLOCK]
        part = matmul(rows, high[:, i * BLOCK :]) + matmul(rows, low[:, i * BLOCK :])
        for j in range(i, width // BLOCK):
            packed_ref[row : row + BLOCK, :] = part[:, (j - i) * BLOCK : (j - i + 1) * BLOCK]
            row += BLOCK
    half = keep_ref.shape[0]
    keep_ref[...] = packed_ref[pl.ds(pl.multiple_of(core * half, 8), half), :]
    send_ref[...] = packed_ref[pl.ds(pl.multiple_of((1 - core) * half, 8), half), :]


def front(order, columns, factor, border, width, wait):
    total = len(upper_blocks(width)) * BLOCK
    half = jax.ShapeDtypeStruct((total // 2, BLOCK), jnp.float32)
    return pl.pallas_call(
        functools.partial(front_kernel, width=width),
        out_shape=[jax.ShapeDtypeStruct(border.shape[1:], jnp.bfloat16), half, half],
        in_specs=[SMEM, HBM, HBM, HBM, VMEM],
        out_specs=[VMEM, VMEM, VMEM],
        scratch_shapes=[
            pltpu.VMEM((total, BLOCK), jnp.float32),
            pltpu.VMEM(factor.shape[1:], factor.dtype),
            pltpu.VMEM(border.shape[1:], border.dtype),
            pltpu.VMEM(columns.shape, columns.dtype),
            pltpu.SemaphoreType.DMA((6,)),
        ],
        compiler_params=PARAMS,
        cost_estimate=long_cost(20),
        name="front",
    )(order, in_hbm(columns), in_hbm(factor), in_hbm(border), wait)


def deal_kernel(border_ref, *refs):
    out_refs, sems = refs[:-1], refs[-1]
    place = lax.axis_index("col")
    loads = [
        pltpu.make_async_copy(border_ref.at[0, place ^ m], out_ref, sems.at[m])
        for m, out_ref in enumerate(out_refs)
    ]
    for load in loads:
        load.start()
    for load in loads:
        load.wait()


def deal(border):
    count = border.shape[1]
    return pl.pallas_call(
        deal_kernel,
        out_shape=[jax.ShapeDtypeStruct(border.shape[2:], border.dtype)] * count,
        in_specs=[HBM],
        out_specs=[VMEM] * count,
        scratch_shapes=[pltpu.SemaphoreType.DMA((count,))],
        compiler_params=PARAMS,
        name="deal",
    )(in_hbm(border))


def quarter_kernel(keep_ref, got_ref, moved_ref, *refs):
    count = (len(refs) - 1) // 2
    borders, own_ref, out_refs = refs[:count], refs[count], refs[count + 1 :]
    place = lax.axis_index("col")
    rows = out_refs[0].shape[0]
    size, wide = own_ref.shape
    moved = moved_ref[...]
    for m, (border_ref, out_ref) in enumerate(zip(borders, out_refs)):
        at = pl.ds(pl.multiple_of((place ^ m) * rows, 8), rows)
        if m > 0:
            rows = out_ref.shape[0] - wide // BLOCK * size
            at = pl.ds(pl.multiple_of((place ^ m) * rows, 8), rows)
        coupling = matmul_nt(border_ref[...], moved)
        out_ref[:rows, :] = keep_ref[at, :] + got_ref[at, :]
        if m == 0:
            own_ref[...] = coupling
            continue
        for n in range(wide // BLOCK):
            out_ref[rows + n * size : rows + (n + 1) * size, :] = coupling[
                :, n * BLOCK : (n + 1) * BLOCK
            ]


def quarters(keep, got, moved, borders):
    count = len(borders)
    rows = keep.shape[0] // count
    size, wide = borders[0].shape[0], moved.shape[0]
    rider = wide // BLOCK * size
    out_shape = [jax.ShapeDtypeStruct((size, wide), jnp.float32)]
    out_shape += [jax.ShapeDtypeStruct((rows, BLOCK), jnp.float32)]
    out_shape += [jax.ShapeDtypeStruct((rows + rider, BLOCK), jnp.float32)] * (count - 1)
    own, *parts = pl.pallas_call(
        quarter_kernel,
        out_shape=out_shape,
        in_specs=[VMEM] * (3 + count),
        out_specs=[VMEM] * (1 + count),
        compiler_params=PARAMS,
        name="quarters",
    )(keep, got, moved, *borders)
    return own, parts


def swap(value, axis, step):
    count = lax.axis_size(axis)
    return lax.ppermute(value, axis, [(i, i ^ step) for i in range(count)])


def tree_sum(values):
    while len(values) > 1:
        values = [values[i] + values[i + 1] for i in range(0, len(values), 2)]
    return values[0]


def row_of(tile, i):
    return jnp.broadcast_to(tile[i : i + 1, :], tile.shape)


def column_of(tile, j):
    return jnp.broadcast_to(tile[:, j : j + 1], (tile.shape[0], BLOCK))


def factor_block(block):
    groups = BLOCK // 8
    sub = lax.broadcasted_iota(jnp.int32, (8, BLOCK), 0)
    lane = lax.broadcasted_iota(jnp.int32, (8, BLOCK), 1)
    left = [block[8 * t : 8 * t + 8, :] for t in range(groups)]
    right = [(lane == sub + 8 * t).astype(jnp.float32) for t in range(groups)]
    upper = []
    inverse = []
    for g in range(groups):
        a, b = left[g], right[g]
        near = [column_of(a, 8 * g + m) for m in range(8)]
        out_a, out_b = a, b
        for i in range(8):
            pivot = row_of(near[i], i)
            recip = 1.0 / pivot
            root = lax.rsqrt(pivot)
            factor = jnp.where(sub == i, 1.0 - recip, near[i] * recip)
            row_a, row_b = row_of(a, i), row_of(b, i)
            out_a = jnp.where(sub == i, row_a * root, out_a)
            out_b = jnp.where(sub == i, row_b * root, out_b)
            for m in range(i + 1, 8):
                near[m] = near[m] - factor * row_of(near[m], i)
            a = a - factor * row_a
            b = b - factor * row_b
        upper.append(jnp.where(lane >= sub + 8 * g, out_a, 0.0))
        inverse.append(out_b)
        if g + 1 < groups:
            rows_a = [row_of(a, i) for i in range(8)]
            rows_b = [row_of(b, i) for i in range(8)]
            for t in range(g + 1, groups):
                weights = [column_of(left[t], 8 * g + i) for i in range(8)]
                sum_a = weights[0] * rows_a[0]
                sum_b = weights[0] * rows_b[0]
                for i in range(1, 8):
                    sum_a = sum_a + weights[i] * rows_a[i]
                    sum_b = sum_b + weights[i] * rows_b[i]
                left[t] = left[t] - sum_a
                right[t] = right[t] - sum_b
    return jnp.concatenate(upper, 0), jnp.concatenate(inverse, 0)


def eliminate(panels, first, last, upper_ref, inverse_ref):
    count = len(panels)
    for i in range(first, last):
        here = slice((i - first) * BLOCK, (i - first + 1) * BLOCK)
        own, inverse = factor_block(panels[i][:, :BLOCK])
        if i > 0:
            upper_ref[here, : i * BLOCK] = jnp.zeros((BLOCK, i * BLOCK), jnp.float32)
        upper_ref[here, i * BLOCK : (i + 1) * BLOCK] = own
        inverse_ref[i - first] = inverse
        if i + 1 < count:
            rest = exact(inverse, panels[i][:, BLOCK:])
            upper_ref[here, (i + 1) * BLOCK :] = rest
            for j in range(i + 1, count):
                at = (j - i - 1) * BLOCK
                panels[j] = panels[j] - exact_tn(rest[:, at : at + BLOCK], rest[:, at:])


def cholesky_kernel(*refs, col_count):
    pieces = refs[: 2 * col_count]
    barrier_ref, upper_ref, inverse_ref, slice_ref, packed_ref, turned_ref = refs[2 * col_count :]
    width = barrier_ref.shape[1]
    count = width // BLOCK
    rows = pieces[0].shape[0]
    core = lax.rem(lax.axis_index("scen"), 2)
    place = lax.axis_index("col")
    for side in range(2):
        owner = core if side == 0 else 1 - core
        for m in range(col_count):
            at = (owner * col_count + (place ^ m)) * rows
            packed_ref[pl.ds(pl.multiple_of(at, 8), rows), :] = pieces[side * col_count + m][...]
    diagonal = lax.broadcasted_iota(jnp.int32, (BLOCK, BLOCK), 0) == lax.broadcasted_iota(
        jnp.int32, (BLOCK, BLOCK), 1
    )
    blocks = {}
    for n, (i, j) in enumerate(upper_blocks(width)):
        blocks[i, j] = packed_ref[n * BLOCK : (n + 1) * BLOCK, :]
        if i == j:
            extra = barrier_ref[:, i * BLOCK : (i + 1) * BLOCK]
            blocks[i, j] = blocks[i, j] + jnp.where(diagonal, extra, 0.0)
    panels = [jnp.concatenate([blocks[i, j] for j in range(i, count)], 1) for i in range(count)]
    eliminate(panels, 0, count, upper_ref, inverse_ref)
    slice_rows = slice_ref.shape[0]
    start = place * slice_rows
    block = pl.ds(pl.multiple_of(start // BLOCK * BLOCK, BLOCK), BLOCK)
    turned_ref[...] = upper_ref[:, block].T
    slice_ref[...] = turned_ref[pl.ds(pl.multiple_of(lax.rem(start, BLOCK), 8), slice_rows), :]


def cholesky(pieces, barrier):
    width = barrier.shape[0]
    col_count = len(pieces) // 2
    return pl.pallas_call(
        functools.partial(cholesky_kernel, col_count=col_count),
        out_shape=[
            jax.ShapeDtypeStruct((width, width), jnp.float32),
            jax.ShapeDtypeStruct((width // BLOCK, BLOCK, BLOCK), jnp.float32),
            jax.ShapeDtypeStruct((width // col_count, width), jnp.float32),
        ],
        in_specs=[VMEM] * (len(pieces) + 1),
        out_specs=[VMEM] * 3,
        scratch_shapes=[
            pltpu.VMEM((len(upper_blocks(width)) * BLOCK, BLOCK), jnp.float32),
            pltpu.VMEM((BLOCK, width), jnp.float32),
        ],
        compiler_params=PARAMS,
        cost_estimate=long_cost(40),
        name="cholesky",
    )(*pieces, barrier[None])


def assemble_kernel(columns_ref, rows_ref, own_ref, *refs):
    parts, total_ref, out_ref = refs[:-2], refs[-2], refs[-1]
    rows = total_ref.shape[0]
    total_ref[...] = tree_sum([part[:rows, :] for part in parts])
    place = lax.axis_index("col")
    size, wide = own_ref.shape
    count = len(parts)
    out_ref[pl.ds(pl.multiple_of(place * size, 8), size), :] = own_ref[...]
    for m in range(1, count):
        at = pl.ds(pl.multiple_of((place ^ m) * size, 8), size)
        for n in range(wide // BLOCK):
            out_ref[at, n * BLOCK : (n + 1) * BLOCK] = parts[m][
                rows + n * size : rows + (n + 1) * size, :
            ]
    out_ref[count * size :, :] = jnp.zeros((out_ref.shape[0] - count * size, wide), jnp.float32)
    out_ref[count * size : count * size + count, :] = columns_ref[...].astype(jnp.float32)
    at = count * size + count
    out_ref[at : at + count, :size] = rows_ref[0].astype(jnp.float32)


def sum_and_assemble(parts, own, columns, rows):
    size, wide = own.shape
    return pl.pallas_call(
        assemble_kernel,
        out_shape=[
            jax.ShapeDtypeStruct(parts[0].shape, jnp.float32),
            jax.ShapeDtypeStruct((len(parts) * size + -(-len(parts) // 4) * 8, wide), jnp.float32),
        ],
        in_specs=[VMEM] * (len(parts) + 3),
        out_specs=[VMEM] * 2,
        compiler_params=PARAMS,
        name="assemble",
    )(columns, rows, own, *parts)


def solve_rows(rows, upper, inverse, out_ref):
    count = rows.shape[1] // BLOCK
    here = [slice(k * BLOCK, (k + 1) * BLOCK) for k in range(count)]
    left = [rows[:, h] for h in here]
    for k in range(count):
        solved = exact_nt(left[k], inverse[k])
        out_ref[:, here[k]] = solved
        for j in range(k + 1, count):
            left[j] = left[j] - exact(solved, upper[here[k], here[j]])


def panel_kernel(source_ref, upper_ref, inverse_ref, out_ref, groups_ref, sems, *, group):
    loads = [
        pltpu.make_async_copy(source_ref.at[s], groups_ref.at[s], sems.at[s])
        for s in range(source_ref.shape[0])
    ]
    for load in loads:
        load.start()
    rows_here, width = out_ref.shape
    first = lax.axis_index("scen") * rows_here
    total = jnp.zeros((rows_here, width), jnp.float32)
    size = (groups_ref.shape[1] - 2 * group) // group
    wide = groups_ref.shape[2]
    for s in range(groups_ref.shape[0]):
        loads[s].wait()
        index = groups_ref[s, group * size :, :]
        spreads = []
        for i in range(group):
            columns = index[i : i + 1, :].astype(jnp.int32)
            spread = lax.broadcasted_iota(jnp.int32, (width, wide), 0) == columns
            high, low = split_two(groups_ref[s, i * size : (i + 1) * size, :])
            both = matmul_nt(jnp.concatenate([high, low], 0), spread.astype(jnp.bfloat16))
            spreads.append(both[:size] + both[size:])
        widened = jnp.concatenate(spreads, 0)
        row_index = jnp.concatenate(
            [index[group + i : group + i + 1, :size] for i in range(group)], 1
        )
        row_index = row_index.astype(jnp.int32) - first
        row_map = (
            lax.broadcasted_iota(jnp.int32, (rows_here, group * size), 0) == row_index
        ).astype(jnp.bfloat16)
        high, low = split_two(widened)
        total = total + (matmul(row_map, high) + matmul(row_map, low))
    solve_rows(total, upper_ref, inverse_ref, out_ref)


def panel_rows_of(groups, group, upper, inverse, rows_here):
    return pl.pallas_call(
        functools.partial(panel_kernel, group=group),
        out_shape=jax.ShapeDtypeStruct((rows_here, upper.shape[1]), jnp.float32),
        in_specs=[HBM, VMEM, VMEM],
        out_specs=VMEM,
        scratch_shapes=[
            pltpu.VMEM(groups.shape, groups.dtype),
            pltpu.SemaphoreType.DMA((groups.shape[0],)),
        ],
        compiler_params=PARAMS,
        name="panel",
    )(in_hbm(groups), upper, inverse)


def dense_panel(couplings_here, rows, columns, rows_panel, width):
    def step(running, operands):
        coupling, row_index, column_index = operands
        column_map = (column_index[:, None] == jnp.arange(width)[None, :]).astype(jnp.float32)
        row_map = (row_index[:, None] == jnp.arange(rows_panel)[None, :]).astype(jnp.float32)
        widened = jnp.dot(coupling, column_map, precision=HIGHEST)
        return running + jnp.einsum("br,bd->rd", row_map, widened, precision=HIGHEST), None

    zero = jnp.zeros((rows_panel, width), jnp.float32)
    total, _ = lax.scan(step, zero, (couplings_here, rows, columns))
    return lax.psum_scatter(total, "scen", scatter_dimension=0, tiled=True)


def dense_solve(rows, upper, inverse):
    width = rows.shape[1]
    solved = []
    for k in range(width // BLOCK):
        here = slice(k * BLOCK, (k + 1) * BLOCK)
        left = rows[:, here]
        if k > 0:
            left = left - jnp.dot(
                jnp.concatenate(solved, 1), upper[: k * BLOCK, here], precision=HIGHEST
            )
        solved.append(jnp.dot(left, inverse[k].T, precision=HIGHEST))
    return jnp.concatenate(solved, 1)


def shards(
    rows_here,
    inverse_factor,
    true_orders,
    slab_border,
    slab_columns,
    panel_border,
    panel_rows,
    barrier_diag,
):
    scen_count = lax.axis_size("scen")
    col_count = lax.axis_size("col")
    width = barrier_diag.shape[0]
    group, size = panel_border.shape[1:3]
    wide = slab_columns.shape[1]

    dealt = deal(panel_border)
    borders = [dealt[0]] + [swap(dealt[m], "col", m) for m in range(1, col_count)]
    moved, keep, send = front(
        true_orders, slab_columns, inverse_factor, slab_border, width, dealt[0]
    )
    got = swap(send, "scen", 1)
    own, parts = quarters(keep, got, moved, borders)
    parts = [parts[0]] + [swap(parts[m], "col", m) for m in range(1, col_count)]
    part, own = sum_and_assemble(parts, own, slab_columns, panel_rows)
    rows_panel = rows_here * scen_count
    sparse = scen_count * group * size * wide < rows_panel * width
    if sparse:
        groups = lax.all_gather(own, "scen")
    part = tree_sum([part] + [swap(part, "scen", 2 * m) for m in range(1, scen_count // 2)])
    pieces = [part] + [swap(part, "col", m) for m in range(1, col_count)]
    pieces = pieces + [swap(piece, "scen", 1) for piece in pieces]
    upper, inverse, factor_rows = cholesky(pieces, barrier_diag)
    if sparse:
        solved = panel_rows_of(groups, group, upper, inverse, rows_here)
    else:
        local = own[: group * size].reshape(group, size, wide)
        rows = dense_panel(local, panel_rows[0], slab_columns, rows_panel, width)
        solved = dense_solve(rows, upper, inverse)
    return factor_rows, solved


def solution(mesh):
    in_specs = (
        P(("scen", "col"), None, None),
        P(("scen", "col")),
        P(("scen", "col"), None, None),
        P("scen", None),
        P("col", "scen", None, None),
        P("col", "scen", None),
        P(),
    )
    out_specs = (P("col", None), P(("scen", "col"), None))

    def whole(*args):
        devices = mesh.shape["scen"] * mesh.shape["col"]
        first_section = NF - args[-1].shape[0]
        body = functools.partial(shards, first_section // devices)
        return jax.shard_map(
            body, mesh=mesh, in_specs=in_specs, out_specs=out_specs, check_vma=False
        )(*args)

    return whole
```

```python
import functools

import jax
import jax.numpy as jnp
from jax import lax
from jax.experimental import pallas as pl
from jax.experimental.pallas import tpu as pltpu
from jax.sharding import PartitionSpec as P

NF = 8192
BLOCK = 128
HIGHEST = lax.Precision.HIGHEST
VMEM = pl.BlockSpec(memory_space=pltpu.VMEM)
SMEM = pl.BlockSpec(memory_space=pltpu.SMEM)
HBM = pl.BlockSpec(memory_space=pltpu.HBM)
PARAMS = pltpu.CompilerParams(vmem_limit_bytes=40 * 2**20)


def long_cost(micros):
    return pl.CostEstimate(flops=micros * 10**9, bytes_accessed=2**20, transcendentals=0)


def in_hbm(value):
    return pltpu.with_memory_space_constraint(value, pltpu.HBM)


def split_two(value):
    high = value.astype(jnp.bfloat16)
    low = (value - high.astype(jnp.float32)).astype(jnp.bfloat16)
    return high, low


def matmul(left, right):
    return jnp.dot(left, right, preferred_element_type=jnp.float32)


def matmul_nt(left, right):
    return lax.dot_general(
        left, right, (((1,), (1,)), ((), ())), preferred_element_type=jnp.float32
    )


def exact_tn(left, right):
    return lax.dot_general(
        left,
        right,
        (((0,), (0,)), ((), ())),
        precision=HIGHEST,
        preferred_element_type=jnp.float32,
    )


def exact(left, right):
    return jnp.dot(left, right, precision=HIGHEST, preferred_element_type=jnp.float32)


def exact_nt(left, right):
    return lax.dot_general(
        left,
        right,
        (((1,), (1,)), ((), ())),
        precision=HIGHEST,
        preferred_element_type=jnp.float32,
    )


def upper_blocks(width):
    count = width // BLOCK
    return [(i, j) for i in range(count) for j in range(i, count)]


def moved_kernel(order_ref, factor_ref, border_ref, moved_ref, factor_here, border_here, sems):
    depth = factor_here.shape[0]
    chunk = depth // 4
    chunks = [slice(k * chunk, (k + 1) * chunk) for k in range(4)]
    loads = [pltpu.make_async_copy(border_ref.at[0], border_here, sems.at[0])]
    for k, at in enumerate(chunks):
        loads.append(
            pltpu.make_async_copy(factor_ref.at[0, at], factor_here.at[at], sems.at[k + 1])
        )
    for load in loads:
        load.start()
    order = order_ref[0]
    loads[0].wait()
    border = border_here[...]
    within = lax.broadcasted_iota(jnp.int32, border.shape, 1) < order
    inside = jnp.where(within, border.astype(jnp.float32), 0.0).astype(jnp.bfloat16)
    product = jnp.zeros(border.shape, jnp.float32)
    for k, at in enumerate(chunks):
        loads[k + 1].wait()
        product = product + matmul(inside[:, at], factor_here[at])
    moved_ref[0] = jnp.where(within, product, 0.0).astype(jnp.bfloat16)
    moved_ref[1] = border


def transform(order, factor, border):
    return pl.pallas_call(
        moved_kernel,
        out_shape=jax.ShapeDtypeStruct((2,) + border.shape[1:], jnp.bfloat16),
        in_specs=[SMEM, HBM, HBM],
        out_specs=VMEM,
        scratch_shapes=[
            pltpu.VMEM(factor.shape[1:], factor.dtype),
            pltpu.VMEM(border.shape[1:], border.dtype),
            pltpu.SemaphoreType.DMA((5,)),
        ],
        compiler_params=PARAMS,
        cost_estimate=long_cost(20),
        name="transform",
    )(order, in_hbm(factor), in_hbm(border))


def front_kernel(columns_ref, moved_ref, *refs, width):
    count = (len(refs) - 3) // 2
    borders, couplings = refs[:count], refs[count : 2 * count]
    keep_ref, send_ref, packed_ref = refs[2 * count :]
    core = lax.rem(lax.axis_index("scen"), 2)
    place = lax.axis_index("col")
    columns = columns_ref[pl.ds(place, 1), :]
    spread = (
        lax.broadcasted_iota(jnp.int32, (width, columns.shape[1]), 0) == columns
    ).astype(jnp.bfloat16)
    moved, border = moved_ref[0], moved_ref[1]
    for panel_ref, coupling_ref in zip(borders, couplings):
        coupling_ref[...] = matmul_nt(panel_ref[...], moved)
    terms = 0.5 * (matmul_nt(border, moved) + matmul_nt(moved, border))
    high, low = split_two(terms)
    half_spread = matmul_nt(high, spread) + matmul_nt(low, spread)
    high, low = split_two(half_spread)
    row = 0
    for i in range(width // BLOCK):
        rows = spread[i * BLOCK : (i + 1) * BLOCK]
        part = matmul(rows, high[:, i * BLOCK :]) + matmul(rows, low[:, i * BLOCK :])
        for j in range(i, width // BLOCK):
            packed_ref[row : row + BLOCK, :] = part[:, (j - i) * BLOCK : (j - i + 1) * BLOCK]
            row += BLOCK
    half = keep_ref.shape[0]
    keep_ref[...] = packed_ref[pl.ds(pl.multiple_of(core * half, 8), half), :]
    send_ref[...] = packed_ref[pl.ds(pl.multiple_of((1 - core) * half, 8), half), :]


def front(columns, moved, width, borders):
    total = len(upper_blocks(width)) * BLOCK
    half = jax.ShapeDtypeStruct((total // 2, BLOCK), jnp.float32)
    coupling = jax.ShapeDtypeStruct((borders[0].shape[0], moved.shape[1]), jnp.float32)
    *couplings, keep, send = pl.pallas_call(
        functools.partial(front_kernel, width=width),
        out_shape=[coupling] * len(borders) + [half, half],
        in_specs=[VMEM] * (len(borders) + 2),
        out_specs=[VMEM] * (len(borders) + 2),
        scratch_shapes=[pltpu.VMEM((total, BLOCK), jnp.float32)],
        compiler_params=PARAMS,
        name="front",
    )(columns, moved, *borders)
    return couplings, keep, send


def deal_kernel(border_ref, *refs):
    out_refs, sems = refs[:-1], refs[-1]
    place = lax.axis_index("col")
    loads = [
        pltpu.make_async_copy(border_ref.at[0, place ^ m], out_ref, sems.at[m])
        for m, out_ref in enumerate(out_refs)
    ]
    for load in loads:
        load.start()
    for load in loads:
        load.wait()


def deal(border):
    count = border.shape[1]
    return pl.pallas_call(
        deal_kernel,
        out_shape=[jax.ShapeDtypeStruct(border.shape[2:], border.dtype)] * count,
        in_specs=[HBM],
        out_specs=[VMEM] * count,
        scratch_shapes=[pltpu.SemaphoreType.DMA((count,))],
        compiler_params=PARAMS,
        name="deal",
    )(in_hbm(border))


def quarter_kernel(keep_ref, got_ref, *refs):
    count = (len(refs) + 1) // 2
    riders, out_refs = refs[: count - 1], refs[count - 1 :]
    place = lax.axis_index("col")
    rows = out_refs[0].shape[0]
    for m, out_ref in enumerate(out_refs):
        at = pl.ds(pl.multiple_of((place ^ m) * rows, 8), rows)
        out_ref[:rows, :] = keep_ref[at, :] + got_ref[at, :]
        if m > 0:
            size, wide = riders[m - 1].shape
            for n in range(wide // BLOCK):
                out_ref[rows + n * size : rows + (n + 1) * size, :] = riders[m - 1][
                    :, n * BLOCK : (n + 1) * BLOCK
                ]


def quarters(keep, got, riders):
    count = len(riders) + 1
    rows = keep.shape[0] // count
    extra = riders[0].size // BLOCK
    out_shape = [jax.ShapeDtypeStruct((rows, BLOCK), jnp.float32)]
    out_shape += [jax.ShapeDtypeStruct((rows + extra, BLOCK), jnp.float32)] * (count - 1)
    return pl.pallas_call(
        quarter_kernel,
        out_shape=out_shape,
        in_specs=[VMEM] * (1 + count),
        out_specs=[VMEM] * count,
        compiler_params=PARAMS,
        name="quarters",
    )(keep, got, *riders)


def swap(value, axis, step):
    count = lax.axis_size(axis)
    return lax.ppermute(value, axis, [(i, i ^ step) for i in range(count)])


def tree_sum(values):
    while len(values) > 1:
        values = [values[i] + values[i + 1] for i in range(0, len(values), 2)]
    return values[0]


def row_of(tile, i):
    return jnp.broadcast_to(tile[i : i + 1, :], tile.shape)


def column_of(tile, j):
    return jnp.broadcast_to(tile[:, j : j + 1], (tile.shape[0], BLOCK))


def factor_block(block):
    groups = BLOCK // 8
    sub = lax.broadcasted_iota(jnp.int32, (8, BLOCK), 0)
    lane = lax.broadcasted_iota(jnp.int32, (8, BLOCK), 1)
    left = [block[8 * t : 8 * t + 8, :] for t in range(groups)]
    right = [(lane == sub + 8 * t).astype(jnp.float32) for t in range(groups)]
    upper = []
    inverse = []
    for g in range(groups):
        a, b = left[g], right[g]
        near = [column_of(a, 8 * g + m) for m in range(8)]
        out_a, out_b = a, b
        for i in range(8):
            pivot = row_of(near[i], i)
            recip = 1.0 / pivot
            root = lax.rsqrt(pivot)
            factor = jnp.where(sub == i, 1.0 - recip, near[i] * recip)
            row_a, row_b = row_of(a, i), row_of(b, i)
            out_a = jnp.where(sub == i, row_a * root, out_a)
            out_b = jnp.where(sub == i, row_b * root, out_b)
            for m in range(i + 1, 8):
                near[m] = near[m] - factor * row_of(near[m], i)
            a = a - factor * row_a
            b = b - factor * row_b
        upper.append(jnp.where(lane >= sub + 8 * g, out_a, 0.0))
        inverse.append(out_b)
        if g + 1 < groups:
            rows_a = [row_of(a, i) for i in range(8)]
            rows_b = [row_of(b, i) for i in range(8)]
            for t in range(g + 1, groups):
                weights = [column_of(left[t], 8 * g + i) for i in range(8)]
                sum_a = weights[0] * rows_a[0]
                sum_b = weights[0] * rows_b[0]
                for i in range(1, 8):
                    sum_a = sum_a + weights[i] * rows_a[i]
                    sum_b = sum_b + weights[i] * rows_b[i]
                left[t] = left[t] - sum_a
                right[t] = right[t] - sum_b
    return jnp.concatenate(upper, 0), jnp.concatenate(inverse, 0)


def eliminate(panels, first, last, upper_ref, inverse_ref):
    count = len(panels)
    for i in range(first, last):
        here = slice((i - first) * BLOCK, (i - first + 1) * BLOCK)
        own, inverse = factor_block(panels[i][:, :BLOCK])
        if i > 0:
            upper_ref[here, : i * BLOCK] = jnp.zeros((BLOCK, i * BLOCK), jnp.float32)
        upper_ref[here, i * BLOCK : (i + 1) * BLOCK] = own
        inverse_ref[i - first] = inverse
        if i + 1 < count:
            rest = exact(inverse, panels[i][:, BLOCK:])
            upper_ref[here, (i + 1) * BLOCK :] = rest
            for j in range(i + 1, count):
                at = (j - i - 1) * BLOCK
                panels[j] = panels[j] - exact_tn(rest[:, at : at + BLOCK], rest[:, at:])


def early_kernel(*refs, col_count):
    pieces = refs[: 2 * col_count]
    barrier_ref, upper_ref, inverse_ref, rest_ref, packed_ref = refs[2 * col_count :]
    width = barrier_ref.shape[1]
    count = width // BLOCK
    rows = pieces[0].shape[0]
    core = lax.rem(lax.axis_index("scen"), 2)
    place = lax.axis_index("col")
    for side in range(2):
        owner = core if side == 0 else 1 - core
        for m in range(col_count):
            at = (owner * col_count + (place ^ m)) * rows
            packed_ref[pl.ds(pl.multiple_of(at, 8), rows), :] = pieces[side * col_count + m][...]
    diagonal = lax.broadcasted_iota(jnp.int32, (BLOCK, BLOCK), 0) == lax.broadcasted_iota(
        jnp.int32, (BLOCK, BLOCK), 1
    )
    blocks = {}
    for n, (i, j) in enumerate(upper_blocks(width)):
        blocks[i, j] = packed_ref[n * BLOCK : (n + 1) * BLOCK, :]
        if i == j:
            extra = barrier_ref[:, i * BLOCK : (i + 1) * BLOCK]
            blocks[i, j] = blocks[i, j] + jnp.where(diagonal, extra, 0.0)
    panels = [jnp.concatenate([blocks[i, j] for j in range(i, count)], 1) for i in range(count)]
    done = inverse_ref.shape[0]
    eliminate(panels, 0, done, upper_ref, inverse_ref)
    for i in range(done, count):
        rest_ref[(i - done) * BLOCK : (i - done + 1) * BLOCK, (i - done) * BLOCK :] = panels[i]


def early_cholesky(pieces, barrier):
    width = barrier.shape[0]
    half = width // 2
    col_count = len(pieces) // 2
    return pl.pallas_call(
        functools.partial(early_kernel, col_count=col_count),
        out_shape=[
            jax.ShapeDtypeStruct((half, width), jnp.float32),
            jax.ShapeDtypeStruct((half // BLOCK, BLOCK, BLOCK), jnp.float32),
            jax.ShapeDtypeStruct((half, half), jnp.float32),
        ],
        in_specs=[VMEM] * (len(pieces) + 1),
        out_specs=[VMEM] * 3,
        scratch_shapes=[pltpu.VMEM((len(upper_blocks(width)) * BLOCK, BLOCK), jnp.float32)],
        compiler_params=PARAMS,
        cost_estimate=long_cost(20),
        name="early",
    )(*pieces, barrier[None])


def late_kernel(*refs):
    early_ref, rest_ref = refs[:2]
    upper_ref, inverse_ref, slice_ref, turned_ref = refs[-4:]
    width = early_ref.shape[1]
    count = width // BLOCK
    done = count // 2
    half = done * BLOCK
    place = lax.axis_index("col")
    panels = [None] * done + [
        rest_ref[i * BLOCK : (i + 1) * BLOCK, i * BLOCK :] for i in range(count - done)
    ]
    eliminate(panels, done, count, upper_ref, inverse_ref)
    slice_rows = slice_ref.shape[0]
    start = place * slice_rows
    block = pl.ds(pl.multiple_of(start // BLOCK * BLOCK, BLOCK), BLOCK)
    turned_ref[:, :half] = early_ref[:, block].T
    turned_ref[:, half:] = upper_ref[:, block].T
    slice_ref[...] = turned_ref[pl.ds(pl.multiple_of(lax.rem(start, BLOCK), 8), slice_rows), :]


def late_cholesky(early, rest, col_count, waits):
    half, width = early.shape
    return pl.pallas_call(
        late_kernel,
        out_shape=[
            jax.ShapeDtypeStruct((half, width), jnp.float32),
            jax.ShapeDtypeStruct((half // BLOCK, BLOCK, BLOCK), jnp.float32),
            jax.ShapeDtypeStruct((width // col_count, width), jnp.float32),
        ],
        in_specs=[VMEM, VMEM] + [HBM] * len(waits),
        out_specs=[VMEM] * 3,
        scratch_shapes=[pltpu.VMEM((BLOCK, width), jnp.float32)],
        compiler_params=PARAMS,
        cost_estimate=long_cost(20),
        name="late",
    )(early, rest, *waits)


def assemble_kernel(columns_ref, rows_ref, own_ref, *refs):
    parts, total_ref, out_ref = refs[:-2], refs[-2], refs[-1]
    rows = total_ref.shape[0]
    total_ref[...] = tree_sum([part[:rows, :] for part in parts])
    place = lax.axis_index("col")
    size, wide = own_ref.shape
    count = len(parts)
    out_ref[pl.ds(pl.multiple_of(place * size, 8), size), :] = own_ref[...]
    for m in range(1, count):
        at = pl.ds(pl.multiple_of((place ^ m) * size, 8), size)
        for n in range(wide // BLOCK):
            out_ref[at, n * BLOCK : (n + 1) * BLOCK] = parts[m][
                rows + n * size : rows + (n + 1) * size, :
            ]
    out_ref[count * size :, :] = jnp.zeros((out_ref.shape[0] - count * size, wide), jnp.float32)
    out_ref[count * size : count * size + count, :] = columns_ref[...].astype(jnp.float32)
    at = count * size + count
    out_ref[at : at + count, :size] = rows_ref[0].astype(jnp.float32)


def sum_and_assemble(parts, own, columns, rows):
    size, wide = own.shape
    return pl.pallas_call(
        assemble_kernel,
        out_shape=[
            jax.ShapeDtypeStruct(parts[0].shape, jnp.float32),
            jax.ShapeDtypeStruct((len(parts) * size + -(-len(parts) // 4) * 8, wide), jnp.float32),
        ],
        in_specs=[VMEM] * (len(parts) + 3),
        out_specs=[VMEM] * 2,
        compiler_params=PARAMS,
        name="assemble",
    )(columns, rows, own, *parts)


def build_kernel(*refs, group):
    groups = refs[1:-2]
    keep_ref, send_ref = refs[-2:]
    rows_here, width = keep_ref.shape
    place = lax.axis_index("scen")
    core = lax.rem(place, 2)
    first = (place - core) * rows_here
    size = (groups[0].shape[0] - 2 * group) // group
    wide = groups[0].shape[1]
    total = jnp.zeros((2 * rows_here, width), jnp.float32)
    slot = lax.broadcasted_iota(jnp.int32, (2 * rows_here, group * size), 0)
    for group_ref in groups:
        index = group_ref[group * size :, :]
        spreads = []
        for i in range(group):
            columns = index[i : i + 1, :].astype(jnp.int32)
            spread = lax.broadcasted_iota(jnp.int32, (width, wide), 0) == columns
            high, low = split_two(group_ref[i * size : (i + 1) * size, :])
            both = matmul_nt(jnp.concatenate([high, low], 0), spread.astype(jnp.bfloat16))
            spreads.append(both[:size] + both[size:])
        row_index = jnp.concatenate(
            [index[group + i : group + i + 1, :size] for i in range(group)], 1
        )
        row_map = (slot == row_index.astype(jnp.int32) - first).astype(jnp.bfloat16)
        high, low = split_two(jnp.concatenate(spreads, 0))
        total = total + (matmul(row_map, high) + matmul(row_map, low))
    lower, upper = total[:rows_here], total[rows_here:]
    keep_ref[...] = jnp.where(core == 0, lower, upper)
    send_ref[...] = jnp.where(core == 0, upper, lower)


def build_rows(groups, group, rows_here, width, wait):
    half = jax.ShapeDtypeStruct((rows_here, width), jnp.float32)
    return pl.pallas_call(
        functools.partial(build_kernel, group=group),
        out_shape=[half, half],
        in_specs=[HBM] + [VMEM] * len(groups),
        out_specs=[VMEM, VMEM],
        compiler_params=PARAMS,
        cost_estimate=long_cost(5),
        name="build",
    )(wait, *groups)


def solve_kernel(keep_ref, got_ref, early_ref, late_ref, first_ref, last_ref, out_ref):
    uppers, inverses = (early_ref, late_ref), (first_ref, last_ref)
    count = out_ref.shape[1] // BLOCK
    done = count // 2
    here = [slice(k * BLOCK, (k + 1) * BLOCK) for k in range(count)]
    left = [keep_ref[:, h] + got_ref[:, h] for h in here]
    for k in range(count):
        solved = exact_nt(left[k], inverses[k // done][k % done])
        out_ref[:, here[k]] = solved
        for j in range(k + 1, count):
            left[j] = left[j] - exact(solved, uppers[k // done][here[k % done], here[j]])


def solve_rows(keep, got, uppers, inverses):
    return pl.pallas_call(
        solve_kernel,
        out_shape=jax.ShapeDtypeStruct(keep.shape, jnp.float32),
        in_specs=[VMEM] * 6,
        out_specs=VMEM,
        compiler_params=PARAMS,
        name="solve",
    )(keep, got, *uppers, *inverses)


def dense_panel(couplings_here, rows, columns, rows_panel, width):
    def step(running, operands):
        coupling, row_index, column_index = operands
        column_map = (column_index[:, None] == jnp.arange(width)[None, :]).astype(jnp.float32)
        row_map = (row_index[:, None] == jnp.arange(rows_panel)[None, :]).astype(jnp.float32)
        widened = jnp.dot(coupling, column_map, precision=HIGHEST)
        return running + jnp.einsum("br,bd->rd", row_map, widened, precision=HIGHEST), None

    zero = jnp.zeros((rows_panel, width), jnp.float32)
    total, _ = lax.scan(step, zero, (couplings_here, rows, columns))
    return lax.psum_scatter(total, "scen", scatter_dimension=0, tiled=True)


def dense_solve(rows, upper, inverse):
    width = rows.shape[1]
    solved = []
    for k in range(width // BLOCK):
        here = slice(k * BLOCK, (k + 1) * BLOCK)
        left = rows[:, here]
        if k > 0:
            left = left - jnp.dot(
                jnp.concatenate(solved, 1), upper[: k * BLOCK, here], precision=HIGHEST
            )
        solved.append(jnp.dot(left, inverse[k].T, precision=HIGHEST))
    return jnp.concatenate(solved, 1)


def shards(
    rows_here,
    inverse_factor,
    true_orders,
    slab_border,
    slab_columns,
    panel_border,
    panel_rows,
    barrier_diag,
):
    scen_count = lax.axis_size("scen")
    col_count = lax.axis_size("col")
    width = barrier_diag.shape[0]
    group, size = panel_border.shape[1:3]
    wide = slab_columns.shape[1]

    dealt = deal(panel_border)
    borders = [dealt[0]] + [swap(dealt[m], "col", m) for m in range(1, col_count)]
    moved = transform(true_orders, inverse_factor, slab_border)
    couplings, keep, send = front(slab_columns, moved, width, borders)
    got = swap(send, "scen", 1)
    parts = quarters(keep, got, couplings[1:])
    parts = [parts[0]] + [swap(parts[m], "col", m) for m in range(1, col_count)]
    part, own = sum_and_assemble(parts, couplings[0], slab_columns, panel_rows)
    rows_panel = rows_here * scen_count
    sparse = scen_count * group * size * wide < rows_panel * width
    part = tree_sum([part] + [swap(part, "scen", 2 * m) for m in range(1, scen_count // 2)])
    pieces = [part] + [swap(part, "col", m) for m in range(1, col_count)]
    pieces = pieces + [swap(piece, "scen", 1) for piece in pieces]
    early, early_inverse, rest = early_cholesky(pieces, barrier_diag)
    if sparse:
        groups = [own] + [swap(own, "scen", 2 * m) for m in range(1, scen_count // 2)]
        rows, other = build_rows(groups, group, rows_here, width, rest)
        late, late_inverse, factor_rows = late_cholesky(early, rest, col_count, [other])
        solved = solve_rows(
            rows, swap(other, "scen", 1), (early, late), (early_inverse, late_inverse)
        )
    else:
        local = own[: group * size].reshape(group, size, wide)
        rows = dense_panel(local, panel_rows[0], slab_columns, rows_panel, width)
        late, late_inverse, factor_rows = late_cholesky(early, rest, col_count, [])
        solved = dense_solve(
            rows,
            jnp.concatenate([early, late], 0),
            jnp.concatenate([early_inverse, late_inverse], 0),
        )
    return factor_rows, solved


def solution(mesh):
    in_specs = (
        P(("scen", "col"), None, None),
        P(("scen", "col")),
        P(("scen", "col"), None, None),
        P("scen", None),
        P("col", "scen", None, None),
        P("col", "scen", None),
        P(),
    )
    out_specs = (P("col", None), P(("scen", "col"), None))

    def whole(*args):
        devices = mesh.shape["scen"] * mesh.shape["col"]
        first_section = NF - args[-1].shape[0]
        body = functools.partial(shards, first_section // devices)
        return jax.shard_map(
            body, mesh=mesh, in_specs=in_specs, out_specs=out_specs, check_vma=False
        )(*args)

    return whole
```

```python
import functools

import jax
import jax.numpy as jnp
from jax import lax
from jax.experimental import pallas as pl
from jax.experimental.pallas import tpu as pltpu
from jax.sharding import PartitionSpec as P

NF = 8192
BLOCK = 128
HIGHEST = lax.Precision.HIGHEST
VMEM = pl.BlockSpec(memory_space=pltpu.VMEM)
SMEM = pl.BlockSpec(memory_space=pltpu.SMEM)
HBM = pl.BlockSpec(memory_space=pltpu.HBM)
ANY = pl.BlockSpec(memory_space=pl.ANY)
PARAMS = pltpu.CompilerParams(vmem_limit_bytes=40 * 2**20)


def long_cost(micros):
    return pl.CostEstimate(flops=micros * 10**9, bytes_accessed=2**20, transcendentals=0)


def in_hbm(value):
    return pltpu.with_memory_space_constraint(value, pltpu.HBM)


def split_two(value):
    high = value.astype(jnp.bfloat16)
    low = (value - high.astype(jnp.float32)).astype(jnp.bfloat16)
    return high, low


def matmul(left, right):
    return jnp.dot(left, right, preferred_element_type=jnp.float32)


def matmul_nt(left, right):
    return lax.dot_general(
        left, right, (((1,), (1,)), ((), ())), preferred_element_type=jnp.float32
    )


def exact_tn(left, right):
    return lax.dot_general(
        left,
        right,
        (((0,), (0,)), ((), ())),
        precision=HIGHEST,
        preferred_element_type=jnp.float32,
    )


def exact(left, right):
    return jnp.dot(left, right, precision=HIGHEST, preferred_element_type=jnp.float32)


def exact_nt(left, right):
    return lax.dot_general(
        left,
        right,
        (((1,), (1,)), ((), ())),
        precision=HIGHEST,
        preferred_element_type=jnp.float32,
    )


def upper_blocks(width):
    count = width // BLOCK
    return [(i, j) for i in range(count) for j in range(i, count)]


def front_kernel(
    order_ref,
    columns_ref,
    factor_ref,
    border_ref,
    moved_ref,
    keep_ref,
    send_ref,
    packed_ref,
    factor_here,
    border_here,
    columns_here,
    sems,
    *,
    width,
):
    chunk = factor_here.shape[0] // 4
    chunks = [slice(k * chunk, (k + 1) * chunk) for k in range(4)]
    loads = [pltpu.make_async_copy(border_ref.at[0], border_here, sems.at[0])]
    for k, at in enumerate(chunks):
        loads.append(
            pltpu.make_async_copy(factor_ref.at[0, at], factor_here.at[at], sems.at[k + 1])
        )
    loads.append(pltpu.make_async_copy(columns_ref, columns_here, sems.at[5]))
    for load in loads:
        load.start()
    core = lax.rem(lax.axis_index("scen"), 2)
    place = lax.axis_index("col")
    order = order_ref[0]
    loads[0].wait()
    border = border_here[...]
    within = lax.broadcasted_iota(jnp.int32, border.shape, 1) < order
    inside = jnp.where(within, border.astype(jnp.float32), 0.0).astype(jnp.bfloat16)
    product = jnp.zeros(border.shape, jnp.float32)
    for k, at in enumerate(chunks):
        loads[k + 1].wait()
        product = product + matmul(inside[:, at], factor_here[at])
    moved = jnp.where(within, product, 0.0).astype(jnp.bfloat16)
    moved_ref[...] = moved
    loads[5].wait()
    columns = columns_here[pl.ds(place, 1), :]
    spread = (
        lax.broadcasted_iota(jnp.int32, (width, columns.shape[1]), 0) == columns
    ).astype(jnp.bfloat16)
    terms = 0.5 * (matmul_nt(border, moved) + matmul_nt(moved, border))
    high, low = split_two(terms)
    half_spread = matmul_nt(high, spread) + matmul_nt(low, spread)
    high, low = split_two(half_spread)
    row = 0
    for i in range(width // BLOCK):
        rows = spread[i * BLOCK : (i + 1) * BLOCK]
        part = matmul(rows, high[:, i * BLOCK :]) + matmul(rows, low[:, i * BLOCK :])
        for j in range(i, width // BLOCK):
            packed_ref[row : row + BLOCK, :] = part[:, (j - i) * BLOCK : (j - i + 1) * BLOCK]
            row += BLOCK
    half = keep_ref.shape[0]
    keep_ref[...] = packed_ref[pl.ds(pl.multiple_of(core * half, 8), half), :]
    send_ref[...] = packed_ref[pl.ds(pl.multiple_of((1 - core) * half, 8), half), :]


def front(order, columns, factor, border, width):
    total = len(upper_blocks(width)) * BLOCK
    half = jax.ShapeDtypeStruct((total // 2, BLOCK), jnp.float32)
    return pl.pallas_call(
        functools.partial(front_kernel, width=width),
        out_shape=[jax.ShapeDtypeStruct(border.shape[1:], jnp.bfloat16), half, half],
        in_specs=[SMEM, HBM, HBM, HBM],
        out_specs=[VMEM] * 3,
        scratch_shapes=[
            pltpu.VMEM((total, BLOCK), jnp.float32),
            pltpu.VMEM(factor.shape[1:], factor.dtype),
            pltpu.VMEM(border.shape[1:], border.dtype),
            pltpu.VMEM(columns.shape, columns.dtype),
            pltpu.SemaphoreType.DMA((6,)),
        ],
        compiler_params=PARAMS,
        cost_estimate=long_cost(20),
        name="front",
    )(order, in_hbm(columns), in_hbm(factor), in_hbm(border))


def deal_kernel(border_ref, *refs):
    out_refs, sems = refs[:-1], refs[-1]
    place = lax.axis_index("col")
    loads = [
        pltpu.make_async_copy(border_ref.at[0, place ^ m], out_ref, sems.at[m])
        for m, out_ref in enumerate(out_refs)
    ]
    for load in loads:
        load.start()
    for load in loads:
        load.wait()


def deal(border):
    count = border.shape[1]
    return pl.pallas_call(
        deal_kernel,
        out_shape=[jax.ShapeDtypeStruct(border.shape[2:], border.dtype)] * count,
        in_specs=[HBM],
        out_specs=[VMEM] * count,
        scratch_shapes=[pltpu.SemaphoreType.DMA((count,))],
        compiler_params=PARAMS,
        name="deal",
    )(in_hbm(border))


def quarter_kernel(keep_ref, got_ref, *out_refs):
    place = lax.axis_index("col")
    rows = out_refs[0].shape[0]
    for m, out_ref in enumerate(out_refs):
        at = pl.ds(pl.multiple_of((place ^ m) * rows, 8), rows)
        out_ref[...] = keep_ref[at, :] + got_ref[at, :]


def quarters(keep, got, col_count):
    piece = jax.ShapeDtypeStruct((keep.shape[0] // col_count, BLOCK), jnp.float32)
    return pl.pallas_call(
        quarter_kernel,
        out_shape=[piece] * col_count,
        in_specs=[VMEM, VMEM],
        out_specs=[VMEM] * col_count,
        compiler_params=PARAMS,
        name="quarters",
    )(keep, got)


def join_kernel(*refs, count):
    pieces, out_ref = refs[:count], refs[-1]
    place = lax.axis_index("col")
    rows = pieces[0].shape[0]
    for m, piece in enumerate(pieces):
        out_ref[pl.ds(pl.multiple_of((place ^ m) * rows, 8), rows), :] = piece[...]


def join(pieces, waits):
    return pl.pallas_call(
        functools.partial(join_kernel, count=len(pieces)),
        out_shape=jax.ShapeDtypeStruct((len(pieces) * pieces[0].shape[0], BLOCK), jnp.float32),
        in_specs=[VMEM] * len(pieces) + [ANY] * len(waits),
        out_specs=VMEM,
        compiler_params=PARAMS,
        name="join",
    )(*pieces, *waits)


def swap(value, axis, step):
    count = lax.axis_size(axis)
    return lax.ppermute(value, axis, [(i, i ^ step) for i in range(count)])


def tree_sum(values):
    while len(values) > 1:
        values = [values[i] + values[i + 1] for i in range(0, len(values), 2)]
    return values[0]


def row_of(tile, i):
    return jnp.broadcast_to(tile[i : i + 1, :], tile.shape)


def column_of(tile, j):
    return jnp.broadcast_to(tile[:, j : j + 1], (tile.shape[0], BLOCK))


def factor_block(block):
    groups = BLOCK // 8
    sub = lax.broadcasted_iota(jnp.int32, (8, BLOCK), 0)
    lane = lax.broadcasted_iota(jnp.int32, (8, BLOCK), 1)
    left = [block[8 * t : 8 * t + 8, :] for t in range(groups)]
    right = [(lane == sub + 8 * t).astype(jnp.float32) for t in range(groups)]
    upper = []
    inverse = []
    for g in range(groups):
        a, b = left[g], right[g]
        near = [column_of(a, 8 * g + m) for m in range(8)]
        out_a, out_b = a, b
        for i in range(8):
            pivot = row_of(near[i], i)
            recip = 1.0 / pivot
            root = lax.rsqrt(pivot)
            factor = jnp.where(sub == i, 1.0 - recip, near[i] * recip)
            row_a, row_b = row_of(a, i), row_of(b, i)
            out_a = jnp.where(sub == i, row_a * root, out_a)
            out_b = jnp.where(sub == i, row_b * root, out_b)
            for m in range(i + 1, 8):
                near[m] = near[m] - factor * row_of(near[m], i)
            a = a - factor * row_a
            b = b - factor * row_b
        upper.append(jnp.where(lane >= sub + 8 * g, out_a, 0.0))
        inverse.append(out_b)
        if g + 1 < groups:
            rows_a = [row_of(a, i) for i in range(8)]
            rows_b = [row_of(b, i) for i in range(8)]
            for t in range(g + 1, groups):
                weights = [column_of(left[t], 8 * g + i) for i in range(8)]
                sum_a = weights[0] * rows_a[0]
                sum_b = weights[0] * rows_b[0]
                for i in range(1, 8):
                    sum_a = sum_a + weights[i] * rows_a[i]
                    sum_b = sum_b + weights[i] * rows_b[i]
                left[t] = left[t] - sum_a
                right[t] = right[t] - sum_b
    return jnp.concatenate(upper, 0), jnp.concatenate(inverse, 0)


def eliminate(panels, first, last, upper_ref, inverse_ref):
    count = len(panels)
    for i in range(first, last):
        here = slice((i - first) * BLOCK, (i - first + 1) * BLOCK)
        own, inverse = factor_block(panels[i][:, :BLOCK])
        if i > 0:
            upper_ref[here, : i * BLOCK] = jnp.zeros((BLOCK, i * BLOCK), jnp.float32)
        upper_ref[here, i * BLOCK : (i + 1) * BLOCK] = own
        inverse_ref[i - first] = inverse
        if i + 1 < count:
            rest = exact(inverse, panels[i][:, BLOCK:])
            upper_ref[here, (i + 1) * BLOCK :] = rest
            for j in range(i + 1, count):
                at = (j - i - 1) * BLOCK
                panels[j] = panels[j] - exact_tn(rest[:, at : at + BLOCK], rest[:, at:])


def early_kernel(mine_ref, other_ref, barrier_ref, upper_ref, inverse_ref, rest_ref):
    width = barrier_ref.shape[1]
    count = width // BLOCK
    core = lax.rem(lax.axis_index("scen"), 2)
    diagonal = lax.broadcasted_iota(jnp.int32, (BLOCK, BLOCK), 0) == lax.broadcasted_iota(
        jnp.int32, (BLOCK, BLOCK), 1
    )
    blocks = {}
    names = upper_blocks(width)
    half = len(names) // 2
    for n, (i, j) in enumerate(names):
        at = slice(n % half * BLOCK, (n % half + 1) * BLOCK)
        blocks[i, j] = jnp.where(core == n // half, mine_ref[at, :], other_ref[at, :])
        if i == j:
            extra = barrier_ref[:, i * BLOCK : (i + 1) * BLOCK]
            blocks[i, j] = blocks[i, j] + jnp.where(diagonal, extra, 0.0)
    panels = [jnp.concatenate([blocks[i, j] for j in range(i, count)], 1) for i in range(count)]
    done = inverse_ref.shape[0]
    eliminate(panels, 0, done, upper_ref, inverse_ref)
    for i in range(done, count):
        rest_ref[(i - done) * BLOCK : (i - done + 1) * BLOCK, (i - done) * BLOCK :] = panels[i]


def early_cholesky(mine, other, barrier, done):
    width = barrier.shape[0]
    rows = done * BLOCK
    return pl.pallas_call(
        early_kernel,
        out_shape=[
            jax.ShapeDtypeStruct((rows, width), jnp.float32),
            jax.ShapeDtypeStruct((done, BLOCK, BLOCK), jnp.float32),
            jax.ShapeDtypeStruct((width - rows, width - rows), jnp.float32),
        ],
        in_specs=[VMEM] * 3,
        out_specs=[VMEM] * 3,
        compiler_params=PARAMS,
        cost_estimate=long_cost(20),
        name="early",
    )(mine, other, barrier[None])


def late_kernel(*refs):
    early_ref, rest_ref = refs[:2]
    upper_ref, inverse_ref, slice_ref, turned_ref = refs[-4:]
    rows, width = early_ref.shape
    count = width // BLOCK
    done = rows // BLOCK
    place = lax.axis_index("col")
    panels = [None] * done + [
        rest_ref[i * BLOCK : (i + 1) * BLOCK, i * BLOCK :] for i in range(count - done)
    ]
    eliminate(panels, done, count, upper_ref, inverse_ref)
    slice_rows = slice_ref.shape[0]
    start = place * slice_rows
    block = pl.ds(pl.multiple_of(start // BLOCK * BLOCK, BLOCK), BLOCK)
    turned_ref[:, :rows] = early_ref[:, block].T
    turned_ref[:, rows:] = upper_ref[:, block].T
    slice_ref[...] = turned_ref[pl.ds(pl.multiple_of(lax.rem(start, BLOCK), 8), slice_rows), :]


def late_cholesky(early, rest, col_count, waits):
    width = early.shape[1]
    rest_rows = width - early.shape[0]
    return pl.pallas_call(
        late_kernel,
        out_shape=[
            jax.ShapeDtypeStruct((rest_rows, width), jnp.float32),
            jax.ShapeDtypeStruct((rest_rows // BLOCK, BLOCK, BLOCK), jnp.float32),
            jax.ShapeDtypeStruct((width // col_count, width), jnp.float32),
        ],
        in_specs=[VMEM, VMEM] + [ANY] * len(waits),
        out_specs=[VMEM] * 3,
        scratch_shapes=[pltpu.VMEM((BLOCK, width), jnp.float32)],
        compiler_params=PARAMS,
        cost_estimate=long_cost(20),
        name="late",
    )(early, rest, *waits)


def coupling_kernel(moved_ref, *refs, parts):
    count = (len(refs) - parts - 1) // 2
    refs[parts + count][...] = tree_sum([ref[...] for ref in refs[:parts]])
    moved = moved_ref[...]
    for border_ref, out_ref in zip(refs[parts:], refs[parts + count + 1 :]):
        out_ref[...] = matmul_nt(border_ref[...], moved)


def sum_and_couplings(parts, moved, borders):
    shape = jax.ShapeDtypeStruct((borders[0].shape[0], moved.shape[0]), jnp.float32)
    total, *partial = pl.pallas_call(
        functools.partial(coupling_kernel, parts=len(parts)),
        out_shape=[jax.ShapeDtypeStruct(parts[0].shape, jnp.float32)] + [shape] * len(borders),
        in_specs=[VMEM] * (len(parts) + len(borders) + 1),
        out_specs=[VMEM] * (len(borders) + 1),
        compiler_params=PARAMS,
        name="couplings",
    )(moved, *parts, *borders)
    return total, partial


def assemble_kernel(columns_ref, rows_ref, *refs, parts):
    refs[-2][...] = tree_sum([ref[...] for ref in refs[:parts]])
    pieces, out_ref = refs[parts:-2], refs[-1]
    place = lax.axis_index("col")
    size = pieces[0].shape[0]
    count = len(pieces)
    for m, piece in enumerate(pieces):
        out_ref[pl.ds(pl.multiple_of((place ^ m) * size, 8), size), :] = piece[...]
    at = count * size
    out_ref[at:, :] = jnp.zeros((out_ref.shape[0] - at, out_ref.shape[1]), jnp.float32)
    out_ref[at : at + count, :] = columns_ref[...].astype(jnp.float32)
    out_ref[at + count : at + 2 * count, :size] = rows_ref[0].astype(jnp.float32)


def sum_and_assemble(parts, pieces, columns, rows):
    size, wide = pieces[0].shape
    count = len(pieces)
    return pl.pallas_call(
        functools.partial(assemble_kernel, parts=len(parts)),
        out_shape=[
            jax.ShapeDtypeStruct(parts[0].shape, jnp.float32),
            jax.ShapeDtypeStruct((count * size + -(-count // 4) * 8, wide), jnp.float32),
        ],
        in_specs=[VMEM] * (len(parts) + count + 2),
        out_specs=[VMEM] * 2,
        compiler_params=PARAMS,
        name="assemble",
    )(columns, rows, *parts, *pieces)


def build_kernel(*refs, group):
    groups = refs[1:-2]
    keep_ref, send_ref = refs[-2:]
    rows_here, width = keep_ref.shape
    place = lax.axis_index("scen")
    core = lax.rem(place, 2)
    first = (place - core) * rows_here
    size = (groups[0].shape[0] - 2 * group) // group
    wide = groups[0].shape[1]
    total = jnp.zeros((2 * rows_here, width), jnp.float32)
    slot = lax.broadcasted_iota(jnp.int32, (2 * rows_here, group * size), 0)
    for group_ref in groups:
        index = group_ref[group * size :, :]
        spreads = []
        for i in range(group):
            columns = index[i : i + 1, :].astype(jnp.int32)
            spread = lax.broadcasted_iota(jnp.int32, (width, wide), 0) == columns
            high, low = split_two(group_ref[i * size : (i + 1) * size, :])
            both = matmul_nt(jnp.concatenate([high, low], 0), spread.astype(jnp.bfloat16))
            spreads.append(both[:size] + both[size:])
        row_index = jnp.concatenate(
            [index[group + i : group + i + 1, :size] for i in range(group)], 1
        )
        row_map = (slot == row_index.astype(jnp.int32) - first).astype(jnp.bfloat16)
        high, low = split_two(jnp.concatenate(spreads, 0))
        total = total + (matmul(row_map, high) + matmul(row_map, low))
    lower, upper = total[:rows_here], total[rows_here:]
    keep_ref[...] = jnp.where(core == 0, lower, upper)
    send_ref[...] = jnp.where(core == 0, upper, lower)


def build_rows(groups, group, rows_here, width, wait):
    half = jax.ShapeDtypeStruct((rows_here, width), jnp.float32)
    return pl.pallas_call(
        functools.partial(build_kernel, group=group),
        out_shape=[half, half],
        in_specs=[ANY] + [VMEM] * len(groups),
        out_specs=[VMEM, VMEM],
        compiler_params=PARAMS,
        cost_estimate=long_cost(5),
        name="build",
    )(wait, *groups)


def solve_kernel(keep_ref, got_ref, early_ref, late_ref, first_ref, last_ref, out_ref):
    count = out_ref.shape[1] // BLOCK
    done = first_ref.shape[0]
    here = [slice(k * BLOCK, (k + 1) * BLOCK) for k in range(count)]
    left = [keep_ref[:, h] + got_ref[:, h] for h in here]
    for k in range(count):
        upper_ref, inverse_ref, at = (
            (early_ref, first_ref, k) if k < done else (late_ref, last_ref, k - done)
        )
        solved = exact_nt(left[k], inverse_ref[at])
        out_ref[:, here[k]] = solved
        for j in range(k + 1, count):
            left[j] = left[j] - exact(solved, upper_ref[here[at], here[j]])


def solve_rows(keep, got, uppers, inverses):
    return pl.pallas_call(
        solve_kernel,
        out_shape=jax.ShapeDtypeStruct(keep.shape, jnp.float32),
        in_specs=[VMEM] * 6,
        out_specs=VMEM,
        compiler_params=PARAMS,
        name="solve",
    )(keep, got, *uppers, *inverses)


def dense_panel(couplings_here, rows, columns, rows_panel, width):
    def step(running, operands):
        coupling, row_index, column_index = operands
        column_map = (column_index[:, None] == jnp.arange(width)[None, :]).astype(jnp.float32)
        row_map = (row_index[:, None] == jnp.arange(rows_panel)[None, :]).astype(jnp.float32)
        widened = jnp.dot(coupling, column_map, precision=HIGHEST)
        return running + jnp.einsum("br,bd->rd", row_map, widened, precision=HIGHEST), None

    zero = jnp.zeros((rows_panel, width), jnp.float32)
    total, _ = lax.scan(step, zero, (couplings_here, rows, columns))
    return lax.psum_scatter(total, "scen", scatter_dimension=0, tiled=True)


def dense_solve(rows, upper, inverse):
    width = rows.shape[1]
    solved = []
    for k in range(width // BLOCK):
        here = slice(k * BLOCK, (k + 1) * BLOCK)
        left = rows[:, here]
        if k > 0:
            left = left - jnp.dot(
                jnp.concatenate(solved, 1), upper[: k * BLOCK, here], precision=HIGHEST
            )
        solved.append(jnp.dot(left, inverse[k].T, precision=HIGHEST))
    return jnp.concatenate(solved, 1)


def shards(
    rows_here,
    inverse_factor,
    true_orders,
    slab_border,
    slab_columns,
    panel_border,
    panel_rows,
    barrier_diag,
):
    scen_count = lax.axis_size("scen")
    col_count = lax.axis_size("col")
    width = barrier_diag.shape[0]
    group, size = panel_border.shape[1:3]
    wide = slab_columns.shape[1]

    moved, keep, send = front(true_orders, slab_columns, inverse_factor, slab_border, width)
    got = swap(send, "scen", 1)
    parts = quarters(keep, got, col_count)
    dealt = deal(panel_border)
    borders = [dealt[0]] + [swap(dealt[m], "col", m) for m in range(1, col_count)]
    parts = [parts[0]] + [swap(parts[m], "col", m) for m in range(1, col_count)]
    part, partial = sum_and_couplings(parts, moved, borders)
    parts = [part] + [swap(part, "scen", 2 * m) for m in range(1, scen_count // 2)]
    pieces = [partial[0]] + [swap(partial[m], "col", m) for m in range(1, col_count)]
    part, own = sum_and_assemble(parts, pieces, slab_columns, panel_rows)
    rows_panel = rows_here * scen_count
    sparse = scen_count * group * size * wide < rows_panel * width
    groups = [own]
    if sparse:
        groups += [swap(own, "scen", 2 * m) for m in range(1, scen_count // 2)]
    mine = join([part] + [swap(part, "col", m) for m in range(1, col_count)], groups[1:2])
    done = (width // BLOCK * 3) // 4
    early, early_inverse, rest = early_cholesky(mine, swap(mine, "scen", 1), barrier_diag, done)
    if sparse:
        rows, other = build_rows(groups, group, rows_here, width, rest)
        late, late_inverse, factor_rows = late_cholesky(early, rest, col_count, [other])
        solved = solve_rows(
            rows, swap(other, "scen", 1), (early, late), (early_inverse, late_inverse)
        )
    else:
        local = own[: group * size].reshape(group, size, wide)
        rows = dense_panel(local, panel_rows[0], slab_columns, rows_panel, width)
        late, late_inverse, factor_rows = late_cholesky(early, rest, col_count, [])
        solved = dense_solve(
            rows,
            jnp.concatenate([early, late], 0),
            jnp.concatenate([early_inverse, late_inverse], 0),
        )
    return factor_rows, solved


def solution(mesh):
    in_specs = (
        P(("scen", "col"), None, None),
        P(("scen", "col")),
        P(("scen", "col"), None, None),
        P("scen", None),
        P("col", "scen", None, None),
        P("col", "scen", None),
        P(),
    )
    out_specs = (P("col", None), P(("scen", "col"), None))

    def whole(*args):
        devices = mesh.shape["scen"] * mesh.shape["col"]
        first_section = NF - args[-1].shape[0]
        body = functools.partial(shards, first_section // devices)
        return jax.shard_map(
            body, mesh=mesh, in_specs=in_specs, out_specs=out_specs, check_vma=False
        )(*args)

    return whole
```

```python
import functools

import jax
import jax.numpy as jnp
from jax import lax
from jax.experimental import pallas as pl
from jax.experimental.pallas import tpu as pltpu
from jax.sharding import PartitionSpec as P

NF = 8192
BLOCK = 128
HIGHEST = lax.Precision.HIGHEST
VMEM = pl.BlockSpec(memory_space=pltpu.VMEM)
SMEM = pl.BlockSpec(memory_space=pltpu.SMEM)
HBM = pl.BlockSpec(memory_space=pltpu.HBM)
ANY = pl.BlockSpec(memory_space=pl.ANY)
PARAMS = pltpu.CompilerParams(vmem_limit_bytes=40 * 2**20)


def long_cost(micros):
    return pl.CostEstimate(flops=micros * 10**9, bytes_accessed=2**10, transcendentals=0)


def in_hbm(value):
    return pltpu.with_memory_space_constraint(value, pltpu.HBM)


def split_two(value):
    high = value.astype(jnp.bfloat16)
    low = (value - high.astype(jnp.float32)).astype(jnp.bfloat16)
    return high, low


def matmul(left, right):
    return jnp.dot(left, right, preferred_element_type=jnp.float32)


def matmul_nt(left, right):
    return lax.dot_general(
        left, right, (((1,), (1,)), ((), ())), preferred_element_type=jnp.float32
    )


def exact_tn(left, right):
    return lax.dot_general(
        left,
        right,
        (((0,), (0,)), ((), ())),
        precision=HIGHEST,
        preferred_element_type=jnp.float32,
    )


def exact(left, right):
    return jnp.dot(left, right, precision=HIGHEST, preferred_element_type=jnp.float32)


def exact_nt(left, right):
    return lax.dot_general(
        left,
        right,
        (((1,), (1,)), ((), ())),
        precision=HIGHEST,
        preferred_element_type=jnp.float32,
    )


def upper_blocks(width):
    count = width // BLOCK
    return [(i, j) for i in range(count) for j in range(i, count)]


def front_kernel(
    order_ref,
    columns_ref,
    factor_ref,
    border_ref,
    moved_ref,
    keep_ref,
    send_ref,
    packed_ref,
    factor_here,
    border_here,
    columns_here,
    sems,
    *,
    width,
):
    chunk = factor_here.shape[0] // 4
    chunks = [slice(k * chunk, (k + 1) * chunk) for k in range(4)]
    loads = [pltpu.make_async_copy(border_ref.at[0], border_here, sems.at[0])]
    for k, at in enumerate(chunks):
        loads.append(
            pltpu.make_async_copy(factor_ref.at[0, at], factor_here.at[at], sems.at[k + 1])
        )
    loads.append(pltpu.make_async_copy(columns_ref, columns_here, sems.at[5]))
    for load in loads:
        load.start()
    core = lax.rem(lax.axis_index("scen"), 2)
    place = lax.axis_index("col")
    order = order_ref[0]
    loads[0].wait()
    border = border_here[...]
    within = lax.broadcasted_iota(jnp.int32, border.shape, 1) < order
    inside = jnp.where(within, border.astype(jnp.float32), 0.0).astype(jnp.bfloat16)
    product = jnp.zeros(border.shape, jnp.float32)
    for k, at in enumerate(chunks):
        loads[k + 1].wait()
        product = product + matmul(inside[:, at], factor_here[at])
    moved = jnp.where(within, product, 0.0).astype(jnp.bfloat16)
    moved_ref[...] = moved
    loads[5].wait()
    columns = columns_here[pl.ds(place, 1), :]
    spread = (
        lax.broadcasted_iota(jnp.int32, (width, columns.shape[1]), 0) == columns
    ).astype(jnp.bfloat16)
    terms = 0.5 * (matmul_nt(border, moved) + matmul_nt(moved, border))
    high, low = split_two(terms)
    half_spread = matmul_nt(high, spread) + matmul_nt(low, spread)
    high, low = split_two(half_spread)
    row = 0
    for i in range(width // BLOCK):
        rows = spread[i * BLOCK : (i + 1) * BLOCK]
        part = matmul(rows, high[:, i * BLOCK :]) + matmul(rows, low[:, i * BLOCK :])
        for j in range(i, width // BLOCK):
            packed_ref[row : row + BLOCK, :] = part[:, (j - i) * BLOCK : (j - i + 1) * BLOCK]
            row += BLOCK
    half = keep_ref.shape[0]
    keep_ref[...] = packed_ref[pl.ds(pl.multiple_of(core * half, 8), half), :]
    send_ref[...] = packed_ref[pl.ds(pl.multiple_of((1 - core) * half, 8), half), :]


def front(order, columns, factor, border, width):
    total = len(upper_blocks(width)) * BLOCK
    half = jax.ShapeDtypeStruct((total // 2, BLOCK), jnp.float32)
    return pl.pallas_call(
        functools.partial(front_kernel, width=width),
        out_shape=[jax.ShapeDtypeStruct(border.shape[1:], jnp.bfloat16), half, half],
        in_specs=[SMEM, HBM, HBM, HBM],
        out_specs=[VMEM] * 3,
        scratch_shapes=[
            pltpu.VMEM((total, BLOCK), jnp.float32),
            pltpu.VMEM(factor.shape[1:], factor.dtype),
            pltpu.VMEM(border.shape[1:], border.dtype),
            pltpu.VMEM(columns.shape, columns.dtype),
            pltpu.SemaphoreType.DMA((6,)),
        ],
        compiler_params=PARAMS,
        cost_estimate=long_cost(20),
        name="front",
    )(order, in_hbm(columns), in_hbm(factor), in_hbm(border))


def deal_kernel(border_ref, *refs):
    out_refs, sems = refs[:-1], refs[-1]
    place = lax.axis_index("col")
    loads = [
        pltpu.make_async_copy(border_ref.at[0, place ^ m], out_ref, sems.at[m])
        for m, out_ref in enumerate(out_refs)
    ]
    for load in loads:
        load.start()
    for load in loads:
        load.wait()


def deal(border):
    count = border.shape[1]
    return pl.pallas_call(
        deal_kernel,
        out_shape=[jax.ShapeDtypeStruct(border.shape[2:], border.dtype)] * count,
        in_specs=[HBM],
        out_specs=[VMEM] * count,
        scratch_shapes=[pltpu.SemaphoreType.DMA((count,))],
        compiler_params=PARAMS,
        name="deal",
    )(in_hbm(border))


def quarter_kernel(keep_ref, got_ref, *out_refs):
    place = lax.axis_index("col")
    rows = out_refs[0].shape[0]
    for m, out_ref in enumerate(out_refs):
        at = pl.ds(pl.multiple_of((place ^ m) * rows, 8), rows)
        out_ref[...] = keep_ref[at, :] + got_ref[at, :]


def quarters(keep, got, col_count):
    piece = jax.ShapeDtypeStruct((keep.shape[0] // col_count, BLOCK), jnp.float32)
    return pl.pallas_call(
        quarter_kernel,
        out_shape=[piece] * col_count,
        in_specs=[VMEM, VMEM],
        out_specs=[VMEM] * col_count,
        compiler_params=PARAMS,
        name="quarters",
    )(keep, got)


def join_kernel(*refs, count):
    pieces, first_ref, last_ref, all_ref = refs[:count], refs[-3], refs[-2], refs[-1]
    place = lax.axis_index("col")
    rows = pieces[0].shape[0]
    for m, piece in enumerate(pieces):
        all_ref[pl.ds(pl.multiple_of((place ^ m) * rows, 8), rows), :] = piece[...]
    half = first_ref.shape[0]
    first_ref[...] = all_ref[:half, :]
    last_ref[...] = all_ref[half:, :]


def join(pieces, waits):
    rows = len(pieces) * pieces[0].shape[0]
    half = jax.ShapeDtypeStruct((rows // 2, BLOCK), jnp.float32)
    return pl.pallas_call(
        functools.partial(join_kernel, count=len(pieces)),
        out_shape=[half, half],
        in_specs=[VMEM] * len(pieces) + [ANY] * len(waits),
        out_specs=[VMEM, VMEM],
        scratch_shapes=[pltpu.VMEM((rows, BLOCK), jnp.float32)],
        compiler_params=PARAMS,
        name="join",
    )(*pieces, *waits)


def swap(value, axis, step):
    count = lax.axis_size(axis)
    return lax.ppermute(value, axis, [(i, i ^ step) for i in range(count)])


def tree_sum(values):
    while len(values) > 1:
        values = [values[i] + values[i + 1] for i in range(0, len(values), 2)]
    return values[0]


def row_of(tile, i):
    return jnp.broadcast_to(tile[i : i + 1, :], tile.shape)


def column_of(tile, j):
    index = jnp.full(tile.shape, j, jnp.int32)
    return jnp.take_along_axis(tile, index, axis=1, mode="promise_in_bounds")


def weighted_rows(weights, rows):
    total = weights[0] * rows[0]
    for weight, row in zip(weights[1:], rows[1:]):
        total = total + weight * row
    return total


def factor_block(block):
    groups = BLOCK // 8
    sub = lax.broadcasted_iota(jnp.int32, (8, BLOCK), 0)
    lane = lax.broadcasted_iota(jnp.int32, (8, BLOCK), 1)
    owner = lax.shift_right_logical(lane, 3)
    tiles = [block[8 * t : 8 * t + 8, :] for t in range(groups)]
    upper = []
    lower = []
    ready = None
    for pair in range(groups // 2):
        far = min(groups, 2 * pair + 4)
        swept = []
        for g in (2 * pair, 2 * pair + 1):
            more = g + 1 < groups
            tile = tiles[g]
            near = ready or [column_of(tile, 8 * g + m) for m in range(8)]
            if more:
                near = near + [column_of(tile, 8 * g + 8 + m) for m in range(8)]
            mixed = jnp.where(owner == g, (lane == sub + 8 * g).astype(jnp.float32), tile)
            out_tile, out_mixed = tile, mixed
            pivot = row_of(near[0], 0)
            for i in range(8):
                root = lax.rsqrt(pivot)
                recip = root * root
                rows = {m: row_of(near[m], i) for m in range(i + 1, len(near))}
                if i < 7:
                    pivot = row_of(near[i + 1], i + 1) - row_of(near[i], i + 1) * rows[i + 1] * recip
                factor = jnp.where(sub == i, 1.0 - recip, near[i] * recip)
                for m in rows:
                    near[m] = near[m] - factor * rows[m]
                row_tile, row_mixed = row_of(tile, i), row_of(mixed, i)
                out_tile = jnp.where(sub == i, row_tile * root, out_tile)
                out_mixed = jnp.where(sub == i, row_mixed * root, out_mixed)
                tile = tile - factor * row_tile
                mixed = mixed - factor * row_mixed
            inner = jnp.where((owner == g) & (lane >= sub + 8 * g), out_tile, 0.0)
            upper.append(jnp.where(owner > g, out_mixed, inner))
            lower.append(jnp.where(owner <= g, out_mixed, 0.0))
            rows = [row_of(mixed, i) for i in range(8)]
            swept.append((mixed, rows))
            if not more:
                break
            following = tiles[g + 1]
            weights = [column_of(following, 8 * g + i) for i in range(8)]
            ready = [
                column_of(following, 8 * g + 8 + m)
                - weighted_rows(weights, [row_of(near[8 + m], i) for i in range(8)])
                for m in range(8)
            ]
            for t in range(g + 1, far):
                if t > g + 1:
                    weights = [column_of(tiles[t], 8 * g + i) for i in range(8)]
                tiles[t] = jnp.where(owner == g, 0.0, tiles[t]) - weighted_rows(weights, rows)
        if far < groups:
            g = 2 * pair
            first, second = swept[0][0], swept[1][0]
            weights = [column_of(first, 8 * g + 8 + i) for i in range(8)]
            first = jnp.where(owner == g + 1, 0.0, first) - weighted_rows(weights, swept[1][1])
            parts = [first, second, jnp.zeros((BLOCK - 8 * g - 16, BLOCK), jnp.float32)]
            if g > 0:
                parts = [jnp.zeros((8 * g, BLOCK), jnp.float32)] + parts
            update = exact(jnp.concatenate(tiles[far:], 0), jnp.concatenate(parts, 0))
            for t in range(far, groups):
                kept = jnp.where((owner == g) | (owner == g + 1), 0.0, tiles[t])
                tiles[t] = kept - update[8 * (t - far) : 8 * (t - far) + 8]
    return jnp.concatenate(upper, 0), jnp.concatenate(lower, 0)


def cholesky_kernel(
    mine_first, mine_last, other_first, other_last, barrier_ref, inverse_ref, slice_ref, upper_ref,
    turned_ref, packed_ref
):
    width = barrier_ref.shape[1]
    count = width // BLOCK
    core = lax.rem(lax.axis_index("scen"), 2)
    place = lax.axis_index("col")
    diagonal = lax.broadcasted_iota(jnp.int32, (BLOCK, BLOCK), 0) == lax.broadcasted_iota(
        jnp.int32, (BLOCK, BLOCK), 1
    )
    blocks = {}
    rows = mine_first.shape[0]
    for n, ref in enumerate((mine_first, mine_last, other_first, other_last)):
        owner = core if n < 2 else 1 - core
        at = (2 * owner + n % 2) * rows
        packed_ref[pl.ds(pl.multiple_of(at, 8), rows), :] = ref[...]
    for n, (i, j) in enumerate(upper_blocks(width)):
        blocks[i, j] = packed_ref[n * BLOCK : (n + 1) * BLOCK, :]
        if i == j:
            extra = barrier_ref[:, i * BLOCK : (i + 1) * BLOCK]
            blocks[i, j] = blocks[i, j] + jnp.where(diagonal, extra, 0.0)
    panels = [jnp.concatenate([blocks[i, j] for j in range(i, count)], 1) for i in range(count)]
    upper_ref[...] = jnp.zeros(upper_ref.shape, jnp.float32)
    inverse_ref[...] = jnp.zeros(inverse_ref.shape, jnp.float32)
    for i in range(count):
        here = slice(i * BLOCK, (i + 1) * BLOCK)
        before = slice(0, i * BLOCK)
        own, inverse = factor_block(panels[i][:, :BLOCK])
        upper_ref[here, here] = own
        inverse_ref[here, here] = inverse
        if i + 1 < count:
            rest = exact(inverse, panels[i][:, BLOCK:])
            upper_ref[here, (i + 1) * BLOCK :] = rest
            for j in range(i + 1, count):
                at = (j - i - 1) * BLOCK
                panels[j] = panels[j] - exact_tn(rest[:, at : at + BLOCK], rest[:, at:])
        if i > 0:
            mixed = exact_tn(upper_ref[before, here], inverse_ref[before, before])
            inverse_ref[here, before] = -exact(inverse, mixed)
    slice_rows = slice_ref.shape[0]
    start = place * slice_rows
    block = pl.ds(pl.multiple_of(start // BLOCK * BLOCK, BLOCK), BLOCK)
    turned_ref[...] = upper_ref[:, block].T
    slice_ref[...] = turned_ref[pl.ds(pl.multiple_of(lax.rem(start, BLOCK), 8), slice_rows), :]


def cholesky(halves, barrier, col_count):
    width = barrier.shape[0]
    return pl.pallas_call(
        cholesky_kernel,
        out_shape=[
            jax.ShapeDtypeStruct((width, width), jnp.float32),
            jax.ShapeDtypeStruct((width // col_count, width), jnp.float32),
        ],
        in_specs=[VMEM] * 5,
        out_specs=[VMEM] * 2,
        scratch_shapes=[
            pltpu.VMEM((width, width), jnp.float32),
            pltpu.VMEM((BLOCK, width), jnp.float32),
            pltpu.VMEM((4 * halves[0].shape[0], BLOCK), jnp.float32),
        ],
        compiler_params=PARAMS,
        cost_estimate=long_cost(0),
        name="cholesky",
    )(*halves, barrier[None])


def coupling_kernel(moved_ref, *refs, parts):
    count = (len(refs) - parts - 1) // 2
    refs[parts + count][...] = tree_sum([ref[...] for ref in refs[:parts]])
    moved = moved_ref[...]
    for border_ref, out_ref in zip(refs[parts:], refs[parts + count + 1 :]):
        out_ref[...] = matmul_nt(border_ref[...], moved)


def sum_and_couplings(parts, moved, borders):
    shape = jax.ShapeDtypeStruct((borders[0].shape[0], moved.shape[0]), jnp.float32)
    total, *partial = pl.pallas_call(
        functools.partial(coupling_kernel, parts=len(parts)),
        out_shape=[jax.ShapeDtypeStruct(parts[0].shape, jnp.float32)] + [shape] * len(borders),
        in_specs=[VMEM] * (len(parts) + len(borders) + 1),
        out_specs=[VMEM] * (len(borders) + 1),
        compiler_params=PARAMS,
        name="couplings",
    )(moved, *parts, *borders)
    return total, partial


def assemble_kernel(columns_ref, rows_ref, *refs, parts):
    refs[-2][...] = tree_sum([ref[...] for ref in refs[:parts]])
    pieces, out_ref = refs[parts:-2], refs[-1]
    place = lax.axis_index("col")
    size = pieces[0].shape[0]
    count = len(pieces)
    for m, piece in enumerate(pieces):
        out_ref[pl.ds(pl.multiple_of((place ^ m) * size, 8), size), :] = piece[...]
    at = count * size
    out_ref[at:, :] = jnp.zeros((out_ref.shape[0] - at, out_ref.shape[1]), jnp.float32)
    out_ref[at : at + count, :] = columns_ref[...].astype(jnp.float32)
    out_ref[at + count : at + 2 * count, :size] = rows_ref[0].astype(jnp.float32)


def sum_and_assemble(parts, pieces, columns, rows):
    size, wide = pieces[0].shape
    count = len(pieces)
    return pl.pallas_call(
        functools.partial(assemble_kernel, parts=len(parts)),
        out_shape=[
            jax.ShapeDtypeStruct(parts[0].shape, jnp.float32),
            jax.ShapeDtypeStruct((count * size + -(-count // 4) * 8, wide), jnp.float32),
        ],
        in_specs=[VMEM] * (len(parts) + count + 2),
        out_specs=[VMEM] * 2,
        compiler_params=PARAMS,
        name="assemble",
    )(columns, rows, *parts, *pieces)


def placed_rows(groups, group, rows_here, width):
    place = lax.axis_index("scen")
    first = (place - lax.rem(place, 2)) * rows_here
    size = (groups[0].shape[0] - 2 * group) // group
    wide = groups[0].shape[1]
    total = None
    slot = lax.broadcasted_iota(jnp.int32, (2 * rows_here, group * size), 0)
    for group_ref in groups:
        index = group_ref[group * size :, :]
        spreads = []
        for i in range(group):
            columns = index[i : i + 1, :].astype(jnp.int32)
            spread = lax.broadcasted_iota(jnp.int32, (width, wide), 0) == columns
            high, low = split_two(group_ref[i * size : (i + 1) * size, :])
            both = matmul_nt(jnp.concatenate([high, low], 0), spread.astype(jnp.bfloat16))
            spreads.append(both[:size] + both[size:])
        row_index = jnp.concatenate(
            [index[group + i : group + i + 1, :size] for i in range(group)], 1
        )
        row_map = (slot == row_index.astype(jnp.int32) - first).astype(jnp.bfloat16)
        high, low = split_two(jnp.concatenate(spreads, 0))
        part = matmul(row_map, high) + matmul(row_map, low)
        total = part if total is None else total + part
    return total


def near_kernel(*refs, group):
    groups, out_ref = refs[1:-1], refs[-1]
    rows, width = out_ref.shape
    out_ref[...] = placed_rows(groups, group, rows // 2, width)


def near_rows(groups, group, rows_here, width, wait):
    return pl.pallas_call(
        functools.partial(near_kernel, group=group),
        out_shape=jax.ShapeDtypeStruct((2 * rows_here, width), jnp.float32),
        in_specs=[ANY] + [VMEM] * len(groups),
        out_specs=VMEM,
        compiler_params=PARAMS,
        cost_estimate=long_cost(0),
        name="near",
    )(wait, *groups)


def far_kernel(near_ref, *refs, group):
    groups = refs[:-2]
    keep_ref, send_ref = refs[-2:]
    rows_here, width = keep_ref.shape
    core = lax.rem(lax.axis_index("scen"), 2)
    total = near_ref[...] + placed_rows(groups, group, rows_here, width)
    lower, upper = total[:rows_here], total[rows_here:]
    keep_ref[...] = jnp.where(core == 0, lower, upper)
    send_ref[...] = jnp.where(core == 0, upper, lower)


def far_rows(near, groups, group):
    rows, width = near.shape
    half = jax.ShapeDtypeStruct((rows // 2, width), jnp.float32)
    return pl.pallas_call(
        functools.partial(far_kernel, group=group),
        out_shape=[half, half],
        in_specs=[VMEM] * (1 + len(groups)),
        out_specs=[VMEM, VMEM],
        compiler_params=PARAMS,
        cost_estimate=long_cost(0),
        name="far",
    )(near, *groups)


def solve_kernel(keep_ref, got_ref, inverse_ref, out_ref):
    out_ref[...] = exact_nt(keep_ref[...] + got_ref[...], inverse_ref[...])


def solve_rows(keep, got, inverse):
    return pl.pallas_call(
        solve_kernel,
        out_shape=jax.ShapeDtypeStruct(keep.shape, jnp.float32),
        in_specs=[VMEM] * 3,
        out_specs=VMEM,
        compiler_params=PARAMS,
        name="solve",
    )(keep, got, inverse)


def dense_panel(couplings_here, rows, columns, rows_panel, width):
    def step(running, operands):
        coupling, row_index, column_index = operands
        column_map = (column_index[:, None] == jnp.arange(width)[None, :]).astype(jnp.float32)
        row_map = (row_index[:, None] == jnp.arange(rows_panel)[None, :]).astype(jnp.float32)
        widened = jnp.dot(coupling, column_map, precision=HIGHEST)
        return running + jnp.einsum("br,bd->rd", row_map, widened, precision=HIGHEST), None

    zero = jnp.zeros((rows_panel, width), jnp.float32)
    total, _ = lax.scan(step, zero, (couplings_here, rows, columns))
    return lax.psum_scatter(total, "scen", scatter_dimension=0, tiled=True)


def shards(
    rows_here,
    inverse_factor,
    true_orders,
    slab_border,
    slab_columns,
    panel_border,
    panel_rows,
    barrier_diag,
):
    scen_count = lax.axis_size("scen")
    col_count = lax.axis_size("col")
    width = barrier_diag.shape[0]
    group, size = panel_border.shape[1:3]
    wide = slab_columns.shape[1]

    moved, keep, send = front(true_orders, slab_columns, inverse_factor, slab_border, width)
    got = swap(send, "scen", 1)
    parts = quarters(keep, got, col_count)
    dealt = deal(panel_border)
    borders = [dealt[0]] + [swap(dealt[m], "col", m) for m in range(1, col_count)]
    parts = [parts[0]] + [swap(parts[m], "col", m) for m in range(1, col_count)]
    part, partial = sum_and_couplings(parts, moved, borders)
    parts = [part] + [swap(part, "scen", 2 * m) for m in range(1, scen_count // 2)]
    pieces = [partial[0]] + [swap(partial[m], "col", m) for m in range(1, col_count)]
    part, own = sum_and_assemble(parts, pieces, slab_columns, panel_rows)
    rows_panel = rows_here * scen_count
    sparse = scen_count * group * size * wide < rows_panel * width
    groups = [own]
    if sparse:
        groups += [swap(own, "scen", 2 * m) for m in range(1, scen_count // 2)]
    mine = join([part] + [swap(part, "col", m) for m in range(1, col_count)], [])
    halves = list(mine) + [swap(half, "scen", 1) for half in mine]
    inverse, factor_rows = cholesky(halves, barrier_diag, col_count)
    if sparse:
        half = len(groups) // 2
        near = near_rows(groups[:half], group, rows_here, width, inverse)
        rows, other = far_rows(near, groups[half:], group)
        solved = solve_rows(rows, swap(other, "scen", 1), inverse)
    else:
        local = own[: group * size].reshape(group, size, wide)
        rows = dense_panel(local, panel_rows[0], slab_columns, rows_panel, width)
        solved = jnp.dot(rows, inverse.T, precision=HIGHEST)
    return factor_rows, solved


def solution(mesh):
    in_specs = (
        P(("scen", "col"), None, None),
        P(("scen", "col")),
        P(("scen", "col"), None, None),
        P("scen", None),
        P("col", "scen", None, None),
        P("col", "scen", None),
        P(),
    )
    out_specs = (P("col", None), P(("scen", "col"), None))

    def whole(*args):
        devices = mesh.shape["scen"] * mesh.shape["col"]
        first_section = NF - args[-1].shape[0]
        body = functools.partial(shards, first_section // devices)
        return jax.shard_map(
            body, mesh=mesh, in_specs=in_specs, out_specs=out_specs, check_vma=False
        )(*args)

    return whole
```

```python
import functools

import jax
import jax.numpy as jnp
from jax import lax
from jax.experimental import pallas as pl
from jax.experimental.pallas import tpu as pltpu
from jax.sharding import PartitionSpec as P

NF = 8192
BLOCK = 128
HIGHEST = lax.Precision.HIGHEST
VMEM = pl.BlockSpec(memory_space=pltpu.VMEM)
SMEM = pl.BlockSpec(memory_space=pltpu.SMEM)
HBM = pl.BlockSpec(memory_space=pltpu.HBM)
ANY = pl.BlockSpec(memory_space=pl.ANY)
PARAMS = pltpu.CompilerParams(vmem_limit_bytes=40 * 2**20)


def long_cost(micros):
    return pl.CostEstimate(flops=micros * 10**9, bytes_accessed=2**10, transcendentals=0)


def in_hbm(value):
    return pltpu.with_memory_space_constraint(value, pltpu.HBM)


def split_two(value):
    high = value.astype(jnp.bfloat16)
    low = (value - high.astype(jnp.float32)).astype(jnp.bfloat16)
    return high, low


def matmul(left, right):
    return jnp.dot(left, right, preferred_element_type=jnp.float32)


def matmul_nt(left, right):
    return lax.dot_general(
        left, right, (((1,), (1,)), ((), ())), preferred_element_type=jnp.float32
    )


def exact_tn(left, right):
    return lax.dot_general(
        left,
        right,
        (((0,), (0,)), ((), ())),
        precision=HIGHEST,
        preferred_element_type=jnp.float32,
    )


def exact(left, right):
    return jnp.dot(left, right, precision=HIGHEST, preferred_element_type=jnp.float32)


def exact_nt(left, right):
    return lax.dot_general(
        left,
        right,
        (((1,), (1,)), ((), ())),
        precision=HIGHEST,
        preferred_element_type=jnp.float32,
    )


def packed_rows(width, unit):
    count = width // BLOCK
    rows = (count * (count - 1) // 2 + count // 2) * BLOCK + count // 2
    return -(-rows // unit) * unit


def upper_blocks(width):
    count = width // BLOCK
    return [(i, j) for i in range(count) for j in range(i + 1, count)]


def row_and_lane():
    shape = (BLOCK, BLOCK)
    return lax.broadcasted_iota(jnp.int32, shape, 0), lax.broadcasted_iota(jnp.int32, shape, 1)


def pack(blocks, width, packed_ref):
    row, lane = row_and_lane()
    first = 0
    for name in upper_blocks(width):
        packed_ref[first : first + BLOCK, :] = blocks[name]
        first += BLOCK
    diagonals = []
    for i in range(0, width // BLOCK, 2):
        one, two = blocks[i, i], blocks[i + 1, i + 1]
        packed_ref[first : first + BLOCK, :] = jnp.where(row <= lane, one, two)
        first += BLOCK
        diagonals.append(jnp.sum(jnp.where(row == lane, two, 0.0), 0, keepdims=True))
    spare = packed_ref.shape[0] - first - len(diagonals)
    diagonals.append(jnp.zeros((spare, BLOCK), jnp.float32))
    packed_ref[first:, :] = jnp.concatenate(diagonals, 0)


def unpack(packed_ref, width):
    row, lane = row_and_lane()
    blocks = {}
    first = 0
    for name in upper_blocks(width):
        blocks[name] = packed_ref[first : first + BLOCK, :]
        first += BLOCK
    last = first + width // BLOCK // 2 * BLOCK
    for n in range(width // BLOCK // 2):
        square = packed_ref[first + n * BLOCK : first + (n + 1) * BLOCK, :]
        turned = square.T
        blocks[2 * n, 2 * n] = jnp.where(row <= lane, square, turned)
        diagonal = packed_ref[last + n : last + n + 1, :]
        other = jnp.where(row > lane, square, turned)
        blocks[2 * n + 1, 2 * n + 1] = jnp.where(row == lane, diagonal, other)
    return blocks


def front_kernel(
    order_ref,
    columns_ref,
    factor_ref,
    border_ref,
    panel_ref,
    moved_ref,
    keep_ref,
    send_ref,
    *refs,
    width,
):
    dealt = refs[:-6]
    packed_ref, factor_here, border_here, columns_here, sems, deal_sems = refs[-6:]
    place = lax.axis_index("col")
    chunk = factor_here.shape[0] // 4
    chunks = [slice(k * chunk, (k + 1) * chunk) for k in range(4)]
    loads = [pltpu.make_async_copy(border_ref.at[0], border_here, sems.at[0])]
    for k, at in enumerate(chunks):
        loads.append(
            pltpu.make_async_copy(factor_ref.at[0, at], factor_here.at[at], sems.at[k + 1])
        )
    loads.append(pltpu.make_async_copy(columns_ref, columns_here, sems.at[5]))
    for load in loads:
        load.start()
    deals = [
        pltpu.make_async_copy(panel_ref.at[0, place ^ m], out_ref, deal_sems.at[m])
        for m, out_ref in enumerate(dealt)
    ]
    for load in deals:
        load.start()
    core = lax.rem(lax.axis_index("scen"), 2)
    order = order_ref[0]
    loads[0].wait()
    border = border_here[...]
    within = lax.broadcasted_iota(jnp.int32, border.shape, 1) < order
    inside = jnp.where(within, border.astype(jnp.float32), 0.0).astype(jnp.bfloat16)
    product = jnp.zeros(border.shape, jnp.float32)
    for k, at in enumerate(chunks):
        loads[k + 1].wait()
        product = product + matmul(inside[:, at], factor_here[at])
    moved = jnp.where(within, product, 0.0).astype(jnp.bfloat16)
    moved_ref[...] = moved
    loads[5].wait()
    columns = columns_here[pl.ds(place, 1), :]
    spread = (
        lax.broadcasted_iota(jnp.int32, (width, columns.shape[1]), 0) == columns
    ).astype(jnp.bfloat16)
    terms = 0.5 * (matmul_nt(border, moved) + matmul_nt(moved, border))
    high, low = split_two(terms)
    half_spread = matmul_nt(high, spread) + matmul_nt(low, spread)
    high, low = split_two(half_spread)
    blocks = {}
    for i in range(width // BLOCK):
        rows = spread[i * BLOCK : (i + 1) * BLOCK]
        part = matmul(rows, high[:, i * BLOCK :]) + matmul(rows, low[:, i * BLOCK :])
        for j in range(i, width // BLOCK):
            blocks[i, j] = part[:, (j - i) * BLOCK : (j - i + 1) * BLOCK]
    pack(blocks, width, packed_ref)
    half = keep_ref.shape[0]
    keep_ref[...] = packed_ref[pl.ds(pl.multiple_of(core * half, 8), half), :]
    send_ref[...] = packed_ref[pl.ds(pl.multiple_of((1 - core) * half, 8), half), :]
    for load in deals:
        load.wait()


def front(order, columns, factor, border, panel, width):
    count = panel.shape[1]
    total = packed_rows(width, 16 * count)
    half = jax.ShapeDtypeStruct((total // 2, BLOCK), jnp.float32)
    piece = jax.ShapeDtypeStruct(panel.shape[2:], panel.dtype)
    moved, keep, send, *dealt = pl.pallas_call(
        functools.partial(front_kernel, width=width),
        out_shape=[jax.ShapeDtypeStruct(border.shape[1:], jnp.bfloat16), half, half]
        + [piece] * count,
        in_specs=[SMEM, HBM, HBM, HBM, HBM],
        out_specs=[VMEM] * (3 + count),
        scratch_shapes=[
            pltpu.VMEM((total, BLOCK), jnp.float32),
            pltpu.VMEM(factor.shape[1:], factor.dtype),
            pltpu.VMEM(border.shape[1:], border.dtype),
            pltpu.VMEM(columns.shape, columns.dtype),
            pltpu.SemaphoreType.DMA((6,)),
            pltpu.SemaphoreType.DMA((count,)),
        ],
        compiler_params=PARAMS,
        cost_estimate=long_cost(20),
        name="front",
    )(order, in_hbm(columns), in_hbm(factor), in_hbm(border), in_hbm(panel))
    return moved, keep, send, dealt


def whole_tiles(rows):
    return -(-rows // 16) * 16


def quarter_kernel(keep_ref, got_ref, *refs):
    count = (len(refs) + 1) // 2
    dealt, own_ref, out_refs = refs[: count - 1], refs[count - 1], refs[count:]
    place = lax.axis_index("col")
    rows = own_ref.shape[0]
    spare = whole_tiles(rows) - rows
    for m in range(count):
        at = pl.ds(pl.multiple_of((place ^ m) * rows, 8), rows)
        value = keep_ref[at, :] + got_ref[at, :]
        if m == 0:
            own_ref[...] = value
            continue
        if spare > 0:
            value = jnp.concatenate([value, jnp.zeros((spare, BLOCK), jnp.float32)], 0)
        border_ref, out_ref = dealt[m - 1], out_refs[m - 1]
        size, depth = border_ref.shape
        parts = list(split_two(value))
        parts += [border_ref[:, n : n + BLOCK] for n in range(0, depth, BLOCK)]
        first = 0
        for part in parts:
            out_ref[first : first + part.shape[0], :] = part
            first += part.shape[0]


def quarters(keep, got, dealt):
    count = len(dealt) + 1
    rows = keep.shape[0] // count
    length = 2 * whole_tiles(rows) + dealt[0].size // BLOCK
    own, *messages = pl.pallas_call(
        quarter_kernel,
        out_shape=[jax.ShapeDtypeStruct((rows, BLOCK), jnp.float32)]
        + [jax.ShapeDtypeStruct((length, BLOCK), jnp.bfloat16)] * (count - 1),
        in_specs=[VMEM] * (1 + count),
        out_specs=[VMEM] * count,
        compiler_params=PARAMS,
        name="quarters",
    )(keep, got, *dealt)
    return own, messages


def join_kernel(*refs, count):
    pieces, first_ref, last_ref, all_ref = refs[:count], refs[-3], refs[-2], refs[-1]
    place = lax.axis_index("col")
    rows = pieces[0].shape[0]
    for m, piece in enumerate(pieces):
        all_ref[pl.ds(pl.multiple_of((place ^ m) * rows, 8), rows), :] = piece[...]
    half = first_ref.shape[0]
    first_ref[...] = all_ref[:half, :]
    last_ref[...] = all_ref[half:, :]


def join(pieces, waits):
    rows = len(pieces) * pieces[0].shape[0]
    half = jax.ShapeDtypeStruct((rows // 2, BLOCK), jnp.float32)
    return pl.pallas_call(
        functools.partial(join_kernel, count=len(pieces)),
        out_shape=[half, half],
        in_specs=[VMEM] * len(pieces) + [ANY] * len(waits),
        out_specs=[VMEM, VMEM],
        scratch_shapes=[pltpu.VMEM((rows, BLOCK), jnp.float32)],
        compiler_params=PARAMS,
        name="join",
    )(*pieces, *waits)


def swap(value, axis, step):
    count = lax.axis_size(axis)
    return lax.ppermute(value, axis, [(i, i ^ step) for i in range(count)])


def tree_sum(values):
    while len(values) > 1:
        values = [values[i] + values[i + 1] for i in range(0, len(values), 2)]
    return values[0]


def row_of(tile, i):
    return jnp.broadcast_to(tile[i : i + 1, :], tile.shape)


def column_of(tile, j):
    index = jnp.full(tile.shape, j, jnp.int32)
    return jnp.take_along_axis(tile, index, axis=1, mode="promise_in_bounds")


def weighted_rows(weights, rows):
    total = weights[0] * rows[0]
    for weight, row in zip(weights[1:], rows[1:]):
        total = total + weight * row
    return total


def factor_block(block):
    groups = BLOCK // 8
    sub = lax.broadcasted_iota(jnp.int32, (8, BLOCK), 0)
    lane = lax.broadcasted_iota(jnp.int32, (8, BLOCK), 1)
    owner = lax.shift_right_logical(lane, 3)
    tiles = [block[8 * t : 8 * t + 8, :] for t in range(groups)]
    upper = []
    lower = []
    ready = None
    for pair in range(groups // 2):
        far = min(groups, 2 * pair + 4)
        swept = []
        for g in (2 * pair, 2 * pair + 1):
            more = g + 1 < groups
            tile = tiles[g]
            near = ready or [column_of(tile, 8 * g + m) for m in range(8)]
            if more:
                near = near + [column_of(tile, 8 * g + 8 + m) for m in range(8)]
            mixed = jnp.where(owner == g, (lane == sub + 8 * g).astype(jnp.float32), tile)
            out_tile, out_mixed = tile, mixed
            pivot = row_of(near[0], 0)
            for i in range(8):
                root = lax.rsqrt(pivot)
                recip = root * root
                rows = {m: row_of(near[m], i) for m in range(i + 1, len(near))}
                if i < 7:
                    pivot = row_of(near[i + 1], i + 1) - row_of(near[i], i + 1) * rows[i + 1] * recip
                factor = jnp.where(sub == i, 1.0 - recip, near[i] * recip)
                for m in rows:
                    near[m] = near[m] - factor * rows[m]
                row_tile, row_mixed = row_of(tile, i), row_of(mixed, i)
                out_tile = jnp.where(sub == i, row_tile * root, out_tile)
                out_mixed = jnp.where(sub == i, row_mixed * root, out_mixed)
                tile = tile - factor * row_tile
                mixed = mixed - factor * row_mixed
            inner = jnp.where((owner == g) & (lane >= sub + 8 * g), out_tile, 0.0)
            upper.append(jnp.where(owner > g, out_mixed, inner))
            lower.append(jnp.where(owner <= g, out_mixed, 0.0))
            rows = [row_of(mixed, i) for i in range(8)]
            swept.append((mixed, rows))
            if not more:
                break
            following = tiles[g + 1]
            weights = [column_of(following, 8 * g + i) for i in range(8)]
            ready = [
                column_of(following, 8 * g + 8 + m)
                - weighted_rows(weights, [row_of(near[8 + m], i) for i in range(8)])
                for m in range(8)
            ]
            for t in range(g + 1, far):
                if t > g + 1:
                    weights = [column_of(tiles[t], 8 * g + i) for i in range(8)]
                tiles[t] = jnp.where(owner == g, 0.0, tiles[t]) - weighted_rows(weights, rows)
        if far < groups:
            g = 2 * pair
            first, second = swept[0][0], swept[1][0]
            weights = [column_of(first, 8 * g + 8 + i) for i in range(8)]
            first = jnp.where(owner == g + 1, 0.0, first) - weighted_rows(weights, swept[1][1])
            parts = [first, second, jnp.zeros((BLOCK - 8 * g - 16, BLOCK), jnp.float32)]
            if g > 0:
                parts = [jnp.zeros((8 * g, BLOCK), jnp.float32)] + parts
            update = exact(jnp.concatenate(tiles[far:], 0), jnp.concatenate(parts, 0))
            for t in range(far, groups):
                kept = jnp.where((owner == g) | (owner == g + 1), 0.0, tiles[t])
                tiles[t] = kept - update[8 * (t - far) : 8 * (t - far) + 8]
    return jnp.concatenate(upper, 0), jnp.concatenate(lower, 0)


def cholesky_kernel(
    mine_first, mine_last, other_first, other_last, barrier_ref, inverse_ref, slice_ref, upper_ref,
    turned_ref, packed_ref
):
    width = barrier_ref.shape[1]
    count = width // BLOCK
    core = lax.rem(lax.axis_index("scen"), 2)
    place = lax.axis_index("col")
    row, lane = row_and_lane()
    diagonal = row == lane
    rows = mine_first.shape[0]
    for n, ref in enumerate((mine_first, mine_last, other_first, other_last)):
        owner = core if n < 2 else 1 - core
        at = (2 * owner + n % 2) * rows
        packed_ref[pl.ds(pl.multiple_of(at, 8), rows), :] = ref[...]
    blocks = unpack(packed_ref, width)
    for i in range(count):
        extra = barrier_ref[:, i * BLOCK : (i + 1) * BLOCK]
        blocks[i, i] = blocks[i, i] + jnp.where(diagonal, extra, 0.0)
    panels = [jnp.concatenate([blocks[i, j] for j in range(i, count)], 1) for i in range(count)]
    upper_ref[...] = jnp.zeros(upper_ref.shape, jnp.float32)
    inverse_ref[...] = jnp.zeros(inverse_ref.shape, jnp.float32)
    for i in range(count):
        here = slice(i * BLOCK, (i + 1) * BLOCK)
        before = slice(0, i * BLOCK)
        own, inverse = factor_block(panels[i][:, :BLOCK])
        upper_ref[here, here] = own
        inverse_ref[here, here] = inverse
        if i + 1 < count:
            rest = exact(inverse, panels[i][:, BLOCK:])
            upper_ref[here, (i + 1) * BLOCK :] = rest
            for j in range(i + 1, count):
                at = (j - i - 1) * BLOCK
                panels[j] = panels[j] - exact_tn(rest[:, at : at + BLOCK], rest[:, at:])
        if i > 0:
            mixed = exact_tn(upper_ref[before, here], inverse_ref[before, before])
            inverse_ref[here, before] = -exact(inverse, mixed)
    slice_rows = slice_ref.shape[0]
    start = place * slice_rows
    block = pl.ds(pl.multiple_of(start // BLOCK * BLOCK, BLOCK), BLOCK)
    turned_ref[...] = upper_ref[:, block].T
    slice_ref[...] = turned_ref[pl.ds(pl.multiple_of(lax.rem(start, BLOCK), 8), slice_rows), :]


def cholesky(halves, barrier, col_count):
    width = barrier.shape[0]
    return pl.pallas_call(
        cholesky_kernel,
        out_shape=[
            jax.ShapeDtypeStruct((width, width), jnp.float32),
            jax.ShapeDtypeStruct((width // col_count, width), jnp.float32),
        ],
        in_specs=[VMEM] * 5,
        out_specs=[VMEM] * 2,
        scratch_shapes=[
            pltpu.VMEM((width, width), jnp.float32),
            pltpu.VMEM((BLOCK, width), jnp.float32),
            pltpu.VMEM((4 * halves[0].shape[0], BLOCK), jnp.float32),
        ],
        compiler_params=PARAMS,
        cost_estimate=long_cost(0),
        name="cholesky",
    )(*halves, barrier[None])


def coupling_kernel(moved_ref, own_ref, border_ref, *refs):
    count = len(refs) // 2
    messages, total_ref, out_refs = refs[: count - 1], refs[count - 1], refs[count:]
    rows = own_ref.shape[0]
    size, depth = border_ref.shape
    tiles = whole_tiles(rows)
    moved = moved_ref[...]
    out_refs[0][...] = matmul_nt(border_ref[...], moved)
    parts = [own_ref[...]]
    for message, out_ref in zip(messages, out_refs[1:]):
        high = message[:tiles, :].astype(jnp.float32)
        low = message[tiles : 2 * tiles, :].astype(jnp.float32)
        parts.append((high + low)[:rows])
        first = [2 * tiles + n * size for n in range(depth // BLOCK)]
        border = jnp.concatenate([message[at : at + size, :] for at in first], 1)
        out_ref[...] = matmul_nt(border, moved)
    total_ref[...] = tree_sum(parts)


def sum_and_couplings(own, messages, moved, border):
    shape = jax.ShapeDtypeStruct((border.shape[0], moved.shape[0]), jnp.float32)
    total, *partial = pl.pallas_call(
        coupling_kernel,
        out_shape=[jax.ShapeDtypeStruct(own.shape, jnp.float32)] + [shape] * (len(messages) + 1),
        in_specs=[VMEM] * (len(messages) + 3),
        out_specs=[VMEM] * (len(messages) + 2),
        compiler_params=PARAMS,
        name="couplings",
    )(moved, own, border, *messages)
    return total, partial


def assemble_kernel(columns_ref, rows_ref, *refs, parts):
    refs[-2][...] = tree_sum([ref[...] for ref in refs[:parts]])
    pieces, out_ref = refs[parts:-2], refs[-1]
    place = lax.axis_index("col")
    size = pieces[0].shape[0]
    count = len(pieces)
    for m, piece in enumerate(pieces):
        out_ref[pl.ds(pl.multiple_of((place ^ m) * size, 8), size), :] = piece[...]
    at = count * size
    out_ref[at:, :] = jnp.zeros((out_ref.shape[0] - at, out_ref.shape[1]), jnp.float32)
    out_ref[at : at + count, :] = columns_ref[...].astype(jnp.float32)
    out_ref[at + count : at + 2 * count, :size] = rows_ref[0].astype(jnp.float32)


def sum_and_assemble(parts, pieces, columns, rows):
    size, wide = pieces[0].shape
    count = len(pieces)
    return pl.pallas_call(
        functools.partial(assemble_kernel, parts=len(parts)),
        out_shape=[
            jax.ShapeDtypeStruct(parts[0].shape, jnp.float32),
            jax.ShapeDtypeStruct((count * size + -(-count // 4) * 8, wide), jnp.float32),
        ],
        in_specs=[VMEM] * (len(parts) + count + 2),
        out_specs=[VMEM] * 2,
        compiler_params=PARAMS,
        name="assemble",
    )(columns, rows, *parts, *pieces)


def placed_rows(groups, group, rows_here, width):
    place = lax.axis_index("scen")
    first = (place - lax.rem(place, 2)) * rows_here
    size = (groups[0].shape[0] - 2 * group) // group
    wide = groups[0].shape[1]
    total = None
    slot = lax.broadcasted_iota(jnp.int32, (2 * rows_here, group * size), 0)
    for group_ref in groups:
        index = group_ref[group * size :, :]
        spreads = []
        for i in range(group):
            columns = index[i : i + 1, :].astype(jnp.int32)
            spread = lax.broadcasted_iota(jnp.int32, (width, wide), 0) == columns
            high, low = split_two(group_ref[i * size : (i + 1) * size, :])
            both = matmul_nt(jnp.concatenate([high, low], 0), spread.astype(jnp.bfloat16))
            spreads.append(both[:size] + both[size:])
        row_index = jnp.concatenate(
            [index[group + i : group + i + 1, :size] for i in range(group)], 1
        )
        row_map = (slot == row_index.astype(jnp.int32) - first).astype(jnp.bfloat16)
        high, low = split_two(jnp.concatenate(spreads, 0))
        part = matmul(row_map, high) + matmul(row_map, low)
        total = part if total is None else total + part
    return total


def near_kernel(*refs, group):
    groups, out_ref = refs[:-1], refs[-1]
    rows, width = out_ref.shape
    out_ref[...] = placed_rows(groups, group, rows // 2, width)


def near_rows(groups, group, rows_here, width):
    return pl.pallas_call(
        functools.partial(near_kernel, group=group),
        out_shape=jax.ShapeDtypeStruct((2 * rows_here, width), jnp.float32),
        in_specs=[VMEM] * len(groups),
        out_specs=VMEM,
        compiler_params=PARAMS,
        cost_estimate=long_cost(0),
        name="near",
    )(*groups)


def far_kernel(wait_ref, near_ref, *refs, group):
    groups = refs[:-2]
    keep_ref, send_ref = refs[-2:]
    rows_here, width = keep_ref.shape
    core = lax.rem(lax.axis_index("scen"), 2)
    total = near_ref[...] + placed_rows(groups, group, rows_here, width)
    lower, upper = total[:rows_here], total[rows_here:]
    keep_ref[...] = jnp.where(core == 0, lower, upper)
    send_ref[...] = jnp.where(core == 0, upper, lower)


def far_rows(near, groups, group, wait):
    rows, width = near.shape
    half = jax.ShapeDtypeStruct((rows // 2, width), jnp.float32)
    return pl.pallas_call(
        functools.partial(far_kernel, group=group),
        out_shape=[half, half],
        in_specs=[ANY] + [VMEM] * (1 + len(groups)),
        out_specs=[VMEM, VMEM],
        compiler_params=PARAMS,
        cost_estimate=long_cost(0),
        name="far",
    )(wait, near, *groups)


def solve_kernel(keep_ref, got_ref, inverse_ref, out_ref):
    out_ref[...] = exact_nt(keep_ref[...] + got_ref[...], inverse_ref[...])


def solve_rows(keep, got, inverse):
    return pl.pallas_call(
        solve_kernel,
        out_shape=jax.ShapeDtypeStruct(keep.shape, jnp.float32),
        in_specs=[VMEM] * 3,
        out_specs=VMEM,
        compiler_params=PARAMS,
        name="solve",
    )(keep, got, inverse)


def dense_panel(couplings_here, rows, columns, rows_panel, width):
    def step(running, operands):
        coupling, row_index, column_index = operands
        column_map = (column_index[:, None] == jnp.arange(width)[None, :]).astype(jnp.float32)
        row_map = (row_index[:, None] == jnp.arange(rows_panel)[None, :]).astype(jnp.float32)
        widened = jnp.dot(coupling, column_map, precision=HIGHEST)
        return running + jnp.einsum("br,bd->rd", row_map, widened, precision=HIGHEST), None

    zero = jnp.zeros((rows_panel, width), jnp.float32)
    total, _ = lax.scan(step, zero, (couplings_here, rows, columns))
    return lax.psum_scatter(total, "scen", scatter_dimension=0, tiled=True)


def shards(
    rows_here,
    inverse_factor,
    true_orders,
    slab_border,
    slab_columns,
    panel_border,
    panel_rows,
    barrier_diag,
):
    scen_count = lax.axis_size("scen")
    col_count = lax.axis_size("col")
    width = barrier_diag.shape[0]
    group, size = panel_border.shape[1:3]
    wide = slab_columns.shape[1]

    moved, keep, send, dealt = front(
        true_orders, slab_columns, inverse_factor, slab_border, panel_border, width
    )
    got = swap(send, "scen", 1)
    part, messages = quarters(keep, got, dealt[1:])
    messages = [swap(message, "col", m + 1) for m, message in enumerate(messages)]
    part, partial = sum_and_couplings(part, messages, moved, dealt[0])
    parts = [part] + [swap(part, "scen", 2 * m) for m in range(1, scen_count // 2)]
    pieces = [partial[0]] + [swap(partial[m], "col", m) for m in range(1, col_count)]
    part, own = sum_and_assemble(parts, pieces, slab_columns, panel_rows)
    rows_panel = rows_here * scen_count
    sparse = scen_count * group * size * wide < rows_panel * width
    groups = [own]
    if sparse:
        groups += [swap(own, "scen", 2 * m) for m in range(1, scen_count // 2)]
    near = [near_rows([own], group, rows_here, width)] if sparse else []
    mine = join([part] + [swap(part, "col", m) for m in range(1, col_count)], near)
    halves = list(mine) + [swap(half, "scen", 1) for half in mine]
    inverse, factor_rows = cholesky(halves, barrier_diag, col_count)
    if sparse:
        rows, other = far_rows(near[0], groups[1:], group, inverse)
        solved = solve_rows(rows, swap(other, "scen", 1), inverse)
    else:
        local = own[: group * size].reshape(group, size, wide)
        rows = dense_panel(local, panel_rows[0], slab_columns, rows_panel, width)
        solved = jnp.dot(rows, inverse.T, precision=HIGHEST)
    return factor_rows, solved


def solution(mesh):
    in_specs = (
        P(("scen", "col"), None, None),
        P(("scen", "col")),
        P(("scen", "col"), None, None),
        P("scen", None),
        P("col", "scen", None, None),
        P("col", "scen", None),
        P(),
    )
    out_specs = (P("col", None), P(("scen", "col"), None))

    def whole(*args):
        devices = mesh.shape["scen"] * mesh.shape["col"]
        first_section = NF - args[-1].shape[0]
        body = functools.partial(shards, first_section // devices)
        return jax.shard_map(
            body, mesh=mesh, in_specs=in_specs, out_specs=out_specs, check_vma=False
        )(*args)

    return whole
```

```python
import functools

import jax
import jax.numpy as jnp
from jax import lax
from jax.experimental import pallas as pl
from jax.experimental.pallas import tpu as pltpu
from jax.sharding import PartitionSpec as P

NF = 8192
BLOCK = 128
HIGHEST = lax.Precision.HIGHEST
VMEM = pl.BlockSpec(memory_space=pltpu.VMEM)
SMEM = pl.BlockSpec(memory_space=pltpu.SMEM)
HBM = pl.BlockSpec(memory_space=pltpu.HBM)
ANY = pl.BlockSpec(memory_space=pl.ANY)
PARAMS = pltpu.CompilerParams(vmem_limit_bytes=40 * 2**20)


def long_cost(micros):
    return pl.CostEstimate(flops=micros * 10**9, bytes_accessed=2**10, transcendentals=0)


def in_hbm(value):
    return pltpu.with_memory_space_constraint(value, pltpu.HBM)


def split_two(value):
    high = value.astype(jnp.bfloat16)
    low = (value - high.astype(jnp.float32)).astype(jnp.bfloat16)
    return high, low


def matmul(left, right):
    return jnp.dot(left, right, preferred_element_type=jnp.float32)


def matmul_nt(left, right):
    return lax.dot_general(
        left, right, (((1,), (1,)), ((), ())), preferred_element_type=jnp.float32
    )


def exact_tn(left, right):
    return lax.dot_general(
        left,
        right,
        (((0,), (0,)), ((), ())),
        precision=HIGHEST,
        preferred_element_type=jnp.float32,
    )


def exact(left, right):
    return jnp.dot(left, right, precision=HIGHEST, preferred_element_type=jnp.float32)


def exact_nt(left, right):
    return lax.dot_general(
        left,
        right,
        (((1,), (1,)), ((), ())),
        precision=HIGHEST,
        preferred_element_type=jnp.float32,
    )


def packed_rows(width, unit):
    count = width // BLOCK
    rows = (count * (count - 1) // 2 + count // 2) * BLOCK + count // 2
    return -(-rows // unit) * unit


def upper_blocks(width):
    count = width // BLOCK
    return [(i, j) for i in range(count) for j in range(i + 1, count)]


def row_and_lane():
    shape = (BLOCK, BLOCK)
    return lax.broadcasted_iota(jnp.int32, shape, 0), lax.broadcasted_iota(jnp.int32, shape, 1)


def pack(blocks, width, packed_ref):
    row, lane = row_and_lane()
    first = 0
    for name in upper_blocks(width):
        packed_ref[first : first + BLOCK, :] = blocks[name]
        first += BLOCK
    diagonals = []
    for i in range(0, width // BLOCK, 2):
        one, two = blocks[i, i], blocks[i + 1, i + 1]
        packed_ref[first : first + BLOCK, :] = jnp.where(row <= lane, one, two)
        first += BLOCK
        diagonals.append(jnp.sum(jnp.where(row == lane, two, 0.0), 0, keepdims=True))
    spare = packed_ref.shape[0] - first - len(diagonals)
    diagonals.append(jnp.zeros((spare, BLOCK), jnp.float32))
    packed_ref[first:, :] = jnp.concatenate(diagonals, 0)


def unpack(packed_ref, width):
    row, lane = row_and_lane()
    blocks = {}
    first = 0
    for name in upper_blocks(width):
        blocks[name] = packed_ref[first : first + BLOCK, :]
        first += BLOCK
    last = first + width // BLOCK // 2 * BLOCK
    for n in range(width // BLOCK // 2):
        square = packed_ref[first + n * BLOCK : first + (n + 1) * BLOCK, :]
        turned = square.T
        blocks[2 * n, 2 * n] = jnp.where(row <= lane, square, turned)
        diagonal = packed_ref[last + n : last + n + 1, :]
        other = jnp.where(row > lane, square, turned)
        blocks[2 * n + 1, 2 * n + 1] = jnp.where(row == lane, diagonal, other)
    return blocks


def front_kernel(
    order_ref,
    columns_ref,
    factor_ref,
    border_ref,
    panel_ref,
    moved_ref,
    keep_ref,
    send_ref,
    *refs,
    width,
):
    dealt = refs[:-6]
    packed_ref, factor_here, border_here, columns_here, sems, deal_sems = refs[-6:]
    place = lax.axis_index("col")
    chunk = factor_here.shape[0] // 4
    chunks = [slice(k * chunk, (k + 1) * chunk) for k in range(4)]
    loads = [pltpu.make_async_copy(border_ref.at[0], border_here, sems.at[0])]
    for k, at in enumerate(chunks):
        loads.append(
            pltpu.make_async_copy(factor_ref.at[0, at], factor_here.at[at], sems.at[k + 1])
        )
    loads.append(pltpu.make_async_copy(columns_ref, columns_here, sems.at[5]))
    for load in loads:
        load.start()
    deals = [
        pltpu.make_async_copy(panel_ref.at[0, place ^ m], out_ref, deal_sems.at[m])
        for m, out_ref in enumerate(dealt)
    ]
    for load in deals:
        load.start()
    core = lax.rem(lax.axis_index("scen"), 2)
    order = order_ref[0]
    loads[0].wait()
    border = border_here[...]
    within = lax.broadcasted_iota(jnp.int32, border.shape, 1) < order
    inside = jnp.where(within, border.astype(jnp.float32), 0.0).astype(jnp.bfloat16)
    product = jnp.zeros(border.shape, jnp.float32)
    for k, at in enumerate(chunks):
        loads[k + 1].wait()
        product = product + matmul(inside[:, at], factor_here[at])
    moved = jnp.where(within, product, 0.0).astype(jnp.bfloat16)
    moved_ref[...] = moved
    loads[5].wait()
    columns = columns_here[pl.ds(place, 1), :]
    spread = (
        lax.broadcasted_iota(jnp.int32, (width, columns.shape[1]), 0) == columns
    ).astype(jnp.bfloat16)
    terms = 0.5 * (matmul_nt(border, moved) + matmul_nt(moved, border))
    high, low = split_two(terms)
    half_spread = matmul_nt(high, spread) + matmul_nt(low, spread)
    high, low = split_two(half_spread)
    blocks = {}
    for i in range(width // BLOCK):
        rows = spread[i * BLOCK : (i + 1) * BLOCK]
        part = matmul(rows, high[:, i * BLOCK :]) + matmul(rows, low[:, i * BLOCK :])
        for j in range(i, width // BLOCK):
            blocks[i, j] = part[:, (j - i) * BLOCK : (j - i + 1) * BLOCK]
    pack(blocks, width, packed_ref)
    half = keep_ref.shape[0]
    keep_ref[...] = packed_ref[pl.ds(pl.multiple_of(core * half, 8), half), :]
    send_ref[...] = packed_ref[pl.ds(pl.multiple_of((1 - core) * half, 8), half), :]
    for load in deals:
        load.wait()


def front(order, columns, factor, border, panel, width):
    count = panel.shape[1]
    total = packed_rows(width, 16 * count)
    half = jax.ShapeDtypeStruct((total // 2, BLOCK), jnp.float32)
    piece = jax.ShapeDtypeStruct(panel.shape[2:], panel.dtype)
    moved, keep, send, *dealt = pl.pallas_call(
        functools.partial(front_kernel, width=width),
        out_shape=[jax.ShapeDtypeStruct(border.shape[1:], jnp.bfloat16), half, half]
        + [piece] * count,
        in_specs=[SMEM, HBM, HBM, HBM, HBM],
        out_specs=[VMEM] * (3 + count),
        scratch_shapes=[
            pltpu.VMEM((total, BLOCK), jnp.float32),
            pltpu.VMEM(factor.shape[1:], factor.dtype),
            pltpu.VMEM(border.shape[1:], border.dtype),
            pltpu.VMEM(columns.shape, columns.dtype),
            pltpu.SemaphoreType.DMA((6,)),
            pltpu.SemaphoreType.DMA((count,)),
        ],
        compiler_params=PARAMS,
        cost_estimate=long_cost(20),
        name="front",
    )(order, in_hbm(columns), in_hbm(factor), in_hbm(border), in_hbm(panel))
    return moved, keep, send, dealt


def whole_tiles(rows):
    return -(-rows // 16) * 16


def quarter_kernel(keep_ref, got_ref, *refs):
    count = (len(refs) + 1) // 2
    dealt, own_ref, out_refs = refs[: count - 1], refs[count - 1], refs[count:]
    place = lax.axis_index("col")
    rows = own_ref.shape[0]
    spare = whole_tiles(rows) - rows
    for m in range(count):
        at = pl.ds(pl.multiple_of((place ^ m) * rows, 8), rows)
        value = keep_ref[at, :] + got_ref[at, :]
        if m == 0:
            own_ref[...] = value
            continue
        if spare > 0:
            value = jnp.concatenate([value, jnp.zeros((spare, BLOCK), jnp.float32)], 0)
        border_ref, out_ref = dealt[m - 1], out_refs[m - 1]
        size, depth = border_ref.shape
        parts = list(split_two(value))
        parts += [border_ref[:, n : n + BLOCK] for n in range(0, depth, BLOCK)]
        first = 0
        for part in parts:
            out_ref[first : first + part.shape[0], :] = part
            first += part.shape[0]


def quarters(keep, got, dealt):
    count = len(dealt) + 1
    rows = keep.shape[0] // count
    length = 2 * whole_tiles(rows) + dealt[0].size // BLOCK
    own, *messages = pl.pallas_call(
        quarter_kernel,
        out_shape=[jax.ShapeDtypeStruct((rows, BLOCK), jnp.float32)]
        + [jax.ShapeDtypeStruct((length, BLOCK), jnp.bfloat16)] * (count - 1),
        in_specs=[VMEM] * (1 + count),
        out_specs=[VMEM] * count,
        compiler_params=PARAMS,
        name="quarters",
    )(keep, got, *dealt)
    return own, messages


def join_kernel(*refs, count):
    pieces, first_ref, last_ref, all_ref = refs[:count], refs[-3], refs[-2], refs[-1]
    place = lax.axis_index("col")
    rows = pieces[0].shape[0]
    for m, piece in enumerate(pieces):
        all_ref[pl.ds(pl.multiple_of((place ^ m) * rows, 8), rows), :] = piece[...]
    half = first_ref.shape[0]
    first_ref[...] = all_ref[:half, :]
    last_ref[...] = all_ref[half:, :]


def join(pieces):
    rows = len(pieces) * pieces[0].shape[0]
    half = jax.ShapeDtypeStruct((rows // 2, BLOCK), jnp.float32)
    return pl.pallas_call(
        functools.partial(join_kernel, count=len(pieces)),
        out_shape=[half, half],
        in_specs=[VMEM] * len(pieces),
        out_specs=[VMEM, VMEM],
        scratch_shapes=[pltpu.VMEM((rows, BLOCK), jnp.float32)],
        compiler_params=PARAMS,
        name="join",
    )(*pieces)


def swap(value, axis, step):
    count = lax.axis_size(axis)
    return lax.ppermute(value, axis, [(i, i ^ step) for i in range(count)])


def tree_sum(values):
    while len(values) > 1:
        values = [values[i] + values[i + 1] for i in range(0, len(values), 2)]
    return values[0]


def row_of(tile, i):
    return jnp.broadcast_to(tile[i : i + 1, :], tile.shape)


def column_of(tile, j):
    index = jnp.full(tile.shape, j, jnp.int32)
    return jnp.take_along_axis(tile, index, axis=1, mode="promise_in_bounds")


def weighted_rows(weights, rows):
    total = weights[0] * rows[0]
    for weight, row in zip(weights[1:], rows[1:]):
        total = total + weight * row
    return total


def factor_block(block):
    groups = BLOCK // 8
    sub = lax.broadcasted_iota(jnp.int32, (8, BLOCK), 0)
    lane = lax.broadcasted_iota(jnp.int32, (8, BLOCK), 1)
    owner = lax.shift_right_logical(lane, 3)
    tiles = [block[8 * t : 8 * t + 8, :] for t in range(groups)]
    upper = []
    lower = []
    ready = None
    for pair in range(groups // 2):
        far = min(groups, 2 * pair + 4)
        swept = []
        for g in (2 * pair, 2 * pair + 1):
            more = g + 1 < groups
            tile = tiles[g]
            near = ready or [column_of(tile, 8 * g + m) for m in range(8)]
            if more:
                near = near + [column_of(tile, 8 * g + 8 + m) for m in range(8)]
            mixed = jnp.where(owner == g, (lane == sub + 8 * g).astype(jnp.float32), tile)
            out_tile, out_mixed = tile, mixed
            pivot = row_of(near[0], 0)
            for i in range(8):
                root = lax.rsqrt(pivot)
                recip = root * root
                rows = {m: row_of(near[m], i) for m in range(i + 1, len(near))}
                if i < 7:
                    pivot = row_of(near[i + 1], i + 1) - row_of(near[i], i + 1) * rows[i + 1] * recip
                factor = jnp.where(sub == i, 1.0 - recip, near[i] * recip)
                for m in rows:
                    near[m] = near[m] - factor * rows[m]
                row_tile, row_mixed = row_of(tile, i), row_of(mixed, i)
                out_tile = jnp.where(sub == i, row_tile * root, out_tile)
                out_mixed = jnp.where(sub == i, row_mixed * root, out_mixed)
                tile = tile - factor * row_tile
                mixed = mixed - factor * row_mixed
            inner = jnp.where((owner == g) & (lane >= sub + 8 * g), out_tile, 0.0)
            upper.append(jnp.where(owner > g, out_mixed, inner))
            lower.append(jnp.where(owner <= g, out_mixed, 0.0))
            rows = [row_of(mixed, i) for i in range(8)]
            swept.append((mixed, rows))
            if not more:
                break
            following = tiles[g + 1]
            weights = [column_of(following, 8 * g + i) for i in range(8)]
            ready = [
                column_of(following, 8 * g + 8 + m)
                - weighted_rows(weights, [row_of(near[8 + m], i) for i in range(8)])
                for m in range(8)
            ]
            for t in range(g + 1, far):
                if t > g + 1:
                    weights = [column_of(tiles[t], 8 * g + i) for i in range(8)]
                tiles[t] = jnp.where(owner == g, 0.0, tiles[t]) - weighted_rows(weights, rows)
        if far < groups:
            g = 2 * pair
            first, second = swept[0][0], swept[1][0]
            weights = [column_of(first, 8 * g + 8 + i) for i in range(8)]
            first = jnp.where(owner == g + 1, 0.0, first) - weighted_rows(weights, swept[1][1])
            parts = [first, second, jnp.zeros((BLOCK - 8 * g - 16, BLOCK), jnp.float32)]
            if g > 0:
                parts = [jnp.zeros((8 * g, BLOCK), jnp.float32)] + parts
            update = exact(jnp.concatenate(tiles[far:], 0), jnp.concatenate(parts, 0))
            for t in range(far, groups):
                kept = jnp.where((owner == g) | (owner == g + 1), 0.0, tiles[t])
                tiles[t] = kept - update[8 * (t - far) : 8 * (t - far) + 8]
    return jnp.concatenate(upper, 0), jnp.concatenate(lower, 0)


def placed_rows(groups, group, rows_here, width):
    place = lax.axis_index("scen")
    first = (place - lax.rem(place, 2)) * rows_here
    size = (groups[0].shape[0] - 2 * group) // group
    wide = groups[0].shape[1]
    total = None
    slot = lax.broadcasted_iota(jnp.int32, (2 * rows_here, group * size), 0)
    for group_ref in groups:
        index = group_ref[group * size :, :]
        spreads = []
        for i in range(group):
            columns = index[i : i + 1, :].astype(jnp.int32)
            spread = lax.broadcasted_iota(jnp.int32, (width, wide), 0) == columns
            high, low = split_two(group_ref[i * size : (i + 1) * size, :])
            both = matmul_nt(jnp.concatenate([high, low], 0), spread.astype(jnp.bfloat16))
            spreads.append(both[:size] + both[size:])
        row_index = jnp.concatenate(
            [index[group + i : group + i + 1, :size] for i in range(group)], 1
        )
        row_map = (slot == row_index.astype(jnp.int32) - first).astype(jnp.bfloat16)
        high, low = split_two(jnp.concatenate(spreads, 0))
        part = matmul(row_map, high) + matmul(row_map, low)
        total = part if total is None else total + part
    return total


def cholesky_kernel(
    mine_first, mine_last, other_first, other_last, barrier_ref, *refs, group
):
    upper_ref, turned_ref, packed_ref = refs[-3:]
    near, near_out = (refs[:1], refs[3:4]) if len(refs) == 7 else ((), ())
    inverse_ref, slice_ref = refs[len(near) : len(near) + 2]
    width = barrier_ref.shape[1]
    count = width // BLOCK
    core = lax.rem(lax.axis_index("scen"), 2)
    place = lax.axis_index("col")
    row, lane = row_and_lane()
    diagonal = row == lane
    rows = mine_first.shape[0]
    for n, ref in enumerate((mine_first, mine_last, other_first, other_last)):
        owner = core if n < 2 else 1 - core
        at = (2 * owner + n % 2) * rows
        packed_ref[pl.ds(pl.multiple_of(at, 8), rows), :] = ref[...]
    blocks = unpack(packed_ref, width)
    for i in range(count):
        extra = barrier_ref[:, i * BLOCK : (i + 1) * BLOCK]
        blocks[i, i] = blocks[i, i] + jnp.where(diagonal, extra, 0.0)
    panels = [jnp.concatenate([blocks[i, j] for j in range(i, count)], 1) for i in range(count)]
    slice_rows = slice_ref.shape[0]
    start = place * slice_rows
    block = pl.ds(pl.multiple_of(start // BLOCK * BLOCK, BLOCK), BLOCK)
    upper_ref[...] = jnp.zeros(upper_ref.shape, jnp.float32)
    inverse_ref[...] = jnp.zeros(inverse_ref.shape, jnp.float32)
    for i in range(count):
        here = slice(i * BLOCK, (i + 1) * BLOCK)
        before = slice(0, i * BLOCK)
        own, inverse = factor_block(panels[i][:, :BLOCK])
        if i == 0 and near_out:
            rows_near = near_out[0].shape[0] // 2
            near_out[0][...] = placed_rows(near, group, rows_near, width)
        upper_ref[here, here] = own
        inverse_ref[here, here] = inverse
        if i + 1 < count:
            rest = []
            for j in range(i + 1, count):
                at = (j - i) * BLOCK
                rest.append(exact(inverse, panels[i][:, at : at + BLOCK]))
                upper_ref[here, j * BLOCK : (j + 1) * BLOCK] = rest[-1]
                if j == i + 1:
                    square = panels[j][:, :BLOCK] - exact_tn(rest[0], rest[0])
            for j in range(i + 1, count):
                parts = [square] if j == i + 1 else []
                done = len(parts)
                if done < count - j:
                    wide = jnp.concatenate(rest[j - i - 1 + done :], 1)
                    update = exact_tn(rest[j - i - 1], wide)
                    parts.append(panels[j][:, done * BLOCK :] - update)
                panels[j] = jnp.concatenate(parts, 1)
        if i + 2 == count:
            turned_ref[:, : (i + 1) * BLOCK] = upper_ref[: (i + 1) * BLOCK, block].T
        if i > 0:
            mixed = exact_tn(upper_ref[before, here], inverse_ref[before, before])
            inverse_ref[here, before] = -exact(inverse, mixed)
    turned_ref[:, width - BLOCK :] = upper_ref[width - BLOCK :, block].T
    slice_ref[...] = turned_ref[pl.ds(pl.multiple_of(lax.rem(start, BLOCK), 8), slice_rows), :]


def cholesky(halves, barrier, col_count, near, group, rows_here):
    width = barrier.shape[0]
    placed = [jax.ShapeDtypeStruct((2 * rows_here, width), jnp.float32)] * len(near)
    return pl.pallas_call(
        functools.partial(cholesky_kernel, group=group),
        out_shape=[
            jax.ShapeDtypeStruct((width, width), jnp.float32),
            jax.ShapeDtypeStruct((width // col_count, width), jnp.float32),
        ]
        + placed,
        in_specs=[VMEM] * (5 + len(near)),
        out_specs=[VMEM] * (2 + len(near)),
        scratch_shapes=[
            pltpu.VMEM((width, width), jnp.float32),
            pltpu.VMEM((BLOCK, width), jnp.float32),
            pltpu.VMEM((4 * halves[0].shape[0], BLOCK), jnp.float32),
        ],
        compiler_params=PARAMS,
        cost_estimate=long_cost(0),
        name="cholesky",
    )(*halves, barrier[None], *near)


def coupling_kernel(moved_ref, own_ref, border_ref, *refs):
    count = len(refs) // 2
    messages, total_ref, out_refs = refs[: count - 1], refs[count - 1], refs[count:]
    rows = own_ref.shape[0]
    size, depth = border_ref.shape
    tiles = whole_tiles(rows)
    moved = moved_ref[...]
    out_refs[0][...] = matmul_nt(border_ref[...], moved)
    parts = [own_ref[...]]
    for message, out_ref in zip(messages, out_refs[1:]):
        high = message[:tiles, :].astype(jnp.float32)
        low = message[tiles : 2 * tiles, :].astype(jnp.float32)
        parts.append((high + low)[:rows])
        first = [2 * tiles + n * size for n in range(depth // BLOCK)]
        border = jnp.concatenate([message[at : at + size, :] for at in first], 1)
        out_ref[...] = matmul_nt(border, moved)
    total_ref[...] = tree_sum(parts)


def sum_and_couplings(own, messages, moved, border):
    shape = jax.ShapeDtypeStruct((border.shape[0], moved.shape[0]), jnp.float32)
    total, *partial = pl.pallas_call(
        coupling_kernel,
        out_shape=[jax.ShapeDtypeStruct(own.shape, jnp.float32)] + [shape] * (len(messages) + 1),
        in_specs=[VMEM] * (len(messages) + 3),
        out_specs=[VMEM] * (len(messages) + 2),
        compiler_params=PARAMS,
        name="couplings",
    )(moved, own, border, *messages)
    return total, partial


def assemble_kernel(columns_ref, rows_ref, *refs, parts):
    refs[-2][...] = tree_sum([ref[...] for ref in refs[:parts]])
    pieces, out_ref = refs[parts:-2], refs[-1]
    place = lax.axis_index("col")
    size = pieces[0].shape[0]
    count = len(pieces)
    for m, piece in enumerate(pieces):
        out_ref[pl.ds(pl.multiple_of((place ^ m) * size, 8), size), :] = piece[...]
    at = count * size
    out_ref[at:, :] = jnp.zeros((out_ref.shape[0] - at, out_ref.shape[1]), jnp.float32)
    out_ref[at : at + count, :] = columns_ref[...].astype(jnp.float32)
    out_ref[at + count : at + 2 * count, :size] = rows_ref[0].astype(jnp.float32)


def sum_and_assemble(parts, pieces, columns, rows):
    size, wide = pieces[0].shape
    count = len(pieces)
    return pl.pallas_call(
        functools.partial(assemble_kernel, parts=len(parts)),
        out_shape=[
            jax.ShapeDtypeStruct(parts[0].shape, jnp.float32),
            jax.ShapeDtypeStruct((count * size + -(-count // 4) * 8, wide), jnp.float32),
        ],
        in_specs=[VMEM] * (len(parts) + count + 2),
        out_specs=[VMEM] * 2,
        compiler_params=PARAMS,
        name="assemble",
    )(columns, rows, *parts, *pieces)


def far_kernel(wait_ref, near_ref, *refs, group):
    groups = refs[:-2]
    keep_ref, send_ref = refs[-2:]
    rows_here, width = keep_ref.shape
    core = lax.rem(lax.axis_index("scen"), 2)
    total = near_ref[...] + placed_rows(groups, group, rows_here, width)
    lower, upper = total[:rows_here], total[rows_here:]
    keep_ref[...] = jnp.where(core == 0, lower, upper)
    send_ref[...] = jnp.where(core == 0, upper, lower)


def far_rows(near, groups, group, wait):
    rows, width = near.shape
    half = jax.ShapeDtypeStruct((rows // 2, width), jnp.float32)
    return pl.pallas_call(
        functools.partial(far_kernel, group=group),
        out_shape=[half, half],
        in_specs=[ANY] + [VMEM] * (1 + len(groups)),
        out_specs=[VMEM, VMEM],
        compiler_params=PARAMS,
        cost_estimate=long_cost(0),
        name="far",
    )(wait, near, *groups)


def solve_kernel(keep_ref, got_ref, inverse_ref, out_ref, solved_ref, sems):
    half = out_ref.shape[1] // 2
    first, last = slice(0, half), slice(half, 2 * half)
    rows = keep_ref[...] + got_ref[...]
    stores = []
    for n, (here, inner) in enumerate(((last, slice(0, 2 * half)), (first, first))):
        solved_ref[:, here] = exact_nt(rows[:, inner], inverse_ref[here, inner])
        stores.append(pltpu.make_async_copy(solved_ref.at[:, here], out_ref.at[:, here], sems.at[n]))
        stores[-1].start()
    for store in stores:
        store.wait()


def solve_rows(keep, got, inverse):
    return pl.pallas_call(
        solve_kernel,
        out_shape=jax.ShapeDtypeStruct(keep.shape, jnp.float32),
        in_specs=[VMEM] * 3,
        out_specs=HBM,
        scratch_shapes=[pltpu.VMEM(keep.shape, jnp.float32), pltpu.SemaphoreType.DMA((2,))],
        compiler_params=PARAMS,
        name="solve",
    )(keep, got, inverse)


def dense_panel(couplings_here, rows, columns, rows_panel, width):
    def step(running, operands):
        coupling, row_index, column_index = operands
        column_map = (column_index[:, None] == jnp.arange(width)[None, :]).astype(jnp.float32)
        row_map = (row_index[:, None] == jnp.arange(rows_panel)[None, :]).astype(jnp.float32)
        widened = jnp.dot(coupling, column_map, precision=HIGHEST)
        return running + jnp.einsum("br,bd->rd", row_map, widened, precision=HIGHEST), None

    zero = jnp.zeros((rows_panel, width), jnp.float32)
    total, _ = lax.scan(step, zero, (couplings_here, rows, columns))
    return lax.psum_scatter(total, "scen", scatter_dimension=0, tiled=True)


def shards(
    rows_here,
    inverse_factor,
    true_orders,
    slab_border,
    slab_columns,
    panel_border,
    panel_rows,
    barrier_diag,
):
    scen_count = lax.axis_size("scen")
    col_count = lax.axis_size("col")
    width = barrier_diag.shape[0]
    group, size = panel_border.shape[1:3]
    wide = slab_columns.shape[1]

    moved, keep, send, dealt = front(
        true_orders, slab_columns, inverse_factor, slab_border, panel_border, width
    )
    got = swap(send, "scen", 1)
    part, messages = quarters(keep, got, dealt[1:])
    messages = [swap(message, "col", m + 1) for m, message in enumerate(messages)]
    part, partial = sum_and_couplings(part, messages, moved, dealt[0])
    parts = [part] + [swap(part, "scen", 2 * m) for m in range(1, scen_count // 2)]
    pieces = [partial[0]] + [swap(partial[m], "col", m) for m in range(1, col_count)]
    part, own = sum_and_assemble(parts, pieces, slab_columns, panel_rows)
    rows_panel = rows_here * scen_count
    sparse = scen_count * group * size * wide < rows_panel * width
    groups = [own]
    if sparse:
        groups += [swap(own, "scen", 2 * m) for m in range(1, scen_count // 2)]
    mine = join([part] + [swap(part, "col", m) for m in range(1, col_count)])
    halves = list(mine) + [swap(half, "scen", 1) for half in mine]
    inverse, factor_rows, *near = cholesky(
        halves, barrier_diag, col_count, groups[:1] if sparse else [], group, rows_here
    )
    if sparse:
        rows, other = far_rows(near[0], groups[1:], group, inverse)
        solved = solve_rows(rows, swap(other, "scen", 1), inverse)
    else:
        local = own[: group * size].reshape(group, size, wide)
        rows = dense_panel(local, panel_rows[0], slab_columns, rows_panel, width)
        solved = jnp.dot(rows, inverse.T, precision=HIGHEST)
    return factor_rows, solved


def solution(mesh):
    in_specs = (
        P(("scen", "col"), None, None),
        P(("scen", "col")),
        P(("scen", "col"), None, None),
        P("scen", None),
        P("col", "scen", None, None),
        P("col", "scen", None),
        P(),
    )
    out_specs = (P("col", None), P(("scen", "col"), None))

    def whole(*args):
        devices = mesh.shape["scen"] * mesh.shape["col"]
        first_section = NF - args[-1].shape[0]
        body = functools.partial(shards, first_section // devices)
        return jax.shard_map(
            body, mesh=mesh, in_specs=in_specs, out_specs=out_specs, check_vma=False
        )(*args)

    return whole
```

```python
import functools

import jax
import jax.numpy as jnp
from jax import lax
from jax.experimental import pallas as pl
from jax.experimental.pallas import tpu as pltpu
from jax.sharding import PartitionSpec as P

NF = 8192
BLOCK = 128
HIGHEST = lax.Precision.HIGHEST
HIGH = lax.Precision.HIGH
VMEM = pl.BlockSpec(memory_space=pltpu.VMEM)
SMEM = pl.BlockSpec(memory_space=pltpu.SMEM)
HBM = pl.BlockSpec(memory_space=pltpu.HBM)
ANY = pl.BlockSpec(memory_space=pl.ANY)
PARAMS = pltpu.CompilerParams(vmem_limit_bytes=40 * 2**20)


def long_cost(micros):
    return pl.CostEstimate(flops=micros * 10**9, bytes_accessed=2**10, transcendentals=0)


def in_hbm(value):
    return pltpu.with_memory_space_constraint(value, pltpu.HBM)


def split_two(value):
    high = value.astype(jnp.bfloat16)
    low = (value - high.astype(jnp.float32)).astype(jnp.bfloat16)
    return high, low


def matmul(left, right):
    return jnp.dot(left, right, preferred_element_type=jnp.float32)


def matmul_nt(left, right):
    return lax.dot_general(
        left, right, (((1,), (1,)), ((), ())), preferred_element_type=jnp.float32
    )


def close_tn(left, right):
    return lax.dot_general(
        left,
        right,
        (((0,), (0,)), ((), ())),
        precision=HIGH,
        preferred_element_type=jnp.float32,
    )


def close(left, right):
    return jnp.dot(left, right, precision=HIGH, preferred_element_type=jnp.float32)


def close_nt(left, right):
    return lax.dot_general(
        left,
        right,
        (((1,), (1,)), ((), ())),
        precision=HIGH,
        preferred_element_type=jnp.float32,
    )


def packed_rows(width, unit):
    count = width // BLOCK
    rows = (count * (count - 1) // 2 + count // 2) * BLOCK + count // 2
    return -(-rows // unit) * unit


def upper_blocks(width):
    count = width // BLOCK
    return [(i, j) for i in range(count) for j in range(i + 1, count)]


def row_and_lane():
    shape = (BLOCK, BLOCK)
    return lax.broadcasted_iota(jnp.int32, shape, 0), lax.broadcasted_iota(jnp.int32, shape, 1)


def pack(blocks, width, packed_ref):
    row, lane = row_and_lane()
    first = 0
    for name in upper_blocks(width):
        packed_ref[first : first + BLOCK, :] = blocks[name]
        first += BLOCK
    diagonals = []
    for i in range(0, width // BLOCK, 2):
        one, two = blocks[i, i], blocks[i + 1, i + 1]
        packed_ref[first : first + BLOCK, :] = jnp.where(row <= lane, one, two)
        first += BLOCK
        diagonals.append(jnp.sum(jnp.where(row == lane, two, 0.0), 0, keepdims=True))
    spare = packed_ref.shape[0] - first - len(diagonals)
    diagonals.append(jnp.zeros((spare, BLOCK), jnp.float32))
    packed_ref[first:, :] = jnp.concatenate(diagonals, 0)


def unpack(packed_ref, width):
    row, lane = row_and_lane()
    blocks = {}
    first = 0
    for name in upper_blocks(width):
        blocks[name] = packed_ref[first : first + BLOCK, :]
        first += BLOCK
    last = first + width // BLOCK // 2 * BLOCK
    for n in range(width // BLOCK // 2):
        square = packed_ref[first + n * BLOCK : first + (n + 1) * BLOCK, :]
        turned = square.T
        blocks[2 * n, 2 * n] = jnp.where(row <= lane, square, turned)
        diagonal = packed_ref[last + n : last + n + 1, :]
        other = jnp.where(row > lane, square, turned)
        blocks[2 * n + 1, 2 * n + 1] = jnp.where(row == lane, diagonal, other)
    return blocks


def front_kernel(
    order_ref,
    columns_ref,
    factor_ref,
    border_ref,
    panel_ref,
    moved_ref,
    keep_ref,
    send_ref,
    *refs,
    width,
):
    dealt = refs[:-6]
    packed_ref, factor_here, border_here, columns_here, sems, deal_sems = refs[-6:]
    place = lax.axis_index("col")
    chunk = factor_here.shape[0] // 4
    chunks = [slice(k * chunk, (k + 1) * chunk) for k in range(4)]
    loads = [pltpu.make_async_copy(border_ref.at[0], border_here, sems.at[0])]
    for k, at in enumerate(chunks):
        loads.append(
            pltpu.make_async_copy(factor_ref.at[0, at], factor_here.at[at], sems.at[k + 1])
        )
    loads.append(pltpu.make_async_copy(columns_ref, columns_here, sems.at[5]))
    for load in loads:
        load.start()
    deals = [
        pltpu.make_async_copy(panel_ref.at[0, place ^ m], out_ref, deal_sems.at[m])
        for m, out_ref in enumerate(dealt)
    ]
    for load in deals:
        load.start()
    core = lax.rem(lax.axis_index("scen"), 2)
    order = order_ref[0]
    loads[0].wait()
    border = border_here[...]
    within = lax.broadcasted_iota(jnp.int32, border.shape, 1) < order
    inside = jnp.where(within, border.astype(jnp.float32), 0.0).astype(jnp.bfloat16)
    product = jnp.zeros(border.shape, jnp.float32)
    for k, at in enumerate(chunks):
        loads[k + 1].wait()
        product = product + matmul(inside[:, at], factor_here[at])
    moved = jnp.where(within, product, 0.0).astype(jnp.bfloat16)
    moved_ref[...] = moved
    loads[5].wait()
    columns = columns_here[pl.ds(place, 1), :]
    spread = (
        lax.broadcasted_iota(jnp.int32, (width, columns.shape[1]), 0) == columns
    ).astype(jnp.bfloat16)
    terms = 0.5 * (matmul_nt(border, moved) + matmul_nt(moved, border))
    high, low = split_two(terms)
    half_spread = matmul_nt(high, spread) + matmul_nt(low, spread)
    high, low = split_two(half_spread)
    blocks = {}
    for i in range(width // BLOCK):
        rows = spread[i * BLOCK : (i + 1) * BLOCK]
        part = matmul(rows, high[:, i * BLOCK :]) + matmul(rows, low[:, i * BLOCK :])
        for j in range(i, width // BLOCK):
            blocks[i, j] = part[:, (j - i) * BLOCK : (j - i + 1) * BLOCK]
    pack(blocks, width, packed_ref)
    half = keep_ref.shape[0]
    keep_ref[...] = packed_ref[pl.ds(pl.multiple_of(core * half, 8), half), :]
    send_ref[...] = packed_ref[pl.ds(pl.multiple_of((1 - core) * half, 8), half), :]
    for load in deals:
        load.wait()


def front(order, columns, factor, border, panel, width):
    count = panel.shape[1]
    total = packed_rows(width, 16 * count)
    half = jax.ShapeDtypeStruct((total // 2, BLOCK), jnp.float32)
    piece = jax.ShapeDtypeStruct(panel.shape[2:], panel.dtype)
    moved, keep, send, *dealt = pl.pallas_call(
        functools.partial(front_kernel, width=width),
        out_shape=[jax.ShapeDtypeStruct(border.shape[1:], jnp.bfloat16), half, half]
        + [piece] * count,
        in_specs=[SMEM, HBM, HBM, HBM, HBM],
        out_specs=[VMEM] * (3 + count),
        scratch_shapes=[
            pltpu.VMEM((total, BLOCK), jnp.float32),
            pltpu.VMEM(factor.shape[1:], factor.dtype),
            pltpu.VMEM(border.shape[1:], border.dtype),
            pltpu.VMEM(columns.shape, columns.dtype),
            pltpu.SemaphoreType.DMA((6,)),
            pltpu.SemaphoreType.DMA((count,)),
        ],
        compiler_params=PARAMS,
        cost_estimate=long_cost(20),
        name="front",
    )(order, in_hbm(columns), in_hbm(factor), in_hbm(border), in_hbm(panel))
    return moved, keep, send, dealt


def whole_tiles(rows):
    return -(-rows // 16) * 16


def quarter_kernel(keep_ref, got_ref, *refs):
    count = (len(refs) + 1) // 2
    dealt, own_ref, out_refs = refs[: count - 1], refs[count - 1], refs[count:]
    place = lax.axis_index("col")
    rows = own_ref.shape[0]
    spare = whole_tiles(rows) - rows
    for m in range(count):
        at = pl.ds(pl.multiple_of((place ^ m) * rows, 8), rows)
        value = keep_ref[at, :] + got_ref[at, :]
        if m == 0:
            own_ref[...] = value
            continue
        if spare > 0:
            value = jnp.concatenate([value, jnp.zeros((spare, BLOCK), jnp.float32)], 0)
        border_ref, out_ref = dealt[m - 1], out_refs[m - 1]
        size, depth = border_ref.shape
        parts = list(split_two(value))
        parts += [border_ref[:, n : n + BLOCK] for n in range(0, depth, BLOCK)]
        first = 0
        for part in parts:
            out_ref[first : first + part.shape[0], :] = part
            first += part.shape[0]


def quarters(keep, got, dealt):
    count = len(dealt) + 1
    rows = keep.shape[0] // count
    length = 2 * whole_tiles(rows) + dealt[0].size // BLOCK
    own, *messages = pl.pallas_call(
        quarter_kernel,
        out_shape=[jax.ShapeDtypeStruct((rows, BLOCK), jnp.float32)]
        + [jax.ShapeDtypeStruct((length, BLOCK), jnp.bfloat16)] * (count - 1),
        in_specs=[VMEM] * (1 + count),
        out_specs=[VMEM] * count,
        compiler_params=PARAMS,
        name="quarters",
    )(keep, got, *dealt)
    return own, messages


def join_kernel(*refs, count):
    pieces, first_ref, last_ref, all_ref = refs[:count], refs[-3], refs[-2], refs[-1]
    place = lax.axis_index("col")
    rows = pieces[0].shape[0]
    for m, piece in enumerate(pieces):
        all_ref[pl.ds(pl.multiple_of((place ^ m) * rows, 8), rows), :] = piece[...]
    half = first_ref.shape[0]
    first_ref[...] = all_ref[:half, :]
    last_ref[...] = all_ref[half:, :]


def join(pieces):
    rows = len(pieces) * pieces[0].shape[0]
    half = jax.ShapeDtypeStruct((rows // 2, BLOCK), jnp.float32)
    return pl.pallas_call(
        functools.partial(join_kernel, count=len(pieces)),
        out_shape=[half, half],
        in_specs=[VMEM] * len(pieces),
        out_specs=[VMEM, VMEM],
        scratch_shapes=[pltpu.VMEM((rows, BLOCK), jnp.float32)],
        compiler_params=PARAMS,
        name="join",
    )(*pieces)


def swap(value, axis, step):
    count = lax.axis_size(axis)
    return lax.ppermute(value, axis, [(i, i ^ step) for i in range(count)])


def tree_sum(values):
    while len(values) > 1:
        values = [values[i] + values[i + 1] for i in range(0, len(values), 2)]
    return values[0]


def row_of(tile, i):
    return jnp.broadcast_to(tile[i : i + 1, :], tile.shape)


def column_of(tile, j):
    index = jnp.full(tile.shape, j, jnp.int32)
    return jnp.take_along_axis(tile, index, axis=1, mode="promise_in_bounds")


def weighted_rows(weights, rows):
    total = weights[0] * rows[0]
    for weight, row in zip(weights[1:], rows[1:]):
        total = total + weight * row
    return total


def factor_block(block):
    groups = BLOCK // 8
    sub = lax.broadcasted_iota(jnp.int32, (8, BLOCK), 0)
    lane = lax.broadcasted_iota(jnp.int32, (8, BLOCK), 1)
    owner = lax.shift_right_logical(lane, 3)
    tiles = [block[8 * t : 8 * t + 8, :] for t in range(groups)]
    upper = []
    lower = []
    ready = None
    for pair in range(groups // 2):
        far = min(groups, 2 * pair + 4)
        swept = []
        for g in (2 * pair, 2 * pair + 1):
            more = g + 1 < groups
            tile = tiles[g]
            near = ready or [column_of(tile, 8 * g + m) for m in range(8)]
            if more:
                near = near + [column_of(tile, 8 * g + 8 + m) for m in range(8)]
            mixed = jnp.where(owner == g, (lane == sub + 8 * g).astype(jnp.float32), tile)
            out_tile, out_mixed = tile, mixed
            pivot = row_of(near[0], 0)
            for i in range(8):
                root = lax.rsqrt(pivot)
                recip = root * root
                rows = {m: row_of(near[m], i) for m in range(i + 1, len(near))}
                if i < 7:
                    pivot = row_of(near[i + 1], i + 1) - row_of(near[i], i + 1) * rows[i + 1] * recip
                factor = jnp.where(sub == i, 1.0 - recip, near[i] * recip)
                for m in rows:
                    near[m] = near[m] - factor * rows[m]
                row_tile, row_mixed = row_of(tile, i), row_of(mixed, i)
                out_tile = jnp.where(sub == i, row_tile * root, out_tile)
                out_mixed = jnp.where(sub == i, row_mixed * root, out_mixed)
                tile = tile - factor * row_tile
                mixed = mixed - factor * row_mixed
            inner = jnp.where((owner == g) & (lane >= sub + 8 * g), out_tile, 0.0)
            upper.append(jnp.where(owner > g, out_mixed, inner))
            lower.append(jnp.where(owner <= g, out_mixed, 0.0))
            rows = [row_of(mixed, i) for i in range(8)]
            swept.append((mixed, rows))
            if not more:
                break
            following = tiles[g + 1]
            weights = [column_of(following, 8 * g + i) for i in range(8)]
            ready = [
                column_of(following, 8 * g + 8 + m)
                - weighted_rows(weights, [row_of(near[8 + m], i) for i in range(8)])
                for m in range(8)
            ]
            for t in range(g + 1, far):
                if t > g + 1:
                    weights = [column_of(tiles[t], 8 * g + i) for i in range(8)]
                tiles[t] = jnp.where(owner == g, 0.0, tiles[t]) - weighted_rows(weights, rows)
        if far < groups:
            g = 2 * pair
            first, second = swept[0][0], swept[1][0]
            weights = [column_of(first, 8 * g + 8 + i) for i in range(8)]
            first = jnp.where(owner == g + 1, 0.0, first) - weighted_rows(weights, swept[1][1])
            parts = [first, second, jnp.zeros((BLOCK - 8 * g - 16, BLOCK), jnp.float32)]
            if g > 0:
                parts = [jnp.zeros((8 * g, BLOCK), jnp.float32)] + parts
            update = close(jnp.concatenate(tiles[far:], 0), jnp.concatenate(parts, 0))
            for t in range(far, groups):
                kept = jnp.where((owner == g) | (owner == g + 1), 0.0, tiles[t])
                tiles[t] = kept - update[8 * (t - far) : 8 * (t - far) + 8]
    return jnp.concatenate(upper, 0), jnp.concatenate(lower, 0)


def placed_rows(groups, group, rows_here, width):
    place = lax.axis_index("scen")
    first = (place - lax.rem(place, 2)) * rows_here
    size = (groups[0].shape[0] - 2 * group) // group
    wide = groups[0].shape[1]
    total = None
    slot = lax.broadcasted_iota(jnp.int32, (2 * rows_here, group * size), 0)
    for group_ref in groups:
        index = group_ref[group * size :, :]
        spreads = []
        for i in range(group):
            columns = index[i : i + 1, :].astype(jnp.int32)
            spread = lax.broadcasted_iota(jnp.int32, (width, wide), 0) == columns
            high, low = split_two(group_ref[i * size : (i + 1) * size, :])
            both = matmul_nt(jnp.concatenate([high, low], 0), spread.astype(jnp.bfloat16))
            spreads.append(both[:size] + both[size:])
        row_index = jnp.concatenate(
            [index[group + i : group + i + 1, :size] for i in range(group)], 1
        )
        row_map = (slot == row_index.astype(jnp.int32) - first).astype(jnp.bfloat16)
        high, low = split_two(jnp.concatenate(spreads, 0))
        part = matmul(row_map, high) + matmul(row_map, low)
        total = part if total is None else total + part
    return total


def cholesky_kernel(
    mine_first, mine_last, other_first, other_last, barrier_ref, *refs, group
):
    upper_ref, turned_ref, packed_ref = refs[-3:]
    near, near_out = (refs[:1], refs[3:4]) if len(refs) == 7 else ((), ())
    inverse_ref, slice_ref = refs[len(near) : len(near) + 2]
    width = barrier_ref.shape[1]
    count = width // BLOCK
    core = lax.rem(lax.axis_index("scen"), 2)
    place = lax.axis_index("col")
    row, lane = row_and_lane()
    diagonal = row == lane
    rows = mine_first.shape[0]
    for n, ref in enumerate((mine_first, mine_last, other_first, other_last)):
        owner = core if n < 2 else 1 - core
        at = (2 * owner + n % 2) * rows
        packed_ref[pl.ds(pl.multiple_of(at, 8), rows), :] = ref[...]
    blocks = unpack(packed_ref, width)
    for i in range(count):
        extra = barrier_ref[:, i * BLOCK : (i + 1) * BLOCK]
        blocks[i, i] = blocks[i, i] + jnp.where(diagonal, extra, 0.0)
    panels = [jnp.concatenate([blocks[i, j] for j in range(i, count)], 1) for i in range(count)]
    slice_rows = slice_ref.shape[0]
    start = place * slice_rows
    block = pl.ds(pl.multiple_of(start // BLOCK * BLOCK, BLOCK), BLOCK)
    upper_ref[...] = jnp.zeros(upper_ref.shape, jnp.float32)
    inverse_ref[...] = jnp.zeros(inverse_ref.shape, jnp.float32)
    for i in range(count):
        here = slice(i * BLOCK, (i + 1) * BLOCK)
        before = slice(0, i * BLOCK)
        own, inverse = factor_block(panels[i][:, :BLOCK])
        if i == 0 and near_out:
            rows_near = near_out[0].shape[0] // 2
            near_out[0][...] = placed_rows(near, group, rows_near, width)
        upper_ref[here, here] = own
        inverse_ref[here, here] = inverse
        if i + 1 < count:
            rest = []
            for j in range(i + 1, count):
                at = (j - i) * BLOCK
                rest.append(close(inverse, panels[i][:, at : at + BLOCK]))
                upper_ref[here, j * BLOCK : (j + 1) * BLOCK] = rest[-1]
                if j == i + 1:
                    square = panels[j][:, :BLOCK] - close_tn(rest[0], rest[0])
            for j in range(i + 1, count):
                parts = [square] if j == i + 1 else []
                done = len(parts)
                if done < count - j:
                    wide = jnp.concatenate(rest[j - i - 1 + done :], 1)
                    update = close_tn(rest[j - i - 1], wide)
                    parts.append(panels[j][:, done * BLOCK :] - update)
                panels[j] = jnp.concatenate(parts, 1)
        if i + 2 == count:
            turned_ref[:, : (i + 1) * BLOCK] = upper_ref[: (i + 1) * BLOCK, block].T
        if i > 0:
            mixed = close_tn(upper_ref[before, here], inverse_ref[before, before])
            inverse_ref[here, before] = -close(inverse, mixed)
    turned_ref[:, width - BLOCK :] = upper_ref[width - BLOCK :, block].T
    slice_ref[...] = turned_ref[pl.ds(pl.multiple_of(lax.rem(start, BLOCK), 8), slice_rows), :]


def cholesky(halves, barrier, col_count, near, group, rows_here):
    width = barrier.shape[0]
    placed = [jax.ShapeDtypeStruct((2 * rows_here, width), jnp.float32)] * len(near)
    return pl.pallas_call(
        functools.partial(cholesky_kernel, group=group),
        out_shape=[
            jax.ShapeDtypeStruct((width, width), jnp.float32),
            jax.ShapeDtypeStruct((width // col_count, width), jnp.float32),
        ]
        + placed,
        in_specs=[VMEM] * (5 + len(near)),
        out_specs=[VMEM] * (2 + len(near)),
        scratch_shapes=[
            pltpu.VMEM((width, width), jnp.float32),
            pltpu.VMEM((BLOCK, width), jnp.float32),
            pltpu.VMEM((4 * halves[0].shape[0], BLOCK), jnp.float32),
        ],
        compiler_params=PARAMS,
        cost_estimate=long_cost(0),
        name="cholesky",
    )(*halves, barrier[None], *near)


def coupling_kernel(moved_ref, own_ref, border_ref, *refs):
    count = len(refs) // 2
    messages, total_ref, out_refs = refs[: count - 1], refs[count - 1], refs[count:]
    rows = own_ref.shape[0]
    size, depth = border_ref.shape
    tiles = whole_tiles(rows)
    moved = moved_ref[...]
    out_refs[0][...] = matmul_nt(border_ref[...], moved)
    parts = [own_ref[...]]
    for message, out_ref in zip(messages, out_refs[1:]):
        high = message[:tiles, :].astype(jnp.float32)
        low = message[tiles : 2 * tiles, :].astype(jnp.float32)
        parts.append((high + low)[:rows])
        first = [2 * tiles + n * size for n in range(depth // BLOCK)]
        border = jnp.concatenate([message[at : at + size, :] for at in first], 1)
        out_ref[...] = matmul_nt(border, moved)
    total_ref[...] = tree_sum(parts)


def sum_and_couplings(own, messages, moved, border):
    shape = jax.ShapeDtypeStruct((border.shape[0], moved.shape[0]), jnp.float32)
    total, *partial = pl.pallas_call(
        coupling_kernel,
        out_shape=[jax.ShapeDtypeStruct(own.shape, jnp.float32)] + [shape] * (len(messages) + 1),
        in_specs=[VMEM] * (len(messages) + 3),
        out_specs=[VMEM] * (len(messages) + 2),
        compiler_params=PARAMS,
        name="couplings",
    )(moved, own, border, *messages)
    return total, partial


def assemble_kernel(columns_ref, rows_ref, *refs, parts):
    refs[-2][...] = tree_sum([ref[...] for ref in refs[:parts]])
    pieces, out_ref = refs[parts:-2], refs[-1]
    place = lax.axis_index("col")
    size = pieces[0].shape[0]
    count = len(pieces)
    for m, piece in enumerate(pieces):
        out_ref[pl.ds(pl.multiple_of((place ^ m) * size, 8), size), :] = piece[...]
    at = count * size
    out_ref[at:, :] = jnp.zeros((out_ref.shape[0] - at, out_ref.shape[1]), jnp.float32)
    out_ref[at : at + count, :] = columns_ref[...].astype(jnp.float32)
    out_ref[at + count : at + 2 * count, :size] = rows_ref[0].astype(jnp.float32)


def sum_and_assemble(parts, pieces, columns, rows):
    size, wide = pieces[0].shape
    count = len(pieces)
    return pl.pallas_call(
        functools.partial(assemble_kernel, parts=len(parts)),
        out_shape=[
            jax.ShapeDtypeStruct(parts[0].shape, jnp.float32),
            jax.ShapeDtypeStruct((count * size + -(-count // 4) * 8, wide), jnp.float32),
        ],
        in_specs=[VMEM] * (len(parts) + count + 2),
        out_specs=[VMEM] * 2,
        compiler_params=PARAMS,
        name="assemble",
    )(columns, rows, *parts, *pieces)


def far_kernel(wait_ref, near_ref, *refs, group):
    groups = refs[:-2]
    keep_ref, send_ref = refs[-2:]
    rows_here, width = keep_ref.shape
    core = lax.rem(lax.axis_index("scen"), 2)
    total = near_ref[...] + placed_rows(groups, group, rows_here, width)
    lower, upper = total[:rows_here], total[rows_here:]
    keep_ref[...] = jnp.where(core == 0, lower, upper)
    send_ref[...] = jnp.where(core == 0, upper, lower)


def far_rows(near, groups, group, wait):
    rows, width = near.shape
    half = jax.ShapeDtypeStruct((rows // 2, width), jnp.float32)
    return pl.pallas_call(
        functools.partial(far_kernel, group=group),
        out_shape=[half, half],
        in_specs=[ANY] + [VMEM] * (1 + len(groups)),
        out_specs=[VMEM, VMEM],
        compiler_params=PARAMS,
        cost_estimate=long_cost(0),
        name="far",
    )(wait, near, *groups)


def solve_kernel(keep_ref, got_ref, inverse_ref, out_ref, solved_ref, sems):
    half = out_ref.shape[1] // 2
    first, last = slice(0, half), slice(half, 2 * half)
    rows = keep_ref[...] + got_ref[...]
    stores = []
    for n, (here, inner) in enumerate(((last, slice(0, 2 * half)), (first, first))):
        solved_ref[:, here] = close_nt(rows[:, inner], inverse_ref[here, inner])
        stores.append(pltpu.make_async_copy(solved_ref.at[:, here], out_ref.at[:, here], sems.at[n]))
        stores[-1].start()
    for store in stores:
        store.wait()


def solve_rows(keep, got, inverse):
    return pl.pallas_call(
        solve_kernel,
        out_shape=jax.ShapeDtypeStruct(keep.shape, jnp.float32),
        in_specs=[VMEM] * 3,
        out_specs=HBM,
        scratch_shapes=[pltpu.VMEM(keep.shape, jnp.float32), pltpu.SemaphoreType.DMA((2,))],
        compiler_params=PARAMS,
        name="solve",
    )(keep, got, inverse)


def dense_panel(couplings_here, rows, columns, rows_panel, width):
    def step(running, operands):
        coupling, row_index, column_index = operands
        column_map = (column_index[:, None] == jnp.arange(width)[None, :]).astype(jnp.float32)
        row_map = (row_index[:, None] == jnp.arange(rows_panel)[None, :]).astype(jnp.float32)
        widened = jnp.dot(coupling, column_map, precision=HIGHEST)
        return running + jnp.einsum("br,bd->rd", row_map, widened, precision=HIGHEST), None

    zero = jnp.zeros((rows_panel, width), jnp.float32)
    total, _ = lax.scan(step, zero, (couplings_here, rows, columns))
    return lax.psum_scatter(total, "scen", scatter_dimension=0, tiled=True)


def shards(
    rows_here,
    inverse_factor,
    true_orders,
    slab_border,
    slab_columns,
    panel_border,
    panel_rows,
    barrier_diag,
):
    scen_count = lax.axis_size("scen")
    col_count = lax.axis_size("col")
    width = barrier_diag.shape[0]
    group, size = panel_border.shape[1:3]
    wide = slab_columns.shape[1]

    moved, keep, send, dealt = front(
        true_orders, slab_columns, inverse_factor, slab_border, panel_border, width
    )
    got = swap(send, "scen", 1)
    part, messages = quarters(keep, got, dealt[1:])
    messages = [swap(message, "col", m + 1) for m, message in enumerate(messages)]
    part, partial = sum_and_couplings(part, messages, moved, dealt[0])
    parts = [part] + [swap(part, "scen", 2 * m) for m in range(1, scen_count // 2)]
    pieces = [partial[0]] + [swap(partial[m], "col", m) for m in range(1, col_count)]
    part, own = sum_and_assemble(parts, pieces, slab_columns, panel_rows)
    rows_panel = rows_here * scen_count
    sparse = scen_count * group * size * wide < rows_panel * width
    groups = [own]
    if sparse:
        groups += [swap(own, "scen", 2 * m) for m in range(1, scen_count // 2)]
    mine = join([part] + [swap(part, "col", m) for m in range(1, col_count)])
    halves = list(mine) + [swap(half, "scen", 1) for half in mine]
    inverse, factor_rows, *near = cholesky(
        halves, barrier_diag, col_count, groups[:1] if sparse else [], group, rows_here
    )
    if sparse:
        rows, other = far_rows(near[0], groups[1:], group, inverse)
        solved = solve_rows(rows, swap(other, "scen", 1), inverse)
    else:
        local = own[: group * size].reshape(group, size, wide)
        rows = dense_panel(local, panel_rows[0], slab_columns, rows_panel, width)
        solved = jnp.dot(rows, inverse.T, precision=HIGHEST)
    return factor_rows, solved


def solution(mesh):
    in_specs = (
        P(("scen", "col"), None, None),
        P(("scen", "col")),
        P(("scen", "col"), None, None),
        P("scen", None),
        P("col", "scen", None, None),
        P("col", "scen", None),
        P(),
    )
    out_specs = (P("col", None), P(("scen", "col"), None))

    def whole(*args):
        devices = mesh.shape["scen"] * mesh.shape["col"]
        first_section = NF - args[-1].shape[0]
        body = functools.partial(shards, first_section // devices)
        return jax.shard_map(
            body, mesh=mesh, in_specs=in_specs, out_specs=out_specs, check_vma=False
        )(*args)

    return whole
```

```python
import functools

import jax
import jax.numpy as jnp
from jax import lax
from jax.experimental import pallas as pl
from jax.experimental.pallas import tpu as pltpu
from jax.sharding import PartitionSpec as P

NF = 8192
BLOCK = 128
HIGHEST = lax.Precision.HIGHEST
HIGH = lax.Precision.HIGH
VMEM = pl.BlockSpec(memory_space=pltpu.VMEM)
SMEM = pl.BlockSpec(memory_space=pltpu.SMEM)
HBM = pl.BlockSpec(memory_space=pltpu.HBM)
ANY = pl.BlockSpec(memory_space=pl.ANY)
PARAMS = pltpu.CompilerParams(vmem_limit_bytes=40 * 2**20)


def long_cost(micros):
    return pl.CostEstimate(flops=micros * 10**9, bytes_accessed=2**10, transcendentals=0)


def in_hbm(value):
    return pltpu.with_memory_space_constraint(value, pltpu.HBM)


def split_two(value):
    high = value.astype(jnp.bfloat16)
    low = (value - high.astype(jnp.float32)).astype(jnp.bfloat16)
    return high, low


def matmul(left, right):
    return jnp.dot(left, right, preferred_element_type=jnp.float32)


def matmul_nt(left, right):
    return lax.dot_general(
        left, right, (((1,), (1,)), ((), ())), preferred_element_type=jnp.float32
    )


def close_tn(left, right):
    return lax.dot_general(
        left,
        right,
        (((0,), (0,)), ((), ())),
        precision=HIGH,
        preferred_element_type=jnp.float32,
    )


def close(left, right):
    return jnp.dot(left, right, precision=HIGH, preferred_element_type=jnp.float32)


def close_nt(left, right):
    return lax.dot_general(
        left,
        right,
        (((1,), (1,)), ((), ())),
        precision=HIGH,
        preferred_element_type=jnp.float32,
    )


def packed_rows(width, unit):
    count = width // BLOCK
    rows = (count * (count - 1) // 2 + count // 2) * BLOCK + count // 2
    return -(-rows // unit) * unit


def upper_blocks(width):
    count = width // BLOCK
    return [(i, j) for i in range(count) for j in range(i + 1, count)]


def row_and_lane():
    shape = (BLOCK, BLOCK)
    return lax.broadcasted_iota(jnp.int32, shape, 0), lax.broadcasted_iota(jnp.int32, shape, 1)


def pack(blocks, width, packed_ref):
    row, lane = row_and_lane()
    first = 0
    for name in upper_blocks(width):
        packed_ref[first : first + BLOCK, :] = blocks[name]
        first += BLOCK
    diagonals = []
    for i in range(0, width // BLOCK, 2):
        one, two = blocks[i, i], blocks[i + 1, i + 1]
        packed_ref[first : first + BLOCK, :] = jnp.where(row <= lane, one, two)
        first += BLOCK
        diagonals.append(jnp.sum(jnp.where(row == lane, two, 0.0), 0, keepdims=True))
    spare = packed_ref.shape[0] - first - len(diagonals)
    diagonals.append(jnp.zeros((spare, BLOCK), jnp.float32))
    packed_ref[first:, :] = jnp.concatenate(diagonals, 0)


def unpack(packed_ref, width):
    row, lane = row_and_lane()
    blocks = {}
    first = 0
    for name in upper_blocks(width):
        blocks[name] = packed_ref[first : first + BLOCK, :]
        first += BLOCK
    last = first + width // BLOCK // 2 * BLOCK
    for n in range(width // BLOCK // 2):
        square = packed_ref[first + n * BLOCK : first + (n + 1) * BLOCK, :]
        turned = square.T
        blocks[2 * n, 2 * n] = jnp.where(row <= lane, square, turned)
        diagonal = packed_ref[last + n : last + n + 1, :]
        other = jnp.where(row > lane, square, turned)
        blocks[2 * n + 1, 2 * n + 1] = jnp.where(row == lane, diagonal, other)
    return blocks


def front_kernel(
    order_ref,
    columns_ref,
    factor_ref,
    border_ref,
    panel_ref,
    moved_ref,
    keep_ref,
    send_ref,
    *refs,
    width,
):
    dealt = refs[:-6]
    packed_ref, factor_here, border_here, columns_here, sems, deal_sems = refs[-6:]
    place = lax.axis_index("col")
    chunk = factor_here.shape[0] // 4
    chunks = [slice(k * chunk, (k + 1) * chunk) for k in range(4)]
    loads = [pltpu.make_async_copy(border_ref.at[0], border_here, sems.at[0])]
    for k, at in enumerate(chunks):
        loads.append(
            pltpu.make_async_copy(factor_ref.at[0, at], factor_here.at[at], sems.at[k + 1])
        )
    loads.append(pltpu.make_async_copy(columns_ref, columns_here, sems.at[5]))
    for load in loads:
        load.start()
    deals = [
        pltpu.make_async_copy(panel_ref.at[0, place ^ m], out_ref, deal_sems.at[m])
        for m, out_ref in enumerate(dealt)
    ]
    for load in deals:
        load.start()
    core = lax.rem(lax.axis_index("scen"), 2)
    order = order_ref[0]
    loads[0].wait()
    border = border_here[...]
    within = lax.broadcasted_iota(jnp.int32, border.shape, 1) < order
    inside = jnp.where(within, border.astype(jnp.float32), 0.0).astype(jnp.bfloat16)
    product = jnp.zeros(border.shape, jnp.float32)
    for k, at in enumerate(chunks):
        loads[k + 1].wait()
        product = product + matmul(inside[:, at], factor_here[at])
    moved = jnp.where(within, product, 0.0).astype(jnp.bfloat16)
    moved_ref[...] = moved
    loads[5].wait()
    columns = columns_here[pl.ds(place, 1), :]
    spread = (
        lax.broadcasted_iota(jnp.int32, (width, columns.shape[1]), 0) == columns
    ).astype(jnp.bfloat16)
    terms = 0.5 * (matmul_nt(border, moved) + matmul_nt(moved, border))
    high, low = split_two(terms)
    half_spread = matmul_nt(high, spread) + matmul_nt(low, spread)
    high, low = split_two(half_spread)
    blocks = {}
    for i in range(width // BLOCK):
        rows = spread[i * BLOCK : (i + 1) * BLOCK]
        part = matmul(rows, high[:, i * BLOCK :]) + matmul(rows, low[:, i * BLOCK :])
        for j in range(i, width // BLOCK):
            blocks[i, j] = part[:, (j - i) * BLOCK : (j - i + 1) * BLOCK]
    pack(blocks, width, packed_ref)
    half = keep_ref.shape[0]
    keep_ref[...] = packed_ref[pl.ds(pl.multiple_of(core * half, 8), half), :]
    send_ref[...] = packed_ref[pl.ds(pl.multiple_of((1 - core) * half, 8), half), :]
    for load in deals:
        load.wait()


def front(order, columns, factor, border, panel, width):
    count = panel.shape[1]
    total = packed_rows(width, 16 * count)
    half = jax.ShapeDtypeStruct((total // 2, BLOCK), jnp.float32)
    piece = jax.ShapeDtypeStruct(panel.shape[2:], panel.dtype)
    moved, keep, send, *dealt = pl.pallas_call(
        functools.partial(front_kernel, width=width),
        out_shape=[jax.ShapeDtypeStruct(border.shape[1:], jnp.bfloat16), half, half]
        + [piece] * count,
        in_specs=[SMEM, HBM, HBM, HBM, HBM],
        out_specs=[VMEM] * (3 + count),
        scratch_shapes=[
            pltpu.VMEM((total, BLOCK), jnp.float32),
            pltpu.VMEM(factor.shape[1:], factor.dtype),
            pltpu.VMEM(border.shape[1:], border.dtype),
            pltpu.VMEM(columns.shape, columns.dtype),
            pltpu.SemaphoreType.DMA((6,)),
            pltpu.SemaphoreType.DMA((count,)),
        ],
        compiler_params=PARAMS,
        cost_estimate=long_cost(20),
        name="front",
    )(order, in_hbm(columns), in_hbm(factor), in_hbm(border), in_hbm(panel))
    return moved, keep, send, dealt


def whole_tiles(rows):
    return -(-rows // 16) * 16


def quarter_kernel(keep_ref, got_ref, *refs):
    count = (len(refs) + 1) // 2
    dealt, own_ref, out_refs = refs[: count - 1], refs[count - 1], refs[count:]
    place = lax.axis_index("col")
    rows = own_ref.shape[0]
    spare = whole_tiles(rows) - rows
    for m in range(count):
        at = pl.ds(pl.multiple_of((place ^ m) * rows, 8), rows)
        value = keep_ref[at, :] + got_ref[at, :]
        if m == 0:
            own_ref[...] = value
            continue
        if spare > 0:
            value = jnp.concatenate([value, jnp.zeros((spare, BLOCK), jnp.float32)], 0)
        border_ref, out_ref = dealt[m - 1], out_refs[m - 1]
        size, depth = border_ref.shape
        parts = list(split_two(value))
        parts += [border_ref[:, n : n + BLOCK] for n in range(0, depth, BLOCK)]
        first = 0
        for part in parts:
            out_ref[first : first + part.shape[0], :] = part
            first += part.shape[0]


def quarters(keep, got, dealt):
    count = len(dealt) + 1
    rows = keep.shape[0] // count
    length = 2 * whole_tiles(rows) + dealt[0].size // BLOCK
    own, *messages = pl.pallas_call(
        quarter_kernel,
        out_shape=[jax.ShapeDtypeStruct((rows, BLOCK), jnp.float32)]
        + [jax.ShapeDtypeStruct((length, BLOCK), jnp.bfloat16)] * (count - 1),
        in_specs=[VMEM] * (1 + count),
        out_specs=[VMEM] * count,
        compiler_params=PARAMS,
        name="quarters",
    )(keep, got, *dealt)
    return own, messages


def join_kernel(*refs, count):
    pieces, first_ref, last_ref, all_ref = refs[:count], refs[-3], refs[-2], refs[-1]
    place = lax.axis_index("col")
    rows = pieces[0].shape[0]
    for m, piece in enumerate(pieces):
        all_ref[pl.ds(pl.multiple_of((place ^ m) * rows, 8), rows), :] = piece[...]
    half = first_ref.shape[0]
    first_ref[...] = all_ref[:half, :]
    last_ref[...] = all_ref[half:, :]


def join(pieces):
    rows = len(pieces) * pieces[0].shape[0]
    half = jax.ShapeDtypeStruct((rows // 2, BLOCK), jnp.float32)
    return pl.pallas_call(
        functools.partial(join_kernel, count=len(pieces)),
        out_shape=[half, half],
        in_specs=[VMEM] * len(pieces),
        out_specs=[VMEM, VMEM],
        scratch_shapes=[pltpu.VMEM((rows, BLOCK), jnp.float32)],
        compiler_params=PARAMS,
        name="join",
    )(*pieces)


def swap(value, axis, step):
    count = lax.axis_size(axis)
    return lax.ppermute(value, axis, [(i, i ^ step) for i in range(count)])


def tree_sum(values):
    while len(values) > 1:
        values = [values[i] + values[i + 1] for i in range(0, len(values), 2)]
    return values[0]


def row_of(tile, i):
    return jnp.broadcast_to(tile[i : i + 1, :], tile.shape)


def column_of(tile, j):
    index = jnp.full(tile.shape, j, jnp.int32)
    return jnp.take_along_axis(tile, index, axis=1, mode="promise_in_bounds")


def weighted_rows(weights, rows):
    total = weights[0] * rows[0]
    for weight, row in zip(weights[1:], rows[1:]):
        total = total + weight * row
    return total


def factor_block(block):
    groups = BLOCK // 8
    sub = lax.broadcasted_iota(jnp.int32, (8, BLOCK), 0)
    lane = lax.broadcasted_iota(jnp.int32, (8, BLOCK), 1)
    owner = lax.shift_right_logical(lane, 3)
    tiles = [block[8 * t : 8 * t + 8, :] for t in range(groups)]
    upper = []
    lower = []
    ready = None
    for pair in range(groups // 2):
        far = min(groups, 2 * pair + 4)
        swept = []
        for g in (2 * pair, 2 * pair + 1):
            more = g + 1 < groups
            tile = tiles[g]
            near = ready or [column_of(tile, 8 * g + m) for m in range(8)]
            if more:
                near = near + [column_of(tile, 8 * g + 8 + m) for m in range(8)]
            mixed = jnp.where(owner == g, (lane == sub + 8 * g).astype(jnp.float32), tile)
            out_tile, out_mixed = tile, mixed
            pivot = row_of(near[0], 0)
            for i in range(8):
                root = lax.rsqrt(pivot)
                recip = root * root
                rows = {m: row_of(near[m], i) for m in range(i + 1, len(near))}
                if i < 7:
                    pivot = row_of(near[i + 1], i + 1) - row_of(near[i], i + 1) * rows[i + 1] * recip
                factor = jnp.where(sub == i, 1.0 - recip, near[i] * recip)
                for m in rows:
                    near[m] = near[m] - factor * rows[m]
                row_tile, row_mixed = row_of(tile, i), row_of(mixed, i)
                out_tile = jnp.where(sub == i, row_tile * root, out_tile)
                out_mixed = jnp.where(sub == i, row_mixed * root, out_mixed)
                tile = tile - factor * row_tile
                mixed = mixed - factor * row_mixed
            inner = jnp.where((owner == g) & (lane >= sub + 8 * g), out_tile, 0.0)
            upper.append(jnp.where(owner > g, out_mixed, inner))
            lower.append(jnp.where(owner <= g, out_mixed, 0.0))
            rows = [row_of(mixed, i) for i in range(8)]
            swept.append((mixed, rows))
            if not more:
                break
            following = tiles[g + 1]
            weights = [column_of(following, 8 * g + i) for i in range(8)]
            ready = [
                column_of(following, 8 * g + 8 + m)
                - weighted_rows(weights, [row_of(near[8 + m], i) for i in range(8)])
                for m in range(8)
            ]
            for t in range(g + 1, far):
                if t > g + 1:
                    weights = [column_of(tiles[t], 8 * g + i) for i in range(8)]
                tiles[t] = jnp.where(owner == g, 0.0, tiles[t]) - weighted_rows(weights, rows)
        if far < groups:
            g = 2 * pair
            first, second = swept[0][0], swept[1][0]
            weights = [column_of(first, 8 * g + 8 + i) for i in range(8)]
            first = jnp.where(owner == g + 1, 0.0, first) - weighted_rows(weights, swept[1][1])
            parts = [first, second, jnp.zeros((BLOCK - 8 * g - 16, BLOCK), jnp.float32)]
            if g > 0:
                parts = [jnp.zeros((8 * g, BLOCK), jnp.float32)] + parts
            update = close(jnp.concatenate(tiles[far:], 0), jnp.concatenate(parts, 0))
            for t in range(far, groups):
                kept = jnp.where((owner == g) | (owner == g + 1), 0.0, tiles[t])
                tiles[t] = kept - update[8 * (t - far) : 8 * (t - far) + 8]
    return jnp.concatenate(upper, 0), jnp.concatenate(lower, 0)


def placed_rows(groups, group, rows_here, width):
    place = lax.axis_index("scen")
    first = (place - lax.rem(place, 2)) * rows_here
    size = (groups[0].shape[0] - 2 * group) // group
    wide = groups[0].shape[1]
    spreads = []
    rows = []
    for group_ref in groups:
        index = group_ref[group * size :, :]
        for i in range(group):
            columns = index[i : i + 1, :].astype(jnp.int32)
            spread = lax.broadcasted_iota(jnp.int32, (width, wide), 0) == columns
            high, low = split_two(group_ref[i * size : (i + 1) * size, :])
            both = matmul_nt(jnp.concatenate([high, low], 0), spread.astype(jnp.bfloat16))
            spreads.append(both[:size] + both[size:])
            rows.append(index[group + i : group + i + 1, :size])
    row_index = jnp.concatenate(rows, 1).astype(jnp.int32) - first
    slot = lax.broadcasted_iota(jnp.int32, (2 * rows_here, row_index.shape[1]), 0)
    row_map = (slot == row_index).astype(jnp.bfloat16)
    high, low = split_two(jnp.concatenate(spreads, 0))
    return matmul(row_map, high) + matmul(row_map, low)


def cholesky_kernel(
    mine_first, mine_last, other_first, other_last, barrier_ref, *refs, group
):
    upper_ref, turned_ref, packed_ref = refs[-3:]
    near, near_out = (refs[:1], refs[3:4]) if len(refs) == 7 else ((), ())
    inverse_ref, slice_ref = refs[len(near) : len(near) + 2]
    width = barrier_ref.shape[1]
    count = width // BLOCK
    core = lax.rem(lax.axis_index("scen"), 2)
    place = lax.axis_index("col")
    row, lane = row_and_lane()
    diagonal = row == lane
    rows = mine_first.shape[0]
    for n, ref in enumerate((mine_first, mine_last, other_first, other_last)):
        owner = core if n < 2 else 1 - core
        at = (2 * owner + n % 2) * rows
        packed_ref[pl.ds(pl.multiple_of(at, 8), rows), :] = ref[...]
    blocks = unpack(packed_ref, width)
    for i in range(count):
        extra = barrier_ref[:, i * BLOCK : (i + 1) * BLOCK]
        blocks[i, i] = blocks[i, i] + jnp.where(diagonal, extra, 0.0)
    panels = [jnp.concatenate([blocks[i, j] for j in range(i, count)], 1) for i in range(count)]
    slice_rows = slice_ref.shape[0]
    start = place * slice_rows
    block = pl.ds(pl.multiple_of(start // BLOCK * BLOCK, BLOCK), BLOCK)
    upper_ref[...] = jnp.zeros(upper_ref.shape, jnp.float32)
    inverse_ref[...] = jnp.zeros(inverse_ref.shape, jnp.float32)
    for i in range(count):
        here = slice(i * BLOCK, (i + 1) * BLOCK)
        before = slice(0, i * BLOCK)
        own, inverse = factor_block(panels[i][:, :BLOCK])
        if i == 0 and near_out:
            rows_near = near_out[0].shape[0] // 2
            near_out[0][...] = placed_rows(near, group, rows_near, width)
        upper_ref[here, here] = own
        inverse_ref[here, here] = inverse
        if i + 1 < count:
            rest = []
            for j in range(i + 1, count):
                at = (j - i) * BLOCK
                rest.append(close(inverse, panels[i][:, at : at + BLOCK]))
                upper_ref[here, j * BLOCK : (j + 1) * BLOCK] = rest[-1]
                if j == i + 1:
                    square = panels[j][:, :BLOCK] - close_tn(rest[0], rest[0])
            for j in range(i + 1, count):
                parts = [square] if j == i + 1 else []
                done = len(parts)
                if done < count - j:
                    wide = jnp.concatenate(rest[j - i - 1 + done :], 1)
                    update = close_tn(rest[j - i - 1], wide)
                    parts.append(panels[j][:, done * BLOCK :] - update)
                panels[j] = jnp.concatenate(parts, 1)
        if i + 2 == count:
            turned_ref[:, : (i + 1) * BLOCK] = upper_ref[: (i + 1) * BLOCK, block].T
        if i > 0:
            mixed = close_tn(upper_ref[before, here], inverse_ref[before, before])
            inverse_ref[here, before] = -close(inverse, mixed)
    turned_ref[:, width - BLOCK :] = upper_ref[width - BLOCK :, block].T
    slice_ref[...] = turned_ref[pl.ds(pl.multiple_of(lax.rem(start, BLOCK), 8), slice_rows), :]


def cholesky(halves, barrier, col_count, near, group, rows_here):
    width = barrier.shape[0]
    placed = [jax.ShapeDtypeStruct((2 * rows_here, width), jnp.float32)] * len(near)
    return pl.pallas_call(
        functools.partial(cholesky_kernel, group=group),
        out_shape=[
            jax.ShapeDtypeStruct((width, width), jnp.float32),
            jax.ShapeDtypeStruct((width // col_count, width), jnp.float32),
        ]
        + placed,
        in_specs=[VMEM] * (5 + len(near)),
        out_specs=[VMEM] * (2 + len(near)),
        scratch_shapes=[
            pltpu.VMEM((width, width), jnp.float32),
            pltpu.VMEM((BLOCK, width), jnp.float32),
            pltpu.VMEM((4 * halves[0].shape[0], BLOCK), jnp.float32),
        ],
        compiler_params=PARAMS,
        cost_estimate=long_cost(0),
        name="cholesky",
    )(*halves, barrier[None], *near)


def coupling_kernel(moved_ref, own_ref, border_ref, *refs):
    count = len(refs) // 2
    messages, total_ref, out_refs = refs[: count - 1], refs[count - 1], refs[count:]
    rows = own_ref.shape[0]
    size, depth = border_ref.shape
    tiles = whole_tiles(rows)
    moved = moved_ref[...]
    out_refs[0][...] = matmul_nt(border_ref[...], moved)
    parts = [own_ref[...]]
    for message, out_ref in zip(messages, out_refs[1:]):
        high = message[:tiles, :].astype(jnp.float32)
        low = message[tiles : 2 * tiles, :].astype(jnp.float32)
        parts.append((high + low)[:rows])
        first = [2 * tiles + n * size for n in range(depth // BLOCK)]
        border = jnp.concatenate([message[at : at + size, :] for at in first], 1)
        out_ref[...] = matmul_nt(border, moved)
    total_ref[...] = tree_sum(parts)


def sum_and_couplings(own, messages, moved, border):
    shape = jax.ShapeDtypeStruct((border.shape[0], moved.shape[0]), jnp.float32)
    total, *partial = pl.pallas_call(
        coupling_kernel,
        out_shape=[jax.ShapeDtypeStruct(own.shape, jnp.float32)] + [shape] * (len(messages) + 1),
        in_specs=[VMEM] * (len(messages) + 3),
        out_specs=[VMEM] * (len(messages) + 2),
        compiler_params=PARAMS,
        name="couplings",
    )(moved, own, border, *messages)
    return total, partial


def assemble_kernel(columns_ref, rows_ref, *refs, parts):
    refs[-2][...] = tree_sum([ref[...] for ref in refs[:parts]])
    pieces, out_ref = refs[parts:-2], refs[-1]
    place = lax.axis_index("col")
    size = pieces[0].shape[0]
    count = len(pieces)
    for m, piece in enumerate(pieces):
        out_ref[pl.ds(pl.multiple_of((place ^ m) * size, 8), size), :] = piece[...]
    at = count * size
    out_ref[at:, :] = jnp.zeros((out_ref.shape[0] - at, out_ref.shape[1]), jnp.float32)
    out_ref[at : at + count, :] = columns_ref[...].astype(jnp.float32)
    out_ref[at + count : at + 2 * count, :size] = rows_ref[0].astype(jnp.float32)


def sum_and_assemble(parts, pieces, columns, rows):
    size, wide = pieces[0].shape
    count = len(pieces)
    return pl.pallas_call(
        functools.partial(assemble_kernel, parts=len(parts)),
        out_shape=[
            jax.ShapeDtypeStruct(parts[0].shape, jnp.float32),
            jax.ShapeDtypeStruct((count * size + -(-count // 4) * 8, wide), jnp.float32),
        ],
        in_specs=[VMEM] * (len(parts) + count + 2),
        out_specs=[VMEM] * 2,
        compiler_params=PARAMS,
        name="assemble",
    )(columns, rows, *parts, *pieces)


def far_kernel(wait_ref, near_ref, *refs, group):
    groups = refs[:-2]
    keep_ref, send_ref = refs[-2:]
    rows_here, width = keep_ref.shape
    core = lax.rem(lax.axis_index("scen"), 2)
    total = near_ref[...] + placed_rows(groups, group, rows_here, width)
    lower, upper = total[:rows_here], total[rows_here:]
    keep_ref[...] = jnp.where(core == 0, lower, upper)
    send_ref[...] = jnp.where(core == 0, upper, lower)


def far_rows(near, groups, group, wait):
    rows, width = near.shape
    half = jax.ShapeDtypeStruct((rows // 2, width), jnp.float32)
    return pl.pallas_call(
        functools.partial(far_kernel, group=group),
        out_shape=[half, half],
        in_specs=[ANY] + [VMEM] * (1 + len(groups)),
        out_specs=[VMEM, VMEM],
        compiler_params=PARAMS,
        cost_estimate=long_cost(0),
        name="far",
    )(wait, near, *groups)


def solve_kernel(keep_ref, got_ref, inverse_ref, out_ref, solved_ref, sems):
    half = out_ref.shape[1] // 2
    first, last = slice(0, half), slice(half, 2 * half)
    rows = keep_ref[...] + got_ref[...]
    stores = []
    for n, (here, inner) in enumerate(((last, slice(0, 2 * half)), (first, first))):
        solved_ref[:, here] = close_nt(rows[:, inner], inverse_ref[here, inner])
        stores.append(pltpu.make_async_copy(solved_ref.at[:, here], out_ref.at[:, here], sems.at[n]))
        stores[-1].start()
    for store in stores:
        store.wait()


def solve_rows(keep, got, inverse):
    return pl.pallas_call(
        solve_kernel,
        out_shape=jax.ShapeDtypeStruct(keep.shape, jnp.float32),
        in_specs=[VMEM] * 3,
        out_specs=HBM,
        scratch_shapes=[pltpu.VMEM(keep.shape, jnp.float32), pltpu.SemaphoreType.DMA((2,))],
        compiler_params=PARAMS,
        name="solve",
    )(keep, got, inverse)


def dense_panel(couplings_here, rows, columns, rows_panel, width):
    def step(running, operands):
        coupling, row_index, column_index = operands
        column_map = (column_index[:, None] == jnp.arange(width)[None, :]).astype(jnp.float32)
        row_map = (row_index[:, None] == jnp.arange(rows_panel)[None, :]).astype(jnp.float32)
        widened = jnp.dot(coupling, column_map, precision=HIGHEST)
        return running + jnp.einsum("br,bd->rd", row_map, widened, precision=HIGHEST), None

    zero = jnp.zeros((rows_panel, width), jnp.float32)
    total, _ = lax.scan(step, zero, (couplings_here, rows, columns))
    return lax.psum_scatter(total, "scen", scatter_dimension=0, tiled=True)


def shards(
    rows_here,
    inverse_factor,
    true_orders,
    slab_border,
    slab_columns,
    panel_border,
    panel_rows,
    barrier_diag,
):
    scen_count = lax.axis_size("scen")
    col_count = lax.axis_size("col")
    width = barrier_diag.shape[0]
    group, size = panel_border.shape[1:3]
    wide = slab_columns.shape[1]

    moved, keep, send, dealt = front(
        true_orders, slab_columns, inverse_factor, slab_border, panel_border, width
    )
    got = swap(send, "scen", 1)
    part, messages = quarters(keep, got, dealt[1:])
    messages = [swap(message, "col", m + 1) for m, message in enumerate(messages)]
    part, partial = sum_and_couplings(part, messages, moved, dealt[0])
    parts = [part] + [swap(part, "scen", 2 * m) for m in range(1, scen_count // 2)]
    pieces = [partial[0]] + [swap(partial[m], "col", m) for m in range(1, col_count)]
    part, own = sum_and_assemble(parts, pieces, slab_columns, panel_rows)
    rows_panel = rows_here * scen_count
    sparse = scen_count * group * size * wide < rows_panel * width
    groups = [own]
    if sparse:
        groups += [swap(own, "scen", 2 * m) for m in range(1, scen_count // 2)]
    mine = join([part] + [swap(part, "col", m) for m in range(1, col_count)])
    halves = list(mine) + [swap(half, "scen", 1) for half in mine]
    inverse, factor_rows, *near = cholesky(
        halves, barrier_diag, col_count, groups[:1] if sparse else [], group, rows_here
    )
    if sparse:
        rows, other = far_rows(near[0], groups[1:], group, inverse)
        solved = solve_rows(rows, swap(other, "scen", 1), inverse)
    else:
        local = own[: group * size].reshape(group, size, wide)
        rows = dense_panel(local, panel_rows[0], slab_columns, rows_panel, width)
        solved = jnp.dot(rows, inverse.T, precision=HIGHEST)
    return factor_rows, solved


def solution(mesh):
    in_specs = (
        P(("scen", "col"), None, None),
        P(("scen", "col")),
        P(("scen", "col"), None, None),
        P("scen", None),
        P("col", "scen", None, None),
        P("col", "scen", None),
        P(),
    )
    out_specs = (P("col", None), P(("scen", "col"), None))

    def whole(*args):
        devices = mesh.shape["scen"] * mesh.shape["col"]
        first_section = NF - args[-1].shape[0]
        body = functools.partial(shards, first_section // devices)
        return jax.shard_map(
            body, mesh=mesh, in_specs=in_specs, out_specs=out_specs, check_vma=False
        )(*args)

    return whole
```
